32 devices in a mesh: strip: 8 (over z, x), cells: 4 (over y, core).
Axes of the slice: x: 2, y: 2, z: 4, core: 2. Of those that a mesh axis runs over, the one named last changes fastest.
Arguments:
- pin_rows: int32 [131072], P(('strip', 'cells')), may hold values from 0 to 2
- pin_cols: int32 [131072], P(('strip', 'cells')), may hold values from 0 to 2558
- pin_fracs: float32 [2, 131072], P(None, ('strip', 'cells')), may hold values from 0 to 1
- pin_weights: float32 [131072], P(('strip', 'cells')), may hold values from 0.5 to 1.5
- capacity: int32 [32, 2560], P('strip', 'cells'), may hold values from 1 to 4
- blockage: float32 [32, 2560], P('strip', 'cells'), may hold values from 0 to 0.5
- row_blocks: float32 [20, 128, 128], P('cells'), may hold values from -0.002 to 0.15
- col_blocks: float32 [1, 32, 32], replicated, may hold values from -0.002 to 0.15
Outputs:
- final_density: float32 [32, 2560], P('strip', 'cells')
- pin_velocity: float32 [2, 131072], P(None, ('strip', 'cells'))
The draws below stay inside these ranges and needn't reach their ends.
All inputs are finite; a program needn't handle non-finite values.
Results may differ from the reference program's by a relative error of at most 0.0052.
Values may be sent and summed in bfloat16 or wider, within the bound.
No kernel may reach another device: no remote copies, remote signals or barrier semaphores. Data moves between devices by JAX's collectives and lax.ppermute only.
A program may use at most 64 MiB of HBM per device.

```python
import jax
import jax.numpy as jnp
from jax import lax

RD = 4
BLK = 128
SWEEPS = 3
STEPS = 2
NROW = 32
NCOL = 2560
PINS_STRIP = 16384
PINS = 131072
BLKY = 32
NBX = 20
NBY = 1


coupling = 2.0


def block_inverses(key, block_count, block_size):
    first_key, second_key = jax.random.split(key)
    reference_level = jnp.exp(jax.random.uniform(first_key, (block_count, 1, 1), jnp.float32, jnp.log(4.0), jnp.log(6.0)))
    shift_rate = reference_level / coupling
    cosh_value = 1.0 + 0.5 * shift_rate
    angle_rate = jnp.log(cosh_value + jnp.sqrt(cosh_value * cosh_value - 1.0))
    positions = jnp.arange(1, block_size + 1).astype(jnp.float32)
    row_pos = positions[None, :, None]
    col_pos = positions[None, None, :]
    spread = jnp.abs(row_pos - col_pos)
    position_sum = row_pos + col_pos
    far_ends = 2.0 * (block_size + 1)
    numerator = jnp.exp(-spread * angle_rate) - jnp.exp(-(far_ends - position_sum) * angle_rate) - jnp.exp(-position_sum * angle_rate) + jnp.exp(-(far_ends - spread) * angle_rate)
    denominator = 2.0 * jnp.sinh(angle_rate) * (1.0 - jnp.exp(-far_ends * angle_rate)) * coupling
    noise = jax.random.uniform(second_key, (block_count, block_size, block_size), jnp.float32, -0.002, 0.002)
    return numerator / denominator + noise


def draw_row_blocks(key, part):
    return block_inverses(jax.random.fold_in(key, 11), NBX, BLK)


def draw_col_blocks(key, part):
    return block_inverses(jax.random.fold_in(key, 23), NBY, BLKY)


def set_ends(drawn, stream_key, low, largest):
    extent = drawn.shape
    index_at = [jax.random.randint(jax.random.fold_in(stream_key, axis), (), 0, extent[axis]) for axis in range(len(extent))]
    drawn = drawn.at[tuple(index_at)].set(low)
    longest = extent.index(max(extent))
    index_at[longest] = (index_at[longest] + 1) % extent[longest]
    return drawn.at[tuple(index_at)].set(largest)


def levels(own_key, dims, cuts, smallest, high):
    loudness, own = 1.0, jax.random.fold_in(own_key, 6)
    for position, blocks in cuts:
        steps = jnp.exp(jax.random.uniform(jax.random.fold_in(own, position), (blocks,), jnp.float32, smallest / len(cuts), high / len(cuts)))
        loudness = loudness * jnp.repeat(steps, dims[position] // blocks).reshape([-1 if axis == position else 1 for axis in range(len(dims))])
    return loudness


def setup_inputs(seed: int = 0) -> dict:
    arg_keys = jax.random.split(jax.random.key(seed), 9)
    pin_rows = set_ends(jax.random.randint(arg_keys[0], (PINS,), 0, RD - 1), jax.random.fold_in(arg_keys[0], 1), 0, (RD - 1) - 1).astype(jnp.int32)
    pin_cols = set_ends(jax.random.randint(arg_keys[1], (PINS,), 0, NCOL - 1), jax.random.fold_in(arg_keys[1], 1), 0, (NCOL - 1) - 1).astype(jnp.int32)
    pin_fracs = jnp.clip(1.0 * jax.random.uniform(arg_keys[2], (2, PINS), jnp.float32) ** levels(arg_keys[2], (2, PINS), ((1, 32),), -0.2, 0.2), 0.0, 1.0)
    pin_weights = jnp.clip(0.5 + 1.0 * jax.random.uniform(arg_keys[3], (PINS,), jnp.float32) ** levels(arg_keys[3], (PINS,), ((0, 32),), -0.2, 0.2), 0.5, 1.5)
    capacity = set_ends(jax.random.randint(arg_keys[4], (NROW, NCOL), 1, 5), jax.random.fold_in(arg_keys[4], 1), 1, 4).astype(jnp.int32)
    blockage = jnp.clip(0.5 * jax.random.uniform(arg_keys[5], (NROW, NCOL), jnp.float32) ** levels(arg_keys[5], (NROW, NCOL), ((0, 8), (1, 4)), -0.2, 0.2), 0.0, 0.5)
    row_blocks = draw_row_blocks(jax.random.fold_in(arg_keys[8], 71), 0)
    col_blocks = draw_col_blocks(jax.random.fold_in(arg_keys[8], 71), 0)
    return dict(pin_rows=pin_rows, pin_cols=pin_cols, pin_fracs=pin_fracs, pin_weights=pin_weights, capacity=capacity, blockage=blockage, row_blocks=row_blocks, col_blocks=col_blocks)


coupling = 2.0
floor_level = 0.5
highest = lax.Precision.HIGHEST


def along_lines(values):
    padded = jnp.pad(values, ((0, 0), (1, 1)), mode="edge")
    return 2.0 * values - padded[:, :-2] - padded[:, 2:]


def across_lines(values):
    padded = jnp.pad(values, ((1, 1), (0, 0)), mode="edge")
    return 2.0 * values - padded[:-2] - padded[2:]


def blockwise(residual, blocks):
    leading = residual.shape[0]
    pieces = residual.reshape(leading, blocks.shape[0], blocks.shape[1])
    result = jnp.einsum("rnj,nij->rni", pieces, blocks, precision=highest)
    return result.reshape(leading, blocks.shape[0] * blocks.shape[1])


def line_solve(source, weights, start_iterate, blocks):
    iterate = start_iterate
    for sweep_index in range(SWEEPS):
        residual = source - (weights * iterate + coupling * along_lines(iterate))
        iterate = iterate + blockwise(residual, blocks)
    return iterate


def rounded(values):
    return lax.optimization_barrier(values.astype(jnp.bfloat16)).astype(jnp.float32)


def reference(pin_rows, pin_cols, pin_fracs, pin_weights, capacity, blockage, row_blocks, col_blocks):
    weights = capacity.astype(jnp.float32) * (1.0 - blockage)
    strip_of = (jnp.arange(PINS) // PINS_STRIP).astype(jnp.int32)
    global_rows = strip_of * RD + pin_rows
    near_y = 1.0 - pin_fracs[0]
    near_x = 1.0 - pin_fracs[1]
    splat_rows = [rounded(pin_weights * near_y), rounded(pin_weights * pin_fracs[0])]
    look_rows = [rounded(near_y), rounded(pin_fracs[0])]
    col_factors = [rounded(near_x), rounded(pin_fracs[1])]
    density = jnp.zeros((NROW, NCOL), jnp.float32)
    for row_offset in range(2):
        for col_offset in range(2):
            density = density.at[global_rows + row_offset, pin_cols + col_offset].add(
                splat_rows[row_offset] * col_factors[col_offset])
    current = density / weights
    source = weights * current - coupling * across_lines(current)
    for step_index in range(STEPS):
        current = line_solve(source, weights, current, row_blocks)
        middle = weights * current - coupling * along_lines(current)
        current = line_solve(middle.T, weights.T, current.T, col_blocks).T
        if step_index + 1 < STEPS:
            source = weights * current - coupling * across_lines(current)
    padded_cols = jnp.pad(current, ((0, 0), (1, 1)), mode="edge")
    padded_rows = jnp.pad(current, ((1, 1), (0, 0)), mode="edge")
    scale = jnp.maximum(current, floor_level)
    velocity_x = rounded(-(0.5 * (padded_cols[:, 2:] - padded_cols[:, :-2])) / scale)
    velocity_y = rounded(-(0.5 * (padded_rows[2:] - padded_rows[:-2])) / scale)
    total_y = jnp.zeros((PINS,), jnp.float32)
    total_x = jnp.zeros((PINS,), jnp.float32)
    for row_offset in range(2):
        for col_offset in range(2):
            factor = look_rows[row_offset] * col_factors[col_offset]
            total_y = total_y + factor * velocity_y[global_rows + row_offset, pin_cols + col_offset]
            total_x = total_x + factor * velocity_x[global_rows + row_offset, pin_cols + col_offset]
    return current, jnp.stack([total_y, total_x])
```

```python
import functools

import jax
import jax.numpy as jnp
from jax import lax
from jax.experimental import pallas as pl
from jax.experimental.pallas import tpu as pltpu
from jax.sharding import PartitionSpec as P

SWEEPS = 3
STEPS = 2
LANES = 128
GROUP = 8

coupling = 2.0
floor_level = 0.5
block_low = -0.002
block_span = 0.152
code_top = 65535.0
code_half = 32768.0

f32 = jnp.float32
bf16 = jnp.bfloat16


def iota(shape, axis):
    return lax.broadcasted_iota(jnp.int32, shape, axis)


def halves(values):
    high = values.astype(bf16)
    return high, (values - high.astype(f32)).astype(bf16)


def last_dims(left, right):
    return lax.dot_general(left, right, (((1,), (1,)), ((), ())), preferred_element_type=f32)


def pick(index, first, near, far):
    return jnp.where(index == first, near, jnp.where(index == first + 1, far, 0.0))


def rounded(values):
    return values.astype(bf16).astype(f32)


def splat_kernel(tiles, parts, rows_ref, cols_ref, fracs_ref, pin_weights_ref, cap_ref, block_ref, out_ref):
    depth = cap_ref.shape[0]
    height = parts * depth
    rows, cols, sizes = rows_ref[...], cols_ref[...], pin_weights_ref[...]
    place = iota((height * (tiles + 1), LANES), 0)
    group, inner = place // height, place % height
    keys = ((inner // depth) * tiles + group - 1) * depth + inner % depth
    lane = iota((LANES + 8, LANES), 0)
    tables, lanes = [], []
    for j in range(rows.shape[0]):
        fy, fx = fracs_ref[0, j : j + 1, :], fracs_ref[1, j : j + 1, :]
        size, col = sizes[j : j + 1], cols[j : j + 1]
        key = (col >> 7) * depth + rows[j : j + 1]
        tables.append(pick(keys, key, rounded(size * (1.0 - fy)), rounded(size * fy)).astype(bf16))
        lanes.append(pick(lane, col & 127, rounded(1.0 - fx), rounded(fx)).astype(bf16))
    total = last_dims(jnp.concatenate(tables, 1), jnp.concatenate(lanes, 1))
    first_lane = iota((height, LANES), 1) == 0
    for t in range(tiles):
        own = total[(t + 1) * height : (t + 2) * height, :LANES]
        spill = total[t * height : (t + 1) * height, LANES : LANES + 1]
        own = own + jnp.where(first_lane, spill, 0.0)
        out_ref[:height, t * LANES : (t + 1) * LANES] = own.astype(bf16)
    weights = cap_ref[...].astype(f32) * (1.0 - block_ref[...])
    high, low = halves(weights)
    rest = jnp.zeros((height - 2 * depth, weights.shape[1]), f32)
    out_ref[height:, :] = jnp.concatenate([high.astype(f32), low.astype(f32), rest], 0).astype(bf16)


def along_lines(values):
    width = values.shape[1]
    column = iota(values.shape, 1)
    left = jnp.where(column == 0, values, pltpu.roll(values, 1, 1))
    right = jnp.where(column == width - 1, values, pltpu.roll(values, width - 1, 1))
    return 2.0 * values - left - right


def across_lines(values):
    height = values.shape[0]
    row = iota(values.shape, 0)
    above = jnp.where(row == 0, values, pltpu.roll(values, 1, 0))
    below = jnp.where(row == height - 1, values, pltpu.roll(values, height - 1, 0))
    return 2.0 * values - above - below


def row_blockwise(residual, pairs_ref):
    high, low = halves(residual)
    result = []
    for k in range(pairs_ref.shape[0]):
        cut = slice(k * LANES, (k + 1) * LANES)
        pair = pairs_ref[k]
        both = last_dims(jnp.concatenate([high[:, cut], low[:, cut]], 1), jnp.concatenate([pair, pair], 1))
        result.append(both[:, :LANES] + both[:, LANES:])
    return jnp.concatenate(result, 1)


def col_blockwise(residual, blocks):
    high, low = halves(residual)
    count, size = len(blocks), blocks[0][0].shape[0]
    result = []
    for k, (block_high, block_low_part) in enumerate(blocks):
        cut = slice(k * size, (k + 1) * size)
        dot = functools.partial(jnp.dot, preferred_element_type=f32)
        result.append(dot(block_high, high[cut]) + (dot(block_low_part, high[cut]) + dot(block_high, low[cut])))
    return result[0] if count == 1 else jnp.concatenate(result, 0)


def each(count, body):
    if count == 1:
        body(0)
    else:
        pl.loop(0, count)(body)


def field_kernel(
    sizes, spot_ref, sent_ref, codes_ref, col_blocks_ref, rows_ref, cols_ref, fracs_ref,
    final_ref, velocity_ref, pairs, weights_ref, source_ref, field_ref,
):
    depth, tiles, parts, strips = sizes
    width_part = tiles * LANES
    width = parts * width_part
    height = strips * depth
    chunk = min(GROUP, strips) * depth
    chunks = height // chunk
    strip, part = spot_ref[0], spot_ref[1]

    def unpack(k):
        code = codes_ref[pl.ds(pl.multiple_of(k * LANES, LANES), LANES), :].astype(f32)
        high, low = halves((code + code_half) * (block_span / code_top) + block_low)
        pairs[k, :LANES, :] = high
        pairs[k, LANES:, :] = low

    for k in range(pairs.shape[0]):
        unpack(k)

    sent_rows = 2 * parts * depth
    span = chunk // depth * parts * sent_rows
    target, origin = iota((parts * chunk, span), 0), iota((parts * chunk, span), 1)
    device, slot = origin // sent_rows, origin % sent_rows
    row_here = target % chunk - (device // parts) * depth
    side = target // chunk
    first = parts * depth
    terms = (slot < first) & (slot // depth == side) & (slot % depth == row_here)
    pieces = (slot >= first) & (slot < first + 2 * depth) & (device % parts == side) & (slot % depth == row_here)
    chosen = jnp.concatenate([jnp.where(terms, 1.0, 0.0), jnp.where(pieces, 1.0, 0.0)], 0).astype(bf16)

    @functools.partial(each, chunks)
    def place(g):
        got = jnp.dot(
            chosen, sent_ref[pl.ds(pl.multiple_of(g * span, span), span), :], preferred_element_type=f32
        )
        here = pl.ds(pl.multiple_of(g * chunk, chunk), chunk)
        for p in range(parts):
            cut = slice(p * width_part, (p + 1) * width_part)
            weight = got[(parts + p) * chunk : (parts + p + 1) * chunk]
            weights_ref[here, cut] = weight
            source_ref[here, cut] = got[p * chunk : (p + 1) * chunk] / weight

    lanes_at_once = width if chunks == 1 else LANES
    col_blocks = [halves(col_blocks_ref[k]) for k in range(col_blocks_ref.shape[0])]
    inner = pl.ds(8, height)

    @functools.partial(each, width // lanes_at_once)
    def start(t):
        cut = pl.ds(pl.multiple_of(t * lanes_at_once, lanes_at_once), lanes_at_once)
        current = source_ref[:, cut]
        field_ref[inner, cut] = current
        source_ref[:, cut] = weights_ref[:, cut] * current - coupling * across_lines(current)

    for step in range(STEPS):

        @functools.partial(each, chunks)
        def solve_rows(g):
            here = pl.ds(pl.multiple_of(g * chunk, chunk), chunk)
            there = pl.ds(pl.multiple_of(g * chunk + 8, 8), chunk)
            source, weights, current = source_ref[here, :], weights_ref[here, :], field_ref[there, :]
            for sweep in range(SWEEPS):
                residual = source - (weights * current + coupling * along_lines(current))
                current = current + row_blockwise(residual, pairs)
            field_ref[there, :] = current
            source_ref[here, :] = weights * current - coupling * along_lines(current)

        @functools.partial(each, width // lanes_at_once)
        def solve_cols(t):
            cut = pl.ds(pl.multiple_of(t * lanes_at_once, lanes_at_once), lanes_at_once)
            middle, weights, current = source_ref[:, cut], weights_ref[:, cut], field_ref[inner, cut]
            for sweep in range(SWEEPS):
                residual = middle - (weights * current + coupling * across_lines(current))
                current = current + col_blockwise(residual, col_blocks)
            field_ref[inner, cut] = current
            if step + 1 < STEPS:
                source_ref[:, cut] = weights * current - coupling * across_lines(current)
            else:
                field_ref[:8, cut] = jnp.broadcast_to(current[:1], (8, lanes_at_once))
                field_ref[height + 8 :, cut] = jnp.broadcast_to(current[-1:], (8, lanes_at_once))

    row0 = strip * depth
    columns = pl.ds(pl.multiple_of(part * width_part, LANES), width_part)
    base, shift = pl.multiple_of(row0 // 8 * 8, 8), 17 - row0 % 8
    final_ref[...] = pltpu.roll(field_ref[pl.ds(base, 24), columns], shift, 0)[1 : 1 + depth]

    window = pltpu.roll(field_ref[pl.ds(base, 24), :], shift, 0)
    above, centre, below = window[:8], pltpu.roll(window, 23, 0)[:8], pltpu.roll(window, 22, 0)[:8]
    column = iota(centre.shape, 1)
    left = jnp.where(column == 0, centre, pltpu.roll(centre, 1, 1))
    right = jnp.where(column == width - 1, centre, pltpu.roll(centre, width - 1, 1))
    scale = jnp.maximum(centre, floor_level)
    velocity_y = rounded(-(0.5 * (below - above)) / scale)
    velocity_x = rounded(-(0.5 * (right - left)) / scale)

    upper = iota((8, LANES), 0) < depth

    def stacked(values):
        stack = []
        for t in range(0, parts * tiles, 2):
            even = values[:, t * LANES : (t + 1) * LANES]
            odd = values[:, (t + 1) * LANES : (t + 2) * LANES]
            stack.append(jnp.where(upper, even, pltpu.roll(odd, depth, 0)))
        return jnp.concatenate(stack, 0)

    stack_y, stack_x = stacked(velocity_y), stacked(velocity_x)
    many = stack_y.shape[0]
    next_y = pltpu.roll(stack_y, many - depth, 0)
    next_x = pltpu.roll(stack_x, many - depth, 0)
    turned = [stack_y.T, next_y.T[:8], stack_x.T, next_x.T[:8]]
    table = jnp.concatenate(turned, 0).astype(bf16)
    rows, cols = rows_ref[...], cols_ref[...]
    keys, lane = iota((many, LANES), 0), iota((LANES + 8, LANES), 0)
    for j in range(rows.shape[0]):
        fy, fx = fracs_ref[0, j : j + 1, :], fracs_ref[1, j : j + 1, :]
        col = cols[j : j + 1]
        key = (col >> 7) * depth + rows[j : j + 1]
        look = pick(keys, key, rounded(1.0 - fy), rounded(fy)).astype(bf16)
        sampled = jnp.dot(table, look, preferred_element_type=f32)
        share = pick(lane, col & 127, rounded(1.0 - fx), rounded(fx))
        cut = slice(j * LANES, (j + 1) * LANES)
        velocity_ref[0:1, cut] = jnp.sum(sampled[: LANES + 8] * share, 0, keepdims=True)
        velocity_ref[1:2, cut] = jnp.sum(sampled[LANES + 8 :] * share, 0, keepdims=True)


def local(pin_rows, pin_cols, pin_fracs, pin_weights, capacity, blockage, row_blocks, col_blocks):
    depth, width_part = capacity.shape
    parts, strips = lax.axis_size("cells"), lax.axis_size("strip")
    tiles = width_part // LANES
    height, width = depth * strips, width_part * parts
    pins = pin_rows.shape[0]
    by_lane = (pins // LANES, LANES)
    rows, cols = pin_rows.reshape(by_lane), pin_cols.reshape(by_lane)
    fracs, sizes = pin_fracs.reshape((2,) + by_lane), pin_weights.reshape(by_lane)
    vmem = pl.BlockSpec(memory_space=pltpu.VMEM)
    params = pltpu.CompilerParams(vmem_limit_bytes=60 * 1024 * 1024)

    codes = jnp.round((row_blocks - block_low) * (code_top / block_span))
    codes = (jnp.clip(codes, 0.0, code_top) - code_half).astype(jnp.int16).reshape(-1, LANES)
    codes = lax.all_gather(codes, "cells", axis=0, tiled=True)

    message = pl.pallas_call(
        functools.partial(splat_kernel, tiles, parts),
        out_shape=jax.ShapeDtypeStruct((2 * parts * depth, width_part), bf16),
        in_specs=[vmem] * 6,
        out_specs=vmem,
        compiler_params=params,
        name="splat",
    )(rows, cols, fracs, sizes, capacity, blockage)
    sent = lax.all_gather(message, ("strip", "cells"), axis=0, tiled=True)

    spot = jnp.stack([lax.axis_index("strip"), lax.axis_index("cells")]).astype(jnp.int32)
    final, velocity = pl.pallas_call(
        functools.partial(field_kernel, (depth, tiles, parts, strips)),
        out_shape=(
            jax.ShapeDtypeStruct((depth, width_part), f32),
            jax.ShapeDtypeStruct((2, pins), f32),
        ),
        in_specs=[pl.BlockSpec(memory_space=pltpu.SMEM)] + [vmem] * 6,
        out_specs=(vmem, vmem),
        scratch_shapes=[
            pltpu.VMEM((width // LANES, 2 * LANES, LANES), bf16),
            pltpu.VMEM((height, width), f32),
            pltpu.VMEM((height, width), f32),
            pltpu.VMEM((height + 16, width), f32),
        ],
        compiler_params=params,
        name="field",
    )(spot, sent, codes, col_blocks, rows, cols, fracs)
    return final, velocity


def solution(mesh):
    placed = (
        P(("strip", "cells")),
        P(("strip", "cells")),
        P(None, ("strip", "cells")),
        P(("strip", "cells")),
        P("strip", "cells"),
        P("strip", "cells"),
        P("cells", None, None),
        P(),
    )
    return jax.shard_map(
        local,
        mesh=mesh,
        in_specs=placed,
        out_specs=(P("strip", "cells"), P(None, ("strip", "cells"))),
        check_vma=False,
    )
```

```python
import functools

import jax
import jax.numpy as jnp
from jax import lax
from jax.experimental import pallas as pl
from jax.experimental.pallas import tpu as pltpu
from jax.sharding import PartitionSpec as P

SWEEPS = 3
STEPS = 2
LANES = 128
GROUP = 8

coupling = 2.0
floor_level = 0.5
block_low, block_span = -0.002, 0.152
weight_low, weight_span = 0.5, 3.5
term_low, term_octaves = -20.0, 34.0
code_top = 65535.0
code_half = 32768.0
remainder_span = 1.25 / code_top
log_two = 0.6931471805599453

f32 = jnp.float32
bf16 = jnp.bfloat16


def iota(shape, axis):
    return lax.broadcasted_iota(jnp.int32, shape, axis)


def halves(values):
    high = values.astype(bf16)
    return high, (values - high.astype(f32)).astype(bf16)


def last_dims(left, right):
    return lax.dot_general(left, right, (((1,), (1,)), ((), ())), preferred_element_type=f32)


def pick(index, first, near, far):
    return jnp.where(index == first, near, jnp.where(index == first + 1, far, 0.0))


def rounded(values):
    return values.astype(bf16).astype(f32)


def coded(share):
    return jnp.clip(jnp.round(share * code_top), 0.0, code_top) - code_half


def decoded(codes):
    return (codes.astype(f32) + code_half) * (1.0 / code_top)


def splat_kernel(
    tiles, parts, rows_ref, cols_ref, fracs_ref, pin_weights_ref, cap_ref, block_ref, row_blocks_ref, out_ref
):
    depth = cap_ref.shape[0]
    height = parts * depth
    rows, cols, sizes = rows_ref[...], cols_ref[...], pin_weights_ref[...]
    place = iota((height * (tiles + 1), LANES), 0)
    group, inner = place // height, place % height
    keys = ((inner // depth) * tiles + group - 1) * depth + inner % depth
    lane = iota((LANES + 8, LANES), 0)
    tables, lanes = [], []
    for j in range(rows.shape[0]):
        cut = slice(j * LANES, (j + 1) * LANES)
        fy, fx = fracs_ref[0:1, cut], fracs_ref[1:2, cut]
        size, col = sizes[j : j + 1], cols[j : j + 1]
        key = (col >> 7) * depth + rows[j : j + 1]
        tables.append(pick(keys, key, rounded(size * (1.0 - fy)), rounded(size * fy)).astype(bf16))
        lanes.append(pick(lane, col & 127, rounded(1.0 - fx), rounded(fx)).astype(bf16))
    total = last_dims(jnp.concatenate(tables, 1), jnp.concatenate(lanes, 1))
    first_lane = iota((height, LANES), 1) == 0
    share_rows = out_ref.shape[0] - 2 * height
    strip = lax.axis_index("strip")
    for t in range(tiles):
        own = total[(t + 1) * height : (t + 2) * height, :LANES]
        spill = total[t * height : (t + 1) * height, LANES : LANES + 1]
        own = own + jnp.where(first_lane, spill, 0.0)
        octave = jnp.log(jnp.maximum(own, 2.0**-40)) * (1.0 / log_two)
        cut = slice(t * LANES, (t + 1) * LANES)
        out_ref[:height, cut] = coded((octave - term_low) * (1.0 / term_octaves)).astype(jnp.int32).astype(jnp.int16)
        if share_rows:
            first = pl.multiple_of(strip * (share_rows * tiles) + t * share_rows, 8)
            block = row_blocks_ref[pl.ds(first, share_rows), :]
            code = coded((block - block_low) * (1.0 / block_span)).astype(jnp.int32)
            out_ref[2 * height :, cut] = code.astype(jnp.int16)
    weights = cap_ref[...].astype(f32) * (1.0 - block_ref[...])
    first = coded((weights - weight_low) * (1.0 / weight_span))
    remainder = weights - ((first + code_half) * (weight_span / code_top) + weight_low)
    second = coded(remainder * (1.0 / (weight_span * remainder_span)) + 0.5)
    rest = jnp.zeros((height - 2 * depth, weights.shape[1]), f32)
    out_ref[height : 2 * height, :] = jnp.concatenate([first, second, rest], 0).astype(jnp.int32).astype(jnp.int16)


def along_lines(values):
    width = values.shape[1]
    column = iota(values.shape, 1)
    left = jnp.where(column == 0, values, pltpu.roll(values, 1, 1))
    right = jnp.where(column == width - 1, values, pltpu.roll(values, width - 1, 1))
    return 2.0 * values - left - right


def across_lines(values):
    height = values.shape[0]
    row = iota(values.shape, 0)
    above = jnp.where(row == 0, values, pltpu.roll(values, 1, 0))
    below = jnp.where(row == height - 1, values, pltpu.roll(values, height - 1, 0))
    return 2.0 * values - above - below


def row_blockwise(residual, pairs_ref):
    high, low = halves(residual)
    result = []
    for k in range(pairs_ref.shape[0]):
        cut = slice(k * LANES, (k + 1) * LANES)
        pair = pairs_ref[k]
        both = last_dims(jnp.concatenate([high[:, cut], low[:, cut]], 1), jnp.concatenate([pair, pair], 1))
        result.append(both[:, :LANES] + both[:, LANES:])
    return jnp.concatenate(result, 1)


def col_blockwise(residual, blocks):
    high, low = halves(residual)
    count, size = len(blocks), blocks[0][0].shape[0]
    result = []
    for k, (block_high, block_low_part) in enumerate(blocks):
        cut = slice(k * size, (k + 1) * size)
        dot = functools.partial(jnp.dot, preferred_element_type=f32)
        result.append(dot(block_high, high[cut]) + (dot(block_low_part, high[cut]) + dot(block_high, low[cut])))
    return result[0] if count == 1 else jnp.concatenate(result, 0)


def each(count, body):
    if count == 1:
        body(0)
    else:
        pl.loop(0, count)(body)


def field_kernel(
    sizes, sent_ref, codes_ref, col_blocks_ref, rows_ref, cols_ref, fracs_ref,
    final_ref, velocity_ref, pairs, weights_ref, source_ref, field_ref,
):
    depth, tiles, parts, strips, share_rows = sizes
    width_part = tiles * LANES
    width = parts * width_part
    height = strips * depth
    chunk = min(GROUP, strips) * depth
    chunks = height // chunk
    strip, part = lax.axis_index("strip"), lax.axis_index("cells")

    sent_rows = 2 * parts * depth + share_rows
    held = LANES // share_rows if share_rows else 1

    def unpack(k):
        for n in range(held):
            if share_rows:
                index = k * held + n
                device = index // tiles % strips * parts + index // tiles // strips
                t = index % tiles
                code = sent_ref[
                    device * sent_rows + sent_rows - share_rows : (device + 1) * sent_rows, t * LANES : (t + 1) * LANES
                ]
            else:
                code = codes_ref[pl.ds(pl.multiple_of(k * LANES, LANES), LANES), :]
            size = code.shape[0]
            high, low = halves(decoded(code) * block_span + block_low)
            pairs[k, n * size : (n + 1) * size, :] = high
            pairs[k, LANES + n * size : LANES + (n + 1) * size, :] = low

    for k in range(pairs.shape[0]):
        unpack(k)

    first = parts * depth
    devices = chunk // depth * parts
    span = devices * sent_rows

    def choice(pick_side, slots, depth_slots):
        target, origin = iota((parts * chunk, devices * slots), 0), iota((parts * chunk, devices * slots), 1)
        device, slot = origin // slots, origin % slots
        row_here = target % chunk - (device // parts) * depth
        fits = (pick_side(device, slot) == target // chunk) & (slot % depth == row_here) & (slot < depth_slots)
        return jnp.where(fits, 1.0, 0.0).astype(bf16)

    term_choice = choice(lambda device, slot: slot // depth, first, first)
    weight_choice = choice(lambda device, slot: device % parts, 8, 2 * depth)

    def placed(chosen, values):
        high, low = halves(values)
        dot = functools.partial(jnp.dot, preferred_element_type=f32)
        return dot(chosen, high) + dot(chosen, low)

    @functools.partial(each, chunks)
    def place(g):
        terms, weights = [], []
        for device in range(devices):
            base = pl.multiple_of(g * span + device * sent_rows, 16)
            code = sent_ref[pl.ds(base, first), :].astype(f32)
            octave = (code + code_half) * (term_octaves / code_top) + term_low
            terms.append(jnp.where(code == -code_half, 0.0, jnp.exp(octave * log_two)))
            share = decoded(sent_ref[pl.ds(base + first, first), :][:8])
            weights.append(
                jnp.where(
                    iota(share.shape, 0) < depth,
                    share * weight_span + weight_low,
                    (share - 0.5) * (weight_span * remainder_span),
                )
            )
        term = placed(term_choice, jnp.concatenate(terms, 0))
        weight = placed(weight_choice, jnp.concatenate(weights, 0))
        here = pl.ds(pl.multiple_of(g * chunk, chunk), chunk)
        for p in range(parts):
            cut = slice(p * width_part, (p + 1) * width_part)
            weights_ref[here, cut] = weight[p * chunk : (p + 1) * chunk]
            source_ref[here, cut] = term[p * chunk : (p + 1) * chunk] / weight[p * chunk : (p + 1) * chunk]

    lanes_at_once = width if chunks == 1 else LANES
    col_blocks = [halves(col_blocks_ref[k]) for k in range(col_blocks_ref.shape[0])]
    inner = pl.ds(8, height)

    @functools.partial(each, width // lanes_at_once)
    def start(t):
        cut = pl.ds(pl.multiple_of(t * lanes_at_once, lanes_at_once), lanes_at_once)
        current = source_ref[:, cut]
        field_ref[inner, cut] = current
        source_ref[:, cut] = weights_ref[:, cut] * current - coupling * across_lines(current)

    for step in range(STEPS):

        @functools.partial(each, chunks)
        def solve_rows(g):
            here = pl.ds(pl.multiple_of(g * chunk, chunk), chunk)
            there = pl.ds(pl.multiple_of(g * chunk + 8, 8), chunk)
            source, weights, current = source_ref[here, :], weights_ref[here, :], field_ref[there, :]
            for sweep in range(SWEEPS):
                residual = source - (weights * current + coupling * along_lines(current))
                current = current + row_blockwise(residual, pairs)
            field_ref[there, :] = current
            source_ref[here, :] = weights * current - coupling * along_lines(current)

        @functools.partial(each, width // lanes_at_once)
        def solve_cols(t):
            cut = pl.ds(pl.multiple_of(t * lanes_at_once, lanes_at_once), lanes_at_once)
            middle, weights, current = source_ref[:, cut], weights_ref[:, cut], field_ref[inner, cut]
            for sweep in range(SWEEPS):
                residual = middle - (weights * current + coupling * across_lines(current))
                current = current + col_blockwise(residual, col_blocks)
            field_ref[inner, cut] = current
            if step + 1 < STEPS:
                source_ref[:, cut] = weights * current - coupling * across_lines(current)
            else:
                field_ref[:8, cut] = jnp.broadcast_to(current[:1], (8, lanes_at_once))
                field_ref[height + 8 :, cut] = jnp.broadcast_to(current[-1:], (8, lanes_at_once))

    row0 = strip * depth
    columns = pl.ds(pl.multiple_of(part * width_part, LANES), width_part)
    base, shift = pl.multiple_of(row0 // 8 * 8, 8), 17 - row0 % 8
    final_ref[...] = pltpu.roll(field_ref[pl.ds(base, 24), columns], shift, 0)[1 : 1 + depth]

    window = pltpu.roll(field_ref[pl.ds(base, 24), :], shift, 0)
    above, centre, below = window[:8], pltpu.roll(window, 23, 0)[:8], pltpu.roll(window, 22, 0)[:8]
    column = iota(centre.shape, 1)
    left = jnp.where(column == 0, centre, pltpu.roll(centre, 1, 1))
    right = jnp.where(column == width - 1, centre, pltpu.roll(centre, width - 1, 1))
    scale = jnp.maximum(centre, floor_level)
    velocity_y = rounded(-(0.5 * (below - above)) / scale)
    velocity_x = rounded(-(0.5 * (right - left)) / scale)

    upper = iota((8, LANES), 0) < depth

    def stacked(values):
        stack = []
        for t in range(0, parts * tiles, 2):
            even = values[:, t * LANES : (t + 1) * LANES]
            odd = values[:, (t + 1) * LANES : (t + 2) * LANES]
            stack.append(jnp.where(upper, even, pltpu.roll(odd, depth, 0)))
        return jnp.concatenate(stack, 0)

    stack_y, stack_x = stacked(velocity_y), stacked(velocity_x)
    many = stack_y.shape[0]
    next_y = pltpu.roll(stack_y, many - depth, 0)
    next_x = pltpu.roll(stack_x, many - depth, 0)
    turned = [stack_y.T, next_y.T[:8], stack_x.T, next_x.T[:8]]
    table = jnp.concatenate(turned, 0).astype(bf16)
    rows, cols = rows_ref[...], cols_ref[...]
    keys, lane = iota((many, LANES), 0), iota((LANES + 8, LANES), 0)
    for j in range(rows.shape[0]):
        cut = slice(j * LANES, (j + 1) * LANES)
        fy, fx = fracs_ref[0:1, cut], fracs_ref[1:2, cut]
        col = cols[j : j + 1]
        key = (col >> 7) * depth + rows[j : j + 1]
        look = pick(keys, key, rounded(1.0 - fy), rounded(fy)).astype(bf16)
        sampled = jnp.dot(table, look, preferred_element_type=f32)
        share = pick(lane, col & 127, rounded(1.0 - fx), rounded(fx))
        velocity_ref[0:1, cut] = jnp.sum(sampled[: LANES + 8] * share, 0, keepdims=True)
        velocity_ref[1:2, cut] = jnp.sum(sampled[LANES + 8 :] * share, 0, keepdims=True)


def local(pin_rows, pin_cols, pin_fracs, pin_weights, capacity, blockage, row_blocks, col_blocks):
    depth, width_part = capacity.shape
    parts, strips = lax.axis_size("cells"), lax.axis_size("strip")
    tiles = width_part // LANES
    height, width = depth * strips, width_part * parts
    pins = pin_rows.shape[0]
    by_lane = (pins // LANES, LANES)
    rows, cols = pin_rows.reshape(by_lane), pin_cols.reshape(by_lane)
    sizes = pin_weights.reshape(by_lane)
    vmem = pl.BlockSpec(memory_space=pltpu.VMEM)
    params = pltpu.CompilerParams(vmem_limit_bytes=60 * 1024 * 1024)

    flat_blocks = row_blocks.reshape(-1, LANES)
    share_rows = flat_blocks.shape[0] // (strips * tiles)
    if share_rows % 16 or share_rows * strips * tiles != flat_blocks.shape[0]:
        share_rows = 0
    message = pl.pallas_call(
        functools.partial(splat_kernel, tiles, parts),
        out_shape=jax.ShapeDtypeStruct((2 * parts * depth + share_rows, width_part), jnp.int16),
        in_specs=[vmem] * 7,
        out_specs=vmem,
        compiler_params=params,
        name="splat",
    )(rows, cols, pin_fracs, sizes, capacity, blockage, flat_blocks)
    sent = lax.all_gather(message, ("strip", "cells"), axis=0, tiled=True)
    if share_rows:
        codes = jnp.zeros((16, LANES), jnp.int16)
    else:
        codes = coded((flat_blocks - block_low) * (1.0 / block_span)).astype(jnp.int16)
        codes = lax.all_gather(codes, "cells", axis=0, tiled=True)

    final, velocity = pl.pallas_call(
        functools.partial(field_kernel, (depth, tiles, parts, strips, share_rows)),
        out_shape=(
            jax.ShapeDtypeStruct((depth, width_part), f32),
            jax.ShapeDtypeStruct((2, pins), f32),
        ),
        in_specs=[vmem] * 6,
        out_specs=(vmem, vmem),
        scratch_shapes=[
            pltpu.VMEM((width // LANES, 2 * LANES, LANES), bf16),
            pltpu.VMEM((height, width), f32),
            pltpu.VMEM((height, width), f32),
            pltpu.VMEM((height + 16, width), f32),
        ],
        compiler_params=params,
        name="field",
    )(sent, codes, col_blocks, rows, cols, pin_fracs)
    return final, velocity


def solution(mesh):
    placed = (
        P(("strip", "cells")),
        P(("strip", "cells")),
        P(None, ("strip", "cells")),
        P(("strip", "cells")),
        P("strip", "cells"),
        P("strip", "cells"),
        P("cells", None, None),
        P(),
    )
    return jax.shard_map(
        local,
        mesh=mesh,
        in_specs=placed,
        out_specs=(P("strip", "cells"), P(None, ("strip", "cells"))),
        check_vma=False,
    )
```

```python
import functools

import jax
import jax.numpy as jnp
from jax import lax
from jax.experimental import pallas as pl
from jax.experimental.pallas import tpu as pltpu
from jax.sharding import PartitionSpec as P

SWEEPS = 3
STEPS = 2
LANES = 128
GROUP = 8

coupling = 2.0
floor_level = 0.5
weight_low, weight_span = 0.5, 3.5
term_low, term_octaves = -20.0, 34.0
code_top = 65535.0
code_half = 32768.0
log_two = 0.6931471805599453

f32 = jnp.float32
bf16 = jnp.bfloat16


def iota(shape, axis):
    return lax.broadcasted_iota(jnp.int32, shape, axis)


def halves(values):
    high = values.astype(bf16)
    return high, (values - high.astype(f32)).astype(bf16)


def last_dims(left, right):
    return lax.dot_general(left, right, (((1,), (1,)), ((), ())), preferred_element_type=f32)


def pick(index, first, near, far):
    return jnp.where(index == first, near, jnp.where(index == first + 1, far, 0.0))


def rounded(values):
    return values.astype(bf16).astype(f32)


def coded(share):
    return jnp.clip(jnp.round(share * code_top), 0.0, code_top) - code_half


def stored(codes):
    return codes.astype(jnp.int32).astype(jnp.int16)


def density_codes(values):
    octave = jnp.log(jnp.maximum(values, 2.0**-40)) * (1.0 / log_two)
    return stored(coded((octave - term_low) * (1.0 / term_octaves)))


def densities(codes):
    codes = codes.astype(f32)
    octave = (codes + code_half) * (term_octaves / code_top) + term_low
    return jnp.where(codes == -code_half, 0.0, jnp.exp(octave * log_two))


def splat_kernel(
    tiles, parts, rows_ref, cols_ref, fracs_ref, pin_weights_ref, cap_ref, block_ref, out_ref
):
    depth = cap_ref.shape[0]
    height = parts * depth
    rows, cols, sizes = rows_ref[...], cols_ref[...], pin_weights_ref[...]
    place = iota((height * (tiles + 1), LANES), 0)
    group, inner = place // height, place % height
    keys = ((inner // depth) * tiles + group - 1) * depth + inner % depth
    lane = iota((LANES + 8, LANES), 0)
    tables, lanes = [], []
    for j in range(rows.shape[0]):
        cut = slice(j * LANES, (j + 1) * LANES)
        fy, fx = fracs_ref[0:1, cut], fracs_ref[1:2, cut]
        size, col = sizes[j : j + 1], cols[j : j + 1]
        key = (col >> 7) * depth + rows[j : j + 1]
        tables.append(pick(keys, key, rounded(size * (1.0 - fy)), rounded(size * fy)).astype(bf16))
        lanes.append(pick(lane, col & 127, rounded(1.0 - fx), rounded(fx)).astype(bf16))
    total = last_dims(jnp.concatenate(tables, 1), jnp.concatenate(lanes, 1))
    first_lane = iota((height, LANES), 1) == 0
    for t in range(tiles):
        own = total[(t + 1) * height : (t + 2) * height, :LANES]
        spill = total[t * height : (t + 1) * height, LANES : LANES + 1]
        own = own + jnp.where(first_lane, spill, 0.0)
        out_ref[:height, t * LANES : (t + 1) * LANES] = density_codes(own)
    weights = cap_ref[...].astype(f32) * (1.0 - block_ref[...])
    code = coded((weights - weight_low) * (1.0 / weight_span))
    row = iota((height, weights.shape[1]), 0)
    mine = row // depth == lax.axis_index("cells")
    out_ref[height:, :] = stored(jnp.where(mine, jnp.concatenate([code] * parts, 0), 0.0))


def sum_kernel(sent_ref, out_ref):
    height = out_ref.shape[0] // 2
    terms, codes = 0.0, 0.0
    for base in range(0, sent_ref.shape[0], 2 * height):
        terms += densities(sent_ref[base : base + height, :])
        codes += sent_ref[base + height : base + 2 * height, :].astype(f32)
    out_ref[:height, :] = density_codes(terms)
    out_ref[height:, :] = stored(codes)


def along_lines(values):
    width = values.shape[1]
    column = iota(values.shape, 1)
    left = jnp.where(column == 0, values, pltpu.roll(values, 1, 1))
    right = jnp.where(column == width - 1, values, pltpu.roll(values, width - 1, 1))
    return 2.0 * values - left - right


def across_lines(values):
    height = values.shape[0]
    row = iota(values.shape, 0)
    above = jnp.where(row == 0, values, pltpu.roll(values, 1, 0))
    below = jnp.where(row == height - 1, values, pltpu.roll(values, height - 1, 0))
    return 2.0 * values - above - below


def row_blockwise(residual, pairs_ref):
    high, low = halves(residual)
    result = []
    for k in range(pairs_ref.shape[0]):
        cut = slice(k * LANES, (k + 1) * LANES)
        pair = pairs_ref[k]
        both = last_dims(jnp.concatenate([high[:, cut], low[:, cut]], 1), jnp.concatenate([pair, pair], 1))
        result.append(both[:, :LANES] + both[:, LANES:])
    return jnp.concatenate(result, 1)


def col_blockwise(residual, blocks):
    high, low = halves(residual)
    count, size = len(blocks), blocks[0][0].shape[0]
    result = []
    for k, (block_high, block_low_part) in enumerate(blocks):
        cut = slice(k * size, (k + 1) * size)
        dot = functools.partial(jnp.dot, preferred_element_type=f32)
        result.append(dot(block_high, high[cut]) + (dot(block_low_part, high[cut]) + dot(block_high, low[cut])))
    return result[0] if count == 1 else jnp.concatenate(result, 0)


def each(count, body):
    if count == 1:
        body(0)
    else:
        pl.loop(0, count)(body)


def field_kernel(
    sizes, sent_ref, blocks_ref, col_blocks_ref, rows_ref, cols_ref, fracs_ref,
    final_ref, velocity_ref, pairs, weights_ref, source_ref, field_ref,
):
    depth, tiles, parts, strips = sizes
    width_part = tiles * LANES
    width = parts * width_part
    height = strips * depth
    chunk = min(GROUP, strips) * depth
    chunks = height // chunk
    strip, part = lax.axis_index("strip"), lax.axis_index("cells")

    for k in range(pairs.shape[0]):
        high, low = halves(blocks_ref[k * LANES : (k + 1) * LANES, :])
        pairs[k, :LANES, :] = high
        pairs[k, LANES:, :] = low

    slots = parts * depth
    group = chunk // depth
    target, origin = iota((parts * chunk, group * slots), 0), iota((parts * chunk, group * slots), 1)
    slot = origin % slots
    fits = (slot // depth == target // chunk) & (origin // slots * depth + slot % depth == target % chunk)
    chosen = jnp.where(fits, 1.0, 0.0).astype(bf16)

    def placed(values):
        high, low = halves(jnp.concatenate(values, 0))
        dot = functools.partial(jnp.dot, preferred_element_type=f32)
        return dot(chosen, high) + dot(chosen, low)

    @functools.partial(each, chunks)
    def place(g):
        terms, codes = [], []
        for n in range(group):
            base = pl.multiple_of((g * group + n) * (2 * slots), 2 * slots)
            terms.append(densities(sent_ref[pl.ds(base, slots), :]))
            codes.append(sent_ref[pl.ds(base + slots, slots), :].astype(f32))
        term = placed(terms)
        weight = (placed(codes) + code_half) * (weight_span / code_top) + weight_low
        here = pl.ds(pl.multiple_of(g * chunk, chunk), chunk)
        for p in range(parts):
            cut = slice(p * width_part, (p + 1) * width_part)
            weights_ref[here, cut] = weight[p * chunk : (p + 1) * chunk]
            source_ref[here, cut] = term[p * chunk : (p + 1) * chunk] / weight[p * chunk : (p + 1) * chunk]

    lanes_at_once = width if chunks == 1 else LANES
    col_blocks = [halves(col_blocks_ref[k]) for k in range(col_blocks_ref.shape[0])]
    inner = pl.ds(8, height)

    @functools.partial(each, width // lanes_at_once)
    def start(t):
        cut = pl.ds(pl.multiple_of(t * lanes_at_once, lanes_at_once), lanes_at_once)
        current = source_ref[:, cut]
        field_ref[inner, cut] = current
        source_ref[:, cut] = weights_ref[:, cut] * current - coupling * across_lines(current)

    for step in range(STEPS):

        @functools.partial(each, chunks)
        def solve_rows(g):
            here = pl.ds(pl.multiple_of(g * chunk, chunk), chunk)
            there = pl.ds(pl.multiple_of(g * chunk + 8, 8), chunk)
            source, weights, current = source_ref[here, :], weights_ref[here, :], field_ref[there, :]
            for sweep in range(SWEEPS):
                residual = source - (weights * current + coupling * along_lines(current))
                current = current + row_blockwise(residual, pairs)
            field_ref[there, :] = current
            source_ref[here, :] = weights * current - coupling * along_lines(current)

        @functools.partial(each, width // lanes_at_once)
        def solve_cols(t):
            cut = pl.ds(pl.multiple_of(t * lanes_at_once, lanes_at_once), lanes_at_once)
            middle, weights, current = source_ref[:, cut], weights_ref[:, cut], field_ref[inner, cut]
            for sweep in range(SWEEPS):
                residual = middle - (weights * current + coupling * across_lines(current))
                current = current + col_blockwise(residual, col_blocks)
            field_ref[inner, cut] = current
            if step + 1 < STEPS:
                source_ref[:, cut] = weights * current - coupling * across_lines(current)
            else:
                field_ref[:8, cut] = jnp.broadcast_to(current[:1], (8, lanes_at_once))
                field_ref[height + 8 :, cut] = jnp.broadcast_to(current[-1:], (8, lanes_at_once))

    row0 = strip * depth
    columns = pl.ds(pl.multiple_of(part * width_part, LANES), width_part)
    base, shift = pl.multiple_of(row0 // 8 * 8, 8), 17 - row0 % 8
    final_ref[...] = pltpu.roll(field_ref[pl.ds(base, 24), columns], shift, 0)[1 : 1 + depth]

    window = pltpu.roll(field_ref[pl.ds(base, 24), :], shift, 0)
    above, centre, below = window[:8], pltpu.roll(window, 23, 0)[:8], pltpu.roll(window, 22, 0)[:8]
    column = iota(centre.shape, 1)
    left = jnp.where(column == 0, centre, pltpu.roll(centre, 1, 1))
    right = jnp.where(column == width - 1, centre, pltpu.roll(centre, width - 1, 1))
    scale = jnp.maximum(centre, floor_level)
    velocity_y = rounded(-(0.5 * (below - above)) / scale)
    velocity_x = rounded(-(0.5 * (right - left)) / scale)

    upper = iota((8, LANES), 0) < depth

    def stacked(values):
        stack = []
        for t in range(0, parts * tiles, 2):
            even = values[:, t * LANES : (t + 1) * LANES]
            odd = values[:, (t + 1) * LANES : (t + 2) * LANES]
            stack.append(jnp.where(upper, even, pltpu.roll(odd, depth, 0)))
        return jnp.concatenate(stack, 0)

    stack_y, stack_x = stacked(velocity_y), stacked(velocity_x)
    many = stack_y.shape[0]
    next_y = pltpu.roll(stack_y, many - depth, 0)
    next_x = pltpu.roll(stack_x, many - depth, 0)
    turned = [stack_y.T, next_y.T[:8], stack_x.T, next_x.T[:8]]
    table = jnp.concatenate(turned, 0).astype(bf16)
    rows, cols = rows_ref[...], cols_ref[...]
    keys, lane = iota((many, LANES), 0), iota((LANES + 8, LANES), 0)
    for j in range(rows.shape[0]):
        cut = slice(j * LANES, (j + 1) * LANES)
        fy, fx = fracs_ref[0:1, cut], fracs_ref[1:2, cut]
        col = cols[j : j + 1]
        key = (col >> 7) * depth + rows[j : j + 1]
        look = pick(keys, key, rounded(1.0 - fy), rounded(fy)).astype(bf16)
        sampled = jnp.dot(table, look, preferred_element_type=f32)
        share = pick(lane, col & 127, rounded(1.0 - fx), rounded(fx))
        velocity_ref[0:1, cut] = jnp.sum(sampled[: LANES + 8] * share, 0, keepdims=True)
        velocity_ref[1:2, cut] = jnp.sum(sampled[LANES + 8 :] * share, 0, keepdims=True)


def local(pin_rows, pin_cols, pin_fracs, pin_weights, capacity, blockage, row_blocks, col_blocks):
    depth, width_part = capacity.shape
    parts, strips = lax.axis_size("cells"), lax.axis_size("strip")
    tiles = width_part // LANES
    height, width = depth * strips, width_part * parts
    pins = pin_rows.shape[0]
    by_lane = (pins // LANES, LANES)
    rows, cols = pin_rows.reshape(by_lane), pin_cols.reshape(by_lane)
    sizes = pin_weights.reshape(by_lane)
    vmem = pl.BlockSpec(memory_space=pltpu.VMEM)
    params = pltpu.CompilerParams(vmem_limit_bytes=60 * 1024 * 1024)

    blocks = lax.all_gather(row_blocks.reshape(-1, LANES), "cells", axis=0, tiled=True)
    carried = jax.ShapeDtypeStruct((2 * parts * depth, width_part), jnp.int16)
    terms = pl.pallas_call(
        functools.partial(splat_kernel, tiles, parts),
        out_shape=carried,
        in_specs=[vmem] * 6,
        out_specs=vmem,
        compiler_params=params,
        name="splat",
    )(rows, cols, pin_fracs, sizes, capacity, blockage)
    sums = pl.pallas_call(
        sum_kernel, out_shape=carried, in_specs=[vmem], out_specs=vmem, compiler_params=params, name="sum_terms"
    )(lax.all_gather(terms, "cells", axis=0, tiled=True))
    sent = lax.all_gather(sums, "strip", axis=0, tiled=True)

    final, velocity = pl.pallas_call(
        functools.partial(field_kernel, (depth, tiles, parts, strips)),
        out_shape=(
            jax.ShapeDtypeStruct((depth, width_part), f32),
            jax.ShapeDtypeStruct((2, pins), f32),
        ),
        in_specs=[vmem] * 6,
        out_specs=(vmem, vmem),
        scratch_shapes=[
            pltpu.VMEM((width // LANES, 2 * LANES, LANES), bf16),
            pltpu.VMEM((height, width), f32),
            pltpu.VMEM((height, width), f32),
            pltpu.VMEM((height + 16, width), f32),
        ],
        compiler_params=params,
        name="field",
    )(sent, blocks, col_blocks, rows, cols, pin_fracs)
    return final, velocity


def solution(mesh):
    placed = (
        P(("strip", "cells")),
        P(("strip", "cells")),
        P(None, ("strip", "cells")),
        P(("strip", "cells")),
        P("strip", "cells"),
        P("strip", "cells"),
        P("cells", None, None),
        P(),
    )
    return jax.shard_map(
        local,
        mesh=mesh,
        in_specs=placed,
        out_specs=(P("strip", "cells"), P(None, ("strip", "cells"))),
        check_vma=False,
    )
```

```python
import functools

import jax
import jax.numpy as jnp
from jax import lax
from jax.experimental import pallas as pl
from jax.experimental.pallas import tpu as pltpu
from jax.sharding import PartitionSpec as P

SWEEPS = 3
STEPS = 2
LANES = 128
GROUP = 8

coupling = 2.0
floor_level = 0.5
weight_low, weight_span = 0.5, 3.5
term_low, term_octaves = -20.0, 34.0
code_top = 65535.0
code_half = 32768.0
log_two = 0.6931471805599453

f32 = jnp.float32
bf16 = jnp.bfloat16


def iota(shape, axis):
    return lax.broadcasted_iota(jnp.int32, shape, axis)


def halves(values):
    high = values.astype(bf16)
    return high, (values - high.astype(f32)).astype(bf16)


def last_dims(left, right):
    return lax.dot_general(left, right, (((1,), (1,)), ((), ())), preferred_element_type=f32)


def pick(index, first, near, far):
    return jnp.where(index == first, near, jnp.where(index == first + 1, far, 0.0))


def rounded(values):
    return values.astype(bf16).astype(f32)


def coded(share):
    return jnp.clip(jnp.round(share * code_top), 0.0, code_top) - code_half


def stored(codes):
    return codes.astype(jnp.int32).astype(jnp.int16)


def density_codes(values):
    octave = jnp.log(jnp.maximum(values, 2.0**-40)) * (1.0 / log_two)
    return stored(coded((octave - term_low) * (1.0 / term_octaves)))


def densities(codes):
    codes = codes.astype(f32)
    octave = (codes + code_half) * (term_octaves / code_top) + term_low
    return jnp.where(codes == -code_half, 0.0, jnp.exp(octave * log_two))


def splat_kernel(
    tiles, parts, rows_ref, cols_ref, fracs_ref, pin_weights_ref, cap_ref, block_ref, out_ref
):
    depth = cap_ref.shape[0]
    height = parts * depth
    rows, cols, sizes = rows_ref[...], cols_ref[...], pin_weights_ref[...]
    place = iota((height * (tiles + 1), LANES), 0)
    group, inner = place // height, place % height
    keys = ((inner // depth) * tiles + group - 1) * depth + inner % depth
    lane = iota((LANES + 8, LANES), 0)
    tables, lanes = [], []
    for j in range(rows.shape[0]):
        cut = slice(j * LANES, (j + 1) * LANES)
        fy, fx = fracs_ref[0:1, cut], fracs_ref[1:2, cut]
        size, col = sizes[j : j + 1], cols[j : j + 1]
        key = (col >> 7) * depth + rows[j : j + 1]
        tables.append(pick(keys, key, rounded(size * (1.0 - fy)), rounded(size * fy)).astype(bf16))
        lanes.append(pick(lane, col & 127, rounded(1.0 - fx), rounded(fx)).astype(bf16))
    total = last_dims(jnp.concatenate(tables, 1), jnp.concatenate(lanes, 1))
    first_lane = iota((height, LANES), 1) == 0
    for t in range(tiles):
        own = total[(t + 1) * height : (t + 2) * height, :LANES]
        spill = total[t * height : (t + 1) * height, LANES : LANES + 1]
        own = own + jnp.where(first_lane, spill, 0.0)
        out_ref[:height, t * LANES : (t + 1) * LANES] = density_codes(own)
    weights = cap_ref[...].astype(f32) * (1.0 - block_ref[...])
    code = coded((weights - weight_low) * (1.0 / weight_span))
    row = iota((height, weights.shape[1]), 0)
    mine = row // depth == lax.axis_index("cells")
    out_ref[height:, :] = stored(jnp.where(mine, jnp.concatenate([code] * parts, 0), 0.0))


def sum_kernel(sent_ref, out_ref):
    rows = out_ref.shape[1]
    height = rows // 2
    terms, codes = 0.0, 0.0
    for base in range(0, sent_ref.shape[0], rows):
        terms += densities(sent_ref[base : base + height, :])
        codes += sent_ref[base + height : base + rows, :].astype(f32)
    message = jnp.concatenate([density_codes(terms), stored(codes)], 0)

    def write(n):
        out_ref[n] = message

    for n in range(out_ref.shape[0]):
        write(n)


def along_lines(values):
    width = values.shape[1]
    column = iota(values.shape, 1)
    left = jnp.where(column == 0, values, pltpu.roll(values, 1, 1))
    right = jnp.where(column == width - 1, values, pltpu.roll(values, width - 1, 1))
    return 2.0 * values - left - right


def across_lines(values):
    height = values.shape[0]
    row = iota(values.shape, 0)
    above = jnp.where(row == 0, values, pltpu.roll(values, 1, 0))
    below = jnp.where(row == height - 1, values, pltpu.roll(values, height - 1, 0))
    return 2.0 * values - above - below


def row_blockwise(residual, pairs_ref):
    high, low = halves(residual)
    result = []
    for k in range(pairs_ref.shape[0]):
        cut = slice(k * LANES, (k + 1) * LANES)
        pair = pairs_ref[k]
        both = last_dims(jnp.concatenate([high[:, cut], low[:, cut]], 1), jnp.concatenate([pair, pair], 1))
        result.append(both[:, :LANES] + both[:, LANES:])
    return jnp.concatenate(result, 1)


def col_blockwise(residual, blocks):
    high, low = halves(residual)
    count, size = len(blocks), blocks[0][0].shape[0]
    result = []
    for k, (block_high, block_low_part) in enumerate(blocks):
        cut = slice(k * size, (k + 1) * size)
        dot = functools.partial(jnp.dot, preferred_element_type=f32)
        result.append(dot(block_high, high[cut]) + (dot(block_low_part, high[cut]) + dot(block_high, low[cut])))
    return result[0] if count == 1 else jnp.concatenate(result, 0)


def each(count, body):
    if count == 1:
        body(0)
    else:
        pl.loop(0, count)(body)


def field_kernel(
    sizes, sent_ref, blocks_ref, col_blocks_ref, rows_ref, cols_ref, fracs_ref,
    final_ref, velocity_ref, pairs, weights_ref, source_ref, field_ref,
):
    depth, tiles, parts, strips = sizes
    width_part = tiles * LANES
    width = parts * width_part
    height = strips * depth
    chunk = min(GROUP, strips) * depth
    chunks = height // chunk
    strip, part = lax.axis_index("strip"), lax.axis_index("cells")

    for k in range(pairs.shape[0]):
        high, low = halves(blocks_ref[k * LANES : (k + 1) * LANES, :])
        pairs[k, :LANES, :] = high
        pairs[k, LANES:, :] = low

    slots = parts * depth
    group = chunk // depth
    target, origin = iota((parts * chunk, group * slots), 0), iota((parts * chunk, group * slots), 1)
    slot = origin % slots
    fits = (slot // depth == target // chunk) & (origin // slots * depth + slot % depth == target % chunk)
    chosen = jnp.where(fits, 1.0, 0.0).astype(bf16)

    def placed(values):
        high, low = halves(jnp.concatenate(values, 0))
        dot = functools.partial(jnp.dot, preferred_element_type=f32)
        return dot(chosen, high) + dot(chosen, low)

    @functools.partial(each, chunks)
    def place(g):
        terms, codes = [], []
        for n in range(group):
            base = pl.multiple_of((g * group + n) * (2 * slots), 2 * slots)
            terms.append(densities(sent_ref[pl.ds(base, slots), :]))
            codes.append(sent_ref[pl.ds(base + slots, slots), :].astype(f32))
        term = placed(terms)
        weight = (placed(codes) + code_half) * (weight_span / code_top) + weight_low
        here = pl.ds(pl.multiple_of(g * chunk, chunk), chunk)
        for p in range(parts):
            cut = slice(p * width_part, (p + 1) * width_part)
            weights_ref[here, cut] = weight[p * chunk : (p + 1) * chunk]
            source_ref[here, cut] = term[p * chunk : (p + 1) * chunk] / weight[p * chunk : (p + 1) * chunk]

    lanes_at_once = width if chunks == 1 else LANES
    col_blocks = [halves(col_blocks_ref[k]) for k in range(col_blocks_ref.shape[0])]
    inner = pl.ds(8, height)

    @functools.partial(each, width // lanes_at_once)
    def start(t):
        cut = pl.ds(pl.multiple_of(t * lanes_at_once, lanes_at_once), lanes_at_once)
        current = source_ref[:, cut]
        field_ref[inner, cut] = current
        source_ref[:, cut] = weights_ref[:, cut] * current - coupling * across_lines(current)

    for step in range(STEPS):

        @functools.partial(each, chunks)
        def solve_rows(g):
            here = pl.ds(pl.multiple_of(g * chunk, chunk), chunk)
            there = pl.ds(pl.multiple_of(g * chunk + 8, 8), chunk)
            source, weights, current = source_ref[here, :], weights_ref[here, :], field_ref[there, :]
            for sweep in range(SWEEPS):
                residual = source - (weights * current + coupling * along_lines(current))
                current = current + row_blockwise(residual, pairs)
            field_ref[there, :] = current
            source_ref[here, :] = weights * current - coupling * along_lines(current)

        @functools.partial(each, width // lanes_at_once)
        def solve_cols(t):
            cut = pl.ds(pl.multiple_of(t * lanes_at_once, lanes_at_once), lanes_at_once)
            middle, weights, current = source_ref[:, cut], weights_ref[:, cut], field_ref[inner, cut]
            for sweep in range(SWEEPS):
                residual = middle - (weights * current + coupling * across_lines(current))
                current = current + col_blockwise(residual, col_blocks)
            field_ref[inner, cut] = current
            if step + 1 < STEPS:
                source_ref[:, cut] = weights * current - coupling * across_lines(current)
            else:
                field_ref[:8, cut] = jnp.broadcast_to(current[:1], (8, lanes_at_once))
                field_ref[height + 8 :, cut] = jnp.broadcast_to(current[-1:], (8, lanes_at_once))

    row0 = strip * depth
    columns = pl.ds(pl.multiple_of(part * width_part, LANES), width_part)
    base, shift = pl.multiple_of(row0 // 8 * 8, 8), 17 - row0 % 8
    final_ref[...] = pltpu.roll(field_ref[pl.ds(base, 24), columns], shift, 0)[1 : 1 + depth]

    window = pltpu.roll(field_ref[pl.ds(base, 24), :], shift, 0)
    above, centre, below = window[:8], pltpu.roll(window, 23, 0)[:8], pltpu.roll(window, 22, 0)[:8]
    column = iota(centre.shape, 1)
    left = jnp.where(column == 0, centre, pltpu.roll(centre, 1, 1))
    right = jnp.where(column == width - 1, centre, pltpu.roll(centre, width - 1, 1))
    scale = jnp.maximum(centre, floor_level)
    velocity_y = rounded(-(0.5 * (below - above)) / scale)
    velocity_x = rounded(-(0.5 * (right - left)) / scale)

    upper = iota((8, LANES), 0) < depth

    def stacked(values):
        stack = []
        for t in range(0, parts * tiles, 2):
            even = values[:, t * LANES : (t + 1) * LANES]
            odd = values[:, (t + 1) * LANES : (t + 2) * LANES]
            stack.append(jnp.where(upper, even, pltpu.roll(odd, depth, 0)))
        return jnp.concatenate(stack, 0)

    stack_y, stack_x = stacked(velocity_y), stacked(velocity_x)
    many = stack_y.shape[0]
    next_y = pltpu.roll(stack_y, many - depth, 0)
    next_x = pltpu.roll(stack_x, many - depth, 0)
    turned = [stack_y.T, next_y.T[:8], stack_x.T, next_x.T[:8]]
    table = jnp.concatenate(turned, 0).astype(bf16)
    rows, cols = rows_ref[...], cols_ref[...]
    keys, lane = iota((many, LANES), 0), iota((LANES + 8, LANES), 0)
    for j in range(rows.shape[0]):
        cut = slice(j * LANES, (j + 1) * LANES)
        fy, fx = fracs_ref[0:1, cut], fracs_ref[1:2, cut]
        col = cols[j : j + 1]
        key = (col >> 7) * depth + rows[j : j + 1]
        look = pick(keys, key, rounded(1.0 - fy), rounded(fy)).astype(bf16)
        sampled = jnp.dot(table, look, preferred_element_type=f32)
        share = pick(lane, col & 127, rounded(1.0 - fx), rounded(fx))
        velocity_ref[0:1, cut] = jnp.sum(sampled[: LANES + 8] * share, 0, keepdims=True)
        velocity_ref[1:2, cut] = jnp.sum(sampled[LANES + 8 :] * share, 0, keepdims=True)


def local(pin_rows, pin_cols, pin_fracs, pin_weights, capacity, blockage, row_blocks, col_blocks):
    depth, width_part = capacity.shape
    parts, strips = lax.axis_size("cells"), lax.axis_size("strip")
    tiles = width_part // LANES
    height, width = depth * strips, width_part * parts
    pins = pin_rows.shape[0]
    by_lane = (pins // LANES, LANES)
    rows, cols = pin_rows.reshape(by_lane), pin_cols.reshape(by_lane)
    sizes = pin_weights.reshape(by_lane)
    vmem = pl.BlockSpec(memory_space=pltpu.VMEM)
    params = pltpu.CompilerParams(vmem_limit_bytes=60 * 1024 * 1024)

    blocks = lax.all_gather(row_blocks.reshape(-1, LANES), "cells", axis=0, tiled=True)
    carried = jax.ShapeDtypeStruct((2 * parts * depth, width_part), jnp.int16)
    terms = pl.pallas_call(
        functools.partial(splat_kernel, tiles, parts),
        out_shape=carried,
        in_specs=[vmem] * 6,
        out_specs=vmem,
        compiler_params=params,
        name="splat",
    )(rows, cols, pin_fracs, sizes, capacity, blockage)
    sums = pl.pallas_call(
        sum_kernel,
        out_shape=jax.ShapeDtypeStruct((strips,) + carried.shape, jnp.int16),
        in_specs=[vmem],
        out_specs=vmem,
        compiler_params=params,
        name="sum_terms",
    )(lax.all_gather(terms, "cells", axis=0, tiled=True))
    sent = lax.all_to_all(sums, "strip", split_axis=0, concat_axis=0, tiled=True).reshape(-1, width_part)

    final, velocity = pl.pallas_call(
        functools.partial(field_kernel, (depth, tiles, parts, strips)),
        out_shape=(
            jax.ShapeDtypeStruct((depth, width_part), f32),
            jax.ShapeDtypeStruct((2, pins), f32),
        ),
        in_specs=[vmem] * 6,
        out_specs=(vmem, vmem),
        scratch_shapes=[
            pltpu.VMEM((width // LANES, 2 * LANES, LANES), bf16),
            pltpu.VMEM((height, width), f32),
            pltpu.VMEM((height, width), f32),
            pltpu.VMEM((height + 16, width), f32),
        ],
        compiler_params=params,
        name="field",
    )(sent, blocks, col_blocks, rows, cols, pin_fracs)
    return final, velocity


def solution(mesh):
    placed = (
        P(("strip", "cells")),
        P(("strip", "cells")),
        P(None, ("strip", "cells")),
        P(("strip", "cells")),
        P("strip", "cells"),
        P("strip", "cells"),
        P("cells", None, None),
        P(),
    )
    return jax.shard_map(
        local,
        mesh=mesh,
        in_specs=placed,
        out_specs=(P("strip", "cells"), P(None, ("strip", "cells"))),
        check_vma=False,
    )
```

```python
import functools

import jax
import jax.numpy as jnp
from jax import lax
from jax.experimental import pallas as pl
from jax.experimental.pallas import tpu as pltpu
from jax.sharding import PartitionSpec as P

SWEEPS = 3
STEPS = 2
LANES = 128
GROUP = 8

coupling = 2.0
floor_level = 0.5
block_low, block_span = -0.002, 0.152
weight_low, weight_span = 0.5, 3.5
term_low, term_octaves = -20.0, 34.0
code_top = 65535.0
code_half = 32768.0
log_two = 0.6931471805599453

f32 = jnp.float32
bf16 = jnp.bfloat16


def iota(shape, axis):
    return lax.broadcasted_iota(jnp.int32, shape, axis)


def halves(values):
    high = values.astype(bf16)
    return high, (values - high.astype(f32)).astype(bf16)


def last_dims(left, right):
    return lax.dot_general(left, right, (((1,), (1,)), ((), ())), preferred_element_type=f32)


def pick(index, first, near, far):
    return jnp.where(index == first, near, jnp.where(index == first + 1, far, 0.0))


def rounded(values):
    return values.astype(bf16).astype(f32)


def coded(share):
    return jnp.clip(jnp.round(share * code_top), 0.0, code_top) - code_half


def stored(codes):
    return codes.astype(jnp.int32).astype(jnp.int16)


def density_codes(values):
    octave = jnp.log(jnp.maximum(values, 2.0**-40)) * (1.0 / log_two)
    return stored(coded((octave - term_low) * (1.0 / term_octaves)))


def densities(codes):
    codes = codes.astype(f32)
    octave = (codes + code_half) * (term_octaves / code_top) + term_low
    return jnp.where(codes == -code_half, 0.0, jnp.exp(octave * log_two))


def splat_kernel(
    tiles, parts, rows_ref, cols_ref, fracs_ref, pin_weights_ref, cap_ref, block_ref, row_blocks_ref, out_ref
):
    depth = cap_ref.shape[0]
    height = parts * depth
    rows, cols, sizes = rows_ref[...], cols_ref[...], pin_weights_ref[...]
    place = iota((height * (tiles + 1), LANES), 0)
    group, inner = place // height, place % height
    keys = ((inner // depth) * tiles + group - 1) * depth + inner % depth
    lane = iota((LANES + 8, LANES), 0)
    tables, lanes = [], []
    for j in range(rows.shape[0]):
        cut = slice(j * LANES, (j + 1) * LANES)
        fy, fx = fracs_ref[0:1, cut], fracs_ref[1:2, cut]
        size, col = sizes[j : j + 1], cols[j : j + 1]
        key = (col >> 7) * depth + rows[j : j + 1]
        tables.append(pick(keys, key, rounded(size * (1.0 - fy)), rounded(size * fy)).astype(bf16))
        lanes.append(pick(lane, col & 127, rounded(1.0 - fx), rounded(fx)).astype(bf16))
    total = last_dims(jnp.concatenate(tables, 1), jnp.concatenate(lanes, 1))
    first_lane = iota((height, LANES), 1) == 0
    for t in range(tiles):
        own = total[(t + 1) * height : (t + 2) * height, :LANES]
        spill = total[t * height : (t + 1) * height, LANES : LANES + 1]
        own = own + jnp.where(first_lane, spill, 0.0)
        cut = slice(t * LANES, (t + 1) * LANES)
        out_ref[:height, cut] = density_codes(own)
        share = (row_blocks_ref[t * LANES : (t + 1) * LANES, :] - block_low) * (1.0 / block_span)
        out_ref[2 * height :, cut] = stored(coded(share))
    weights = cap_ref[...].astype(f32) * (1.0 - block_ref[...])
    code = coded((weights - weight_low) * (1.0 / weight_span))
    row = iota((height, weights.shape[1]), 0)
    mine = row // depth == lax.axis_index("cells")
    out_ref[height : 2 * height, :] = stored(jnp.where(mine, jnp.concatenate([code] * parts, 0), 0.0))


def sum_kernel(*refs):
    sent_refs, out_ref = refs[:-1], refs[-1]
    height = out_ref.shape[1] // 2
    terms, codes = 0.0, 0.0
    for sent_ref in sent_refs:
        terms += densities(sent_ref[:height, :])
        codes += sent_ref[height:, :].astype(f32)
    message = jnp.concatenate([density_codes(terms), stored(codes)], 0)

    def write(n):
        out_ref[n] = message

    for n in range(out_ref.shape[0]):
        write(n)


def along_lines(values):
    width = values.shape[1]
    column = iota(values.shape, 1)
    left = jnp.where(column == 0, values, pltpu.roll(values, 1, 1))
    right = jnp.where(column == width - 1, values, pltpu.roll(values, width - 1, 1))
    return 2.0 * values - left - right


def across_lines(values):
    height = values.shape[0]
    row = iota(values.shape, 0)
    above = jnp.where(row == 0, values, pltpu.roll(values, 1, 0))
    below = jnp.where(row == height - 1, values, pltpu.roll(values, height - 1, 0))
    return 2.0 * values - above - below


def row_blockwise(residual, pairs_ref):
    high, low = halves(residual)
    result = []
    for k in range(pairs_ref.shape[0]):
        cut = slice(k * LANES, (k + 1) * LANES)
        pair = pairs_ref[k]
        both = last_dims(jnp.concatenate([high[:, cut], low[:, cut]], 1), jnp.concatenate([pair, pair], 1))
        result.append(both[:, :LANES] + both[:, LANES:])
    return jnp.concatenate(result, 1)


def col_blockwise(residual, blocks):
    high, low = halves(residual)
    count, size = len(blocks), blocks[0][0].shape[0]
    result = []
    for k, (block_high, block_low_part) in enumerate(blocks):
        cut = slice(k * size, (k + 1) * size)
        dot = functools.partial(jnp.dot, preferred_element_type=f32)
        result.append(dot(block_high, high[cut]) + (dot(block_low_part, high[cut]) + dot(block_high, low[cut])))
    return result[0] if count == 1 else jnp.concatenate(result, 0)


def each(count, body):
    if count == 1:
        body(0)
    else:
        pl.loop(0, count)(body)


def field_kernel(
    sizes, sent_ref, blocks_ref, col_blocks_ref, rows_ref, cols_ref, fracs_ref,
    final_ref, velocity_ref, pairs, weights_ref, source_ref, field_ref,
):
    depth, tiles, parts, strips = sizes
    width_part = tiles * LANES
    width = parts * width_part
    height = strips * depth
    chunk = min(GROUP, strips) * depth
    chunks = height // chunk
    strip, part = lax.axis_index("strip"), lax.axis_index("cells")

    for k in range(pairs.shape[0]):
        base = (k // tiles) * (2 * parts * depth + LANES) + 2 * parts * depth
        code = blocks_ref[base : base + LANES, k % tiles * LANES : (k % tiles + 1) * LANES].astype(f32)
        high, low = halves((code + code_half) * (block_span / code_top) + block_low)
        pairs[k, :LANES, :] = high
        pairs[k, LANES:, :] = low

    slots = parts * depth
    group = chunk // depth
    target, origin = iota((parts * chunk, group * slots), 0), iota((parts * chunk, group * slots), 1)
    slot = origin % slots
    fits = (slot // depth == target // chunk) & (origin // slots * depth + slot % depth == target % chunk)
    chosen = jnp.where(fits, 1.0, 0.0).astype(bf16)

    def placed(values):
        high, low = halves(jnp.concatenate(values, 0))
        dot = functools.partial(jnp.dot, preferred_element_type=f32)
        return dot(chosen, high) + dot(chosen, low)

    @functools.partial(each, chunks)
    def place(g):
        terms, codes = [], []
        for n in range(group):
            base = pl.multiple_of((g * group + n) * (2 * slots), 2 * slots)
            terms.append(densities(sent_ref[pl.ds(base, slots), :]))
            codes.append(sent_ref[pl.ds(base + slots, slots), :].astype(f32))
        term = placed(terms)
        weight = (placed(codes) + code_half) * (weight_span / code_top) + weight_low
        here = pl.ds(pl.multiple_of(g * chunk, chunk), chunk)
        for p in range(parts):
            cut = slice(p * width_part, (p + 1) * width_part)
            weights_ref[here, cut] = weight[p * chunk : (p + 1) * chunk]
            source_ref[here, cut] = term[p * chunk : (p + 1) * chunk] / weight[p * chunk : (p + 1) * chunk]

    lanes_at_once = width if chunks == 1 else LANES
    col_blocks = [halves(col_blocks_ref[k]) for k in range(col_blocks_ref.shape[0])]
    inner = pl.ds(8, height)

    @functools.partial(each, width // lanes_at_once)
    def start(t):
        cut = pl.ds(pl.multiple_of(t * lanes_at_once, lanes_at_once), lanes_at_once)
        current = source_ref[:, cut]
        field_ref[inner, cut] = current
        source_ref[:, cut] = weights_ref[:, cut] * current - coupling * across_lines(current)

    for step in range(STEPS):

        @functools.partial(each, chunks)
        def solve_rows(g):
            here = pl.ds(pl.multiple_of(g * chunk, chunk), chunk)
            there = pl.ds(pl.multiple_of(g * chunk + 8, 8), chunk)
            source, weights, current = source_ref[here, :], weights_ref[here, :], field_ref[there, :]
            for sweep in range(SWEEPS):
                residual = source - (weights * current + coupling * along_lines(current))
                current = current + row_blockwise(residual, pairs)
            field_ref[there, :] = current
            source_ref[here, :] = weights * current - coupling * along_lines(current)

        @functools.partial(each, width // lanes_at_once)
        def solve_cols(t):
            cut = pl.ds(pl.multiple_of(t * lanes_at_once, lanes_at_once), lanes_at_once)
            middle, weights, current = source_ref[:, cut], weights_ref[:, cut], field_ref[inner, cut]
            for sweep in range(SWEEPS):
                residual = middle - (weights * current + coupling * across_lines(current))
                current = current + col_blockwise(residual, col_blocks)
            field_ref[inner, cut] = current
            if step + 1 < STEPS:
                source_ref[:, cut] = weights * current - coupling * across_lines(current)
            else:
                field_ref[:8, cut] = jnp.broadcast_to(current[:1], (8, lanes_at_once))
                field_ref[height + 8 :, cut] = jnp.broadcast_to(current[-1:], (8, lanes_at_once))

    row0 = strip * depth
    columns = pl.ds(pl.multiple_of(part * width_part, LANES), width_part)
    base, shift = pl.multiple_of(row0 // 8 * 8, 8), 17 - row0 % 8
    final_ref[...] = pltpu.roll(field_ref[pl.ds(base, 24), columns], shift, 0)[1 : 1 + depth]

    window = pltpu.roll(field_ref[pl.ds(base, 24), :], shift, 0)
    above, centre, below = window[:8], pltpu.roll(window, 23, 0)[:8], pltpu.roll(window, 22, 0)[:8]
    column = iota(centre.shape, 1)
    left = jnp.where(column == 0, centre, pltpu.roll(centre, 1, 1))
    right = jnp.where(column == width - 1, centre, pltpu.roll(centre, width - 1, 1))
    scale = jnp.maximum(centre, floor_level)
    velocity_y = rounded(-(0.5 * (below - above)) / scale)
    velocity_x = rounded(-(0.5 * (right - left)) / scale)

    upper = iota((8, LANES), 0) < depth

    def stacked(values):
        stack = []
        for t in range(0, parts * tiles, 2):
            even = values[:, t * LANES : (t + 1) * LANES]
            odd = values[:, (t + 1) * LANES : (t + 2) * LANES]
            stack.append(jnp.where(upper, even, pltpu.roll(odd, depth, 0)))
        return jnp.concatenate(stack, 0)

    stack_y, stack_x = stacked(velocity_y), stacked(velocity_x)
    many = stack_y.shape[0]
    next_y = pltpu.roll(stack_y, many - depth, 0)
    next_x = pltpu.roll(stack_x, many - depth, 0)
    turned = [stack_y.T, next_y.T[:8], stack_x.T, next_x.T[:8]]
    table = jnp.concatenate(turned, 0).astype(bf16)
    rows, cols = rows_ref[...], cols_ref[...]
    keys, lane = iota((many, LANES), 0), iota((LANES + 8, LANES), 0)
    for j in range(rows.shape[0]):
        cut = slice(j * LANES, (j + 1) * LANES)
        fy, fx = fracs_ref[0:1, cut], fracs_ref[1:2, cut]
        col = cols[j : j + 1]
        key = (col >> 7) * depth + rows[j : j + 1]
        look = pick(keys, key, rounded(1.0 - fy), rounded(fy)).astype(bf16)
        sampled = jnp.dot(table, look, preferred_element_type=f32)
        share = pick(lane, col & 127, rounded(1.0 - fx), rounded(fx))
        velocity_ref[0:1, cut] = jnp.sum(sampled[: LANES + 8] * share, 0, keepdims=True)
        velocity_ref[1:2, cut] = jnp.sum(sampled[LANES + 8 :] * share, 0, keepdims=True)


def local(pin_rows, pin_cols, pin_fracs, pin_weights, capacity, blockage, row_blocks, col_blocks):
    depth, width_part = capacity.shape
    parts, strips = lax.axis_size("cells"), lax.axis_size("strip")
    tiles = width_part // LANES
    height, width = depth * strips, width_part * parts
    pins = pin_rows.shape[0]
    by_lane = (pins // LANES, LANES)
    rows, cols = pin_rows.reshape(by_lane), pin_cols.reshape(by_lane)
    sizes = pin_weights.reshape(by_lane)
    vmem = pl.BlockSpec(memory_space=pltpu.VMEM)
    params = pltpu.CompilerParams(vmem_limit_bytes=60 * 1024 * 1024)

    carried = 2 * parts * depth
    terms = pl.pallas_call(
        functools.partial(splat_kernel, tiles, parts),
        out_shape=jax.ShapeDtypeStruct((carried + LANES, width_part), jnp.int16),
        in_specs=[vmem] * 7,
        out_specs=vmem,
        compiler_params=params,
        name="splat",
    )(rows, cols, pin_fracs, sizes, capacity, blockage, row_blocks.reshape(-1, LANES))
    blocks = lax.all_gather(terms, "cells", axis=0, tiled=True)

    def terms_of(part):
        place = part * (carried + LANES) // carried
        return pl.BlockSpec((carried, width_part), lambda i: (place, 0))

    sums = pl.pallas_call(
        sum_kernel,
        grid=(1,),
        out_shape=jax.ShapeDtypeStruct((strips, carried, width_part), jnp.int16),
        in_specs=[terms_of(part) for part in range(parts)],
        out_specs=pl.BlockSpec((strips, carried, width_part), lambda i: (0, 0, 0)),
        compiler_params=params,
        name="sum_terms",
    )(*[blocks] * parts)
    sent = lax.all_to_all(sums, "strip", split_axis=0, concat_axis=0, tiled=True).reshape(-1, width_part)

    final, velocity = pl.pallas_call(
        functools.partial(field_kernel, (depth, tiles, parts, strips)),
        out_shape=(
            jax.ShapeDtypeStruct((depth, width_part), f32),
            jax.ShapeDtypeStruct((2, pins), f32),
        ),
        in_specs=[vmem] * 6,
        out_specs=(vmem, vmem),
        scratch_shapes=[
            pltpu.VMEM((width // LANES, 2 * LANES, LANES), bf16),
            pltpu.VMEM((height, width), f32),
            pltpu.VMEM((height, width), f32),
            pltpu.VMEM((height + 16, width), f32),
        ],
        compiler_params=params,
        name="field",
    )(sent, blocks, col_blocks, rows, cols, pin_fracs)
    return final, velocity


def solution(mesh):
    placed = (
        P(("strip", "cells")),
        P(("strip", "cells")),
        P(None, ("strip", "cells")),
        P(("strip", "cells")),
        P("strip", "cells"),
        P("strip", "cells"),
        P("cells", None, None),
        P(),
    )
    return jax.shard_map(
        local,
        mesh=mesh,
        in_specs=placed,
        out_specs=(P("strip", "cells"), P(None, ("strip", "cells"))),
        check_vma=False,
    )
```

```python
import functools

import jax
import jax.numpy as jnp
from jax import lax
from jax.experimental import pallas as pl
from jax.experimental.pallas import tpu as pltpu
from jax.sharding import PartitionSpec as P

SWEEPS = 3
STEPS = 2
LANES = 128
GROUP = 8

coupling = 2.0
floor_level = 0.5
block_low, block_span = -0.002, 0.152
weight_low, weight_span = 0.5, 3.5
term_low, term_octaves = -20.0, 34.0
code_top = 65535.0
code_half = 32768.0
log_two = 0.6931471805599453

f32 = jnp.float32
bf16 = jnp.bfloat16


def iota(shape, axis):
    return lax.broadcasted_iota(jnp.int32, shape, axis)


def halves(values):
    high = values.astype(bf16)
    return high, (values - high.astype(f32)).astype(bf16)


def last_dims(left, right):
    return lax.dot_general(left, right, (((1,), (1,)), ((), ())), preferred_element_type=f32)


def pick(index, first, near, far):
    return jnp.where(index == first, near, jnp.where(index == first + 1, far, 0.0))


def rounded(values):
    return values.astype(bf16).astype(f32)


def coded(share):
    return jnp.clip(jnp.round(share * code_top), 0.0, code_top) - code_half


def stored(codes):
    return codes.astype(jnp.int32).astype(jnp.int16)


def density_codes(values):
    octave = jnp.log(jnp.maximum(values, 2.0**-40)) * (1.0 / log_two)
    return stored(coded((octave - term_low) * (1.0 / term_octaves)))


def densities(codes):
    codes = codes.astype(f32)
    octave = (codes + code_half) * (term_octaves / code_top) + term_low
    return jnp.where(codes == -code_half, 0.0, jnp.exp(octave * log_two))


def splat_kernel(
    tiles, parts, rows_ref, cols_ref, fracs_ref, pin_weights_ref, cap_ref, block_ref, row_blocks_ref, out_ref
):
    depth = cap_ref.shape[0]
    height = parts * depth
    rows, cols, sizes = rows_ref[...], cols_ref[...], pin_weights_ref[...]
    place = iota((height * (tiles + 1), LANES), 0)
    group, inner = place // height, place % height
    keys = ((inner // depth) * tiles + group - 1) * depth + inner % depth
    lane = iota((LANES + 8, LANES), 0)
    tables, lanes = [], []
    for j in range(rows.shape[0]):
        cut = slice(j * LANES, (j + 1) * LANES)
        fy, fx = fracs_ref[0:1, cut], fracs_ref[1:2, cut]
        size, col = sizes[j : j + 1], cols[j : j + 1]
        key = (col >> 7) * depth + rows[j : j + 1]
        tables.append(pick(keys, key, rounded(size * (1.0 - fy)), rounded(size * fy)).astype(bf16))
        lanes.append(pick(lane, col & 127, rounded(1.0 - fx), rounded(fx)).astype(bf16))
    total = last_dims(jnp.concatenate(tables, 1), jnp.concatenate(lanes, 1))
    first_lane = iota((height, LANES), 1) == 0
    for t in range(tiles):
        own = total[(t + 1) * height : (t + 2) * height, :LANES]
        spill = total[t * height : (t + 1) * height, LANES : LANES + 1]
        own = own + jnp.where(first_lane, spill, 0.0)
        cut = slice(t * LANES, (t + 1) * LANES)
        out_ref[:height, cut] = density_codes(own)
        share = (row_blocks_ref[t * LANES : (t + 1) * LANES, :] - block_low) * (1.0 / block_span)
        out_ref[2 * height :, cut] = stored(coded(share))
    weights = cap_ref[...].astype(f32) * (1.0 - block_ref[...])
    code = coded((weights - weight_low) * (1.0 / weight_span))
    row = iota((height, weights.shape[1]), 0)
    mine = row // depth == lax.axis_index("cells")
    out_ref[height : 2 * height, :] = stored(jnp.where(mine, jnp.concatenate([code] * parts, 0), 0.0))


def sum_kernel(*refs):
    sent_refs, out_ref = refs[:-1], refs[-1]
    height = out_ref.shape[0] // 2
    terms, codes = 0.0, 0.0
    for sent_ref in sent_refs:
        terms += densities(sent_ref[:height, :])
        codes += sent_ref[height:, :].astype(f32)
    out_ref[:height, :] = density_codes(terms)
    out_ref[height:, :] = stored(codes)


def along_lines(values):
    width = values.shape[1]
    column = iota(values.shape, 1)
    left = jnp.where(column == 0, values, pltpu.roll(values, 1, 1))
    right = jnp.where(column == width - 1, values, pltpu.roll(values, width - 1, 1))
    return 2.0 * values - left - right


def across_lines(values):
    height = values.shape[0]
    row = iota(values.shape, 0)
    above = jnp.where(row == 0, values, pltpu.roll(values, 1, 0))
    below = jnp.where(row == height - 1, values, pltpu.roll(values, height - 1, 0))
    return 2.0 * values - above - below


def row_blockwise(residual, pairs_ref):
    high, low = halves(residual)
    result = []
    for k in range(pairs_ref.shape[0]):
        cut = slice(k * LANES, (k + 1) * LANES)
        pair = pairs_ref[k]
        both = last_dims(jnp.concatenate([high[:, cut], low[:, cut]], 1), jnp.concatenate([pair, pair], 1))
        result.append(both[:, :LANES] + both[:, LANES:])
    return jnp.concatenate(result, 1)


def col_blockwise(residual, blocks):
    high, low = halves(residual)
    count, size = len(blocks), blocks[0][0].shape[0]
    result = []
    for k, (block_high, block_low_part) in enumerate(blocks):
        cut = slice(k * size, (k + 1) * size)
        dot = functools.partial(jnp.dot, preferred_element_type=f32)
        result.append(dot(block_high, high[cut]) + (dot(block_low_part, high[cut]) + dot(block_high, low[cut])))
    return result[0] if count == 1 else jnp.concatenate(result, 0)


def each(count, body):
    if count == 1:
        body(0)
    else:
        pl.loop(0, count)(body)


def field_kernel(
    sizes, blocks_ref, col_blocks_ref, rows_ref, cols_ref, fracs_ref, *refs,
):
    depth, tiles, parts, strips = sizes
    sent_refs, (final_ref, velocity_ref, pairs, weights_ref, source_ref, field_ref, ordered) = refs[:-7], refs[-7:]
    width_part = tiles * LANES
    width = parts * width_part
    height = strips * depth
    chunk = min(GROUP, strips) * depth
    chunks = height // chunk
    strip, part = lax.axis_index("strip"), lax.axis_index("cells")

    for k in range(pairs.shape[0]):
        base = (k // tiles) * (2 * parts * depth + LANES) + 2 * parts * depth
        code = blocks_ref[base : base + LANES, k % tiles * LANES : (k % tiles + 1) * LANES].astype(f32)
        high, low = halves((code + code_half) * (block_span / code_top) + block_low)
        pairs[k, :LANES, :] = high
        pairs[k, LANES:, :] = low

    slots = parts * depth
    if len(sent_refs) == 1:
        sent = sent_refs[0]
    else:
        sent = ordered
        for k, sent_ref in enumerate(sent_refs):
            ordered[strip ^ k] = sent_ref[...]
    group = chunk // depth
    target, origin = iota((parts * chunk, group * slots), 0), iota((parts * chunk, group * slots), 1)
    slot = origin % slots
    fits = (slot // depth == target // chunk) & (origin // slots * depth + slot % depth == target % chunk)
    chosen = jnp.where(fits, 1.0, 0.0).astype(bf16)

    def placed(values):
        high, low = halves(jnp.concatenate(values, 0))
        dot = functools.partial(jnp.dot, preferred_element_type=f32)
        return dot(chosen, high) + dot(chosen, low)

    @functools.partial(each, chunks)
    def place(g):
        terms, codes = [], []
        for n in range(group):
            got = sent[g * group + n]
            terms.append(densities(got[:slots]))
            codes.append(got[slots:].astype(f32))
        term = placed(terms)
        weight = (placed(codes) + code_half) * (weight_span / code_top) + weight_low
        here = pl.ds(pl.multiple_of(g * chunk, chunk), chunk)
        for p in range(parts):
            cut = slice(p * width_part, (p + 1) * width_part)
            weights_ref[here, cut] = weight[p * chunk : (p + 1) * chunk]
            source_ref[here, cut] = term[p * chunk : (p + 1) * chunk] / weight[p * chunk : (p + 1) * chunk]

    lanes_at_once = width if chunks == 1 else LANES
    col_blocks = [halves(col_blocks_ref[k]) for k in range(col_blocks_ref.shape[0])]
    inner = pl.ds(8, height)

    @functools.partial(each, width // lanes_at_once)
    def start(t):
        cut = pl.ds(pl.multiple_of(t * lanes_at_once, lanes_at_once), lanes_at_once)
        current = source_ref[:, cut]
        field_ref[inner, cut] = current
        source_ref[:, cut] = weights_ref[:, cut] * current - coupling * across_lines(current)

    for step in range(STEPS):

        @functools.partial(each, chunks)
        def solve_rows(g):
            here = pl.ds(pl.multiple_of(g * chunk, chunk), chunk)
            there = pl.ds(pl.multiple_of(g * chunk + 8, 8), chunk)
            source, weights, current = source_ref[here, :], weights_ref[here, :], field_ref[there, :]
            for sweep in range(SWEEPS):
                residual = source - (weights * current + coupling * along_lines(current))
                current = current + row_blockwise(residual, pairs)
            field_ref[there, :] = current
            source_ref[here, :] = weights * current - coupling * along_lines(current)

        @functools.partial(each, width // lanes_at_once)
        def solve_cols(t):
            cut = pl.ds(pl.multiple_of(t * lanes_at_once, lanes_at_once), lanes_at_once)
            middle, weights, current = source_ref[:, cut], weights_ref[:, cut], field_ref[inner, cut]
            for sweep in range(SWEEPS):
                residual = middle - (weights * current + coupling * across_lines(current))
                current = current + col_blockwise(residual, col_blocks)
            field_ref[inner, cut] = current
            if step + 1 < STEPS:
                source_ref[:, cut] = weights * current - coupling * across_lines(current)
            else:
                field_ref[:8, cut] = jnp.broadcast_to(current[:1], (8, lanes_at_once))
                field_ref[height + 8 :, cut] = jnp.broadcast_to(current[-1:], (8, lanes_at_once))

    row0 = strip * depth
    columns = pl.ds(pl.multiple_of(part * width_part, LANES), width_part)
    base, shift = pl.multiple_of(row0 // 8 * 8, 8), 17 - row0 % 8
    final_ref[...] = pltpu.roll(field_ref[pl.ds(base, 24), columns], shift, 0)[1 : 1 + depth]

    window = pltpu.roll(field_ref[pl.ds(base, 24), :], shift, 0)
    above, centre, below = window[:8], pltpu.roll(window, 23, 0)[:8], pltpu.roll(window, 22, 0)[:8]
    column = iota(centre.shape, 1)
    left = jnp.where(column == 0, centre, pltpu.roll(centre, 1, 1))
    right = jnp.where(column == width - 1, centre, pltpu.roll(centre, width - 1, 1))
    scale = jnp.maximum(centre, floor_level)
    velocity_y = rounded(-(0.5 * (below - above)) / scale)
    velocity_x = rounded(-(0.5 * (right - left)) / scale)

    upper = iota((8, LANES), 0) < depth

    def stacked(values):
        stack = []
        for t in range(0, parts * tiles, 2):
            even = values[:, t * LANES : (t + 1) * LANES]
            odd = values[:, (t + 1) * LANES : (t + 2) * LANES]
            stack.append(jnp.where(upper, even, pltpu.roll(odd, depth, 0)))
        return jnp.concatenate(stack, 0)

    stack_y, stack_x = stacked(velocity_y), stacked(velocity_x)
    many = stack_y.shape[0]
    next_y = pltpu.roll(stack_y, many - depth, 0)
    next_x = pltpu.roll(stack_x, many - depth, 0)
    turned = [stack_y.T, next_y.T[:8], stack_x.T, next_x.T[:8]]
    table = jnp.concatenate(turned, 0).astype(bf16)
    rows, cols = rows_ref[...], cols_ref[...]
    keys, lane = iota((many, LANES), 0), iota((LANES + 8, LANES), 0)
    for j in range(rows.shape[0]):
        cut = slice(j * LANES, (j + 1) * LANES)
        fy, fx = fracs_ref[0:1, cut], fracs_ref[1:2, cut]
        col = cols[j : j + 1]
        key = (col >> 7) * depth + rows[j : j + 1]
        look = pick(keys, key, rounded(1.0 - fy), rounded(fy)).astype(bf16)
        sampled = jnp.dot(table, look, preferred_element_type=f32)
        share = pick(lane, col & 127, rounded(1.0 - fx), rounded(fx))
        velocity_ref[0:1, cut] = jnp.sum(sampled[: LANES + 8] * share, 0, keepdims=True)
        velocity_ref[1:2, cut] = jnp.sum(sampled[LANES + 8 :] * share, 0, keepdims=True)


def local(pin_rows, pin_cols, pin_fracs, pin_weights, capacity, blockage, row_blocks, col_blocks):
    depth, width_part = capacity.shape
    parts, strips = lax.axis_size("cells"), lax.axis_size("strip")
    tiles = width_part // LANES
    height, width = depth * strips, width_part * parts
    pins = pin_rows.shape[0]
    by_lane = (pins // LANES, LANES)
    rows, cols = pin_rows.reshape(by_lane), pin_cols.reshape(by_lane)
    sizes = pin_weights.reshape(by_lane)
    vmem = pl.BlockSpec(memory_space=pltpu.VMEM)
    small = pltpu.CompilerParams(vmem_limit_bytes=16 * 1024 * 1024)
    grid_bytes = 4 * height * width
    large = pltpu.CompilerParams(vmem_limit_bytes=(20 << 20) + 6 * grid_bytes)

    carried = 2 * parts * depth
    terms = pl.pallas_call(
        functools.partial(splat_kernel, tiles, parts),
        out_shape=jax.ShapeDtypeStruct((carried + LANES, width_part), jnp.int16),
        in_specs=[vmem] * 7,
        out_specs=vmem,
        compiler_params=small,
        name="splat",
    )(rows, cols, pin_fracs, sizes, capacity, blockage, row_blocks.reshape(-1, LANES))
    blocks = lax.all_gather(terms, "cells", axis=0, tiled=True)

    def terms_of(part):
        place = part * (carried + LANES) // carried
        return pl.BlockSpec((carried, width_part), lambda i: (place, 0))

    sums = pl.pallas_call(
        sum_kernel,
        grid=(1,),
        out_shape=jax.ShapeDtypeStruct((carried, width_part), jnp.int16),
        in_specs=[terms_of(part) for part in range(parts)],
        out_specs=pl.BlockSpec((carried, width_part), lambda i: (0, 0)),
        compiler_params=small,
        name="sum_terms",
    )(*[blocks] * parts)
    if strips == 8:
        sent = [sums] + [None] * 7
        for k in (6, 7, 4, 5, 2, 3, 1):
            sent[k] = lax.ppermute(sums, "strip", [(n, n ^ k) for n in range(strips)])
    else:
        sent = [lax.all_gather(sums, "strip", axis=0)]

    final, velocity = pl.pallas_call(
        functools.partial(field_kernel, (depth, tiles, parts, strips)),
        out_shape=(
            jax.ShapeDtypeStruct((depth, width_part), f32),
            jax.ShapeDtypeStruct((2, pins), f32),
        ),
        in_specs=[vmem] * (5 + len(sent)),
        out_specs=(vmem, vmem),
        scratch_shapes=[
            pltpu.VMEM((width // LANES, 2 * LANES, LANES), bf16),
            pltpu.VMEM((height, width), f32),
            pltpu.VMEM((height, width), f32),
            pltpu.VMEM((height + 16, width), f32),
            pltpu.VMEM((len(sent), carried, width_part), jnp.int16),
        ],
        compiler_params=large,
        name="field",
    )(blocks, col_blocks, rows, cols, pin_fracs, *sent)
    return final, velocity


def solution(mesh):
    placed = (
        P(("strip", "cells")),
        P(("strip", "cells")),
        P(None, ("strip", "cells")),
        P(("strip", "cells")),
        P("strip", "cells"),
        P("strip", "cells"),
        P("cells", None, None),
        P(),
    )
    return jax.shard_map(
        local,
        mesh=mesh,
        in_specs=placed,
        out_specs=(P("strip", "cells"), P(None, ("strip", "cells"))),
        check_vma=False,
    )
```

```python
import functools

import jax
import jax.numpy as jnp
from jax import lax
from jax.experimental import pallas as pl
from jax.experimental.pallas import tpu as pltpu
from jax.sharding import PartitionSpec as P

SWEEPS = 3
STEPS = 2
LANES = 128
GROUP = 8

coupling = 2.0
floor_level = 0.5
block_low, block_span = -0.002, 0.152
weight_low, weight_span = 0.5, 3.5
term_low, term_octaves = -20.0, 34.0
code_top = 65535.0
code_half = 32768.0
log_two = 0.6931471805599453

f32 = jnp.float32
bf16 = jnp.bfloat16


def iota(shape, axis):
    return lax.broadcasted_iota(jnp.int32, shape, axis)


def halves(values):
    high = values.astype(bf16)
    return high, (values - high.astype(f32)).astype(bf16)


def last_dims(left, right):
    return lax.dot_general(left, right, (((1,), (1,)), ((), ())), preferred_element_type=f32)


def pick(index, first, near, far):
    return jnp.where(index == first, near, jnp.where(index == first + 1, far, 0.0))


def rounded(values):
    return values.astype(bf16).astype(f32)


def coded(share):
    return jnp.clip(jnp.round(share * code_top), 0.0, code_top) - code_half


def stored(codes):
    return codes.astype(jnp.int32).astype(jnp.int16)


def density_codes(values):
    octave = jnp.log(jnp.maximum(values, 2.0**-40)) * (1.0 / log_two)
    return stored(coded((octave - term_low) * (1.0 / term_octaves)))


def densities(codes):
    codes = codes.astype(f32)
    octave = (codes + code_half) * (term_octaves / code_top) + term_low
    return jnp.where(codes == -code_half, 0.0, jnp.exp(octave * log_two))


def splat_kernel(
    tiles, parts, rows_ref, cols_ref, fracs_ref, pin_weights_ref, cap_ref, block_ref, row_blocks_ref, out_ref
):
    depth = cap_ref.shape[0]
    height = parts * depth
    rows, cols, sizes = rows_ref[...], cols_ref[...], pin_weights_ref[...]
    place = iota((height * (tiles + 1), LANES), 0)
    group, inner = place // height, place % height
    keys = ((inner // depth) * tiles + group - 1) * depth + inner % depth
    lane = iota((LANES + 8, LANES), 0)
    tables, lanes = [], []
    for j in range(rows.shape[0]):
        cut = slice(j * LANES, (j + 1) * LANES)
        fy, fx = fracs_ref[0:1, cut], fracs_ref[1:2, cut]
        size, col = sizes[j : j + 1], cols[j : j + 1]
        key = (col >> 7) * depth + rows[j : j + 1]
        tables.append(pick(keys, key, rounded(size * (1.0 - fy)), rounded(size * fy)).astype(bf16))
        lanes.append(pick(lane, col & 127, rounded(1.0 - fx), rounded(fx)).astype(bf16))
    total = last_dims(jnp.concatenate(tables, 1), jnp.concatenate(lanes, 1))
    first_lane = iota((height, LANES), 1) == 0
    for t in range(tiles):
        own = total[(t + 1) * height : (t + 2) * height, :LANES]
        spill = total[t * height : (t + 1) * height, LANES : LANES + 1]
        own = own + jnp.where(first_lane, spill, 0.0)
        cut = slice(t * LANES, (t + 1) * LANES)
        out_ref[:height, cut] = density_codes(own)
        share = (row_blocks_ref[t * LANES : (t + 1) * LANES, :] - block_low) * (1.0 / block_span)
        out_ref[2 * height :, cut] = stored(coded(share))
    weights = cap_ref[...].astype(f32) * (1.0 - block_ref[...])
    code = coded((weights - weight_low) * (1.0 / weight_span))
    row = iota((height, weights.shape[1]), 0)
    mine = row // depth == lax.axis_index("cells")
    out_ref[height : 2 * height, :] = stored(jnp.where(mine, jnp.concatenate([code] * parts, 0), 0.0))


def sum_kernel(*refs):
    sent_refs, out_ref = refs[:-1], refs[-1]
    height = out_ref.shape[0] // 2
    terms, codes = 0.0, 0.0
    for sent_ref in sent_refs:
        terms += densities(sent_ref[:height, :])
        codes += sent_ref[height:, :].astype(f32)
    out_ref[:height, :] = density_codes(terms)
    out_ref[height:, :] = stored(codes)


def beside(values):
    width = values.shape[1]
    lane = iota((values.shape[0], LANES), 1)
    left, right = pltpu.roll(values, 1, 1), pltpu.roll(values, width - 1, 1)
    first = jnp.where(lane == 0, values[:, :LANES], left[:, :LANES])
    last = jnp.where(lane == LANES - 1, values[:, width - LANES :], right[:, width - LANES :])
    return (
        jnp.concatenate([first, left[:, LANES:]], 1),
        jnp.concatenate([right[:, : width - LANES], last], 1),
    )


def along_lines(values):
    left, right = beside(values)
    return 2.0 * values - left - right


def across_lines(values):
    height = values.shape[0]
    row = iota((8, values.shape[1]), 0)
    above, below = pltpu.roll(values, 1, 0), pltpu.roll(values, height - 1, 0)
    first = jnp.where(row == 0, values[:8], above[:8])
    last = jnp.where(row == 7, values[height - 8 :], below[height - 8 :])
    above = jnp.concatenate([first, above[8:]], 0)
    below = jnp.concatenate([below[: height - 8], last], 0)
    return 2.0 * values - above - below


def row_blockwise(residual, pairs_ref):
    count = residual.shape[0]
    both = jnp.concatenate(halves(residual), 0)
    result = []
    for k in range(pairs_ref.shape[0]):
        product = last_dims(both[:, k * LANES : (k + 1) * LANES], pairs_ref[k])
        high, low = product[:count], product[count:]
        result.append(high[:, :LANES] + (high[:, LANES:] + low[:, :LANES]))
    return jnp.concatenate(result, 1)


def col_blockwise(residual, blocks):
    high, low = halves(residual)
    size = blocks[0].shape[0] // 2
    dot = functools.partial(jnp.dot, preferred_element_type=f32)
    result = []
    for k, pair in enumerate(blocks):
        cut = slice(k * size, (k + 1) * size)
        both = dot(pair, high[cut])
        result.append(both[:size] + (both[size:] + dot(pair[:size], low[cut])))
    return result[0] if len(blocks) == 1 else jnp.concatenate(result, 0)


def each(count, body):
    if count == 1:
        body(0)
    else:
        pl.loop(0, count)(body)


def field_kernel(
    sizes, blocks_ref, col_blocks_ref, rows_ref, cols_ref, fracs_ref, *refs,
):
    depth, tiles, parts, strips = sizes
    sent_refs, (final_ref, velocity_ref, pairs, weights_ref, source_ref, field_ref, ordered) = refs[:-7], refs[-7:]
    width_part = tiles * LANES
    width = parts * width_part
    height = strips * depth
    chunk = min(GROUP, strips) * depth
    chunks = height // chunk
    strip, part = lax.axis_index("strip"), lax.axis_index("cells")

    for k in range(pairs.shape[0]):
        base = (k // tiles) * (2 * parts * depth + LANES) + 2 * parts * depth
        code = blocks_ref[base : base + LANES, k % tiles * LANES : (k % tiles + 1) * LANES].astype(f32)
        high, low = halves((code + code_half) * (block_span / code_top) + block_low)
        pairs[k, :LANES, :] = high
        pairs[k, LANES:, :] = low

    slots = parts * depth
    if len(sent_refs) == 1:
        sent = sent_refs[0]
    else:
        sent = ordered
        for k, sent_ref in enumerate(sent_refs):
            ordered[strip ^ k] = sent_ref[...]
    group = chunk // depth
    target, origin = iota((parts * chunk, group * slots), 0), iota((parts * chunk, group * slots), 1)
    slot = origin % slots
    fits = (slot // depth == target // chunk) & (origin // slots * depth + slot % depth == target % chunk)
    chosen = jnp.where(fits, 1.0, 0.0).astype(bf16)

    def placed(values):
        high, low = halves(jnp.concatenate(values, 0))
        dot = functools.partial(jnp.dot, preferred_element_type=f32)
        return dot(chosen, high) + dot(chosen, low)

    @functools.partial(each, chunks)
    def place(g):
        terms, codes = [], []
        for n in range(group):
            got = sent[g * group + n]
            terms.append(densities(got[:slots]))
            codes.append(got[slots:].astype(f32))
        term = placed(terms)
        weight = (placed(codes) + code_half) * (weight_span / code_top) + weight_low
        here = pl.ds(pl.multiple_of(g * chunk, chunk), chunk)
        for p in range(parts):
            cut = slice(p * width_part, (p + 1) * width_part)
            weights_ref[here, cut] = weight[p * chunk : (p + 1) * chunk]
            source_ref[here, cut] = term[p * chunk : (p + 1) * chunk] / weight[p * chunk : (p + 1) * chunk]

    lanes_at_once = width if chunks == 1 else LANES
    col_blocks = [jnp.concatenate(halves(col_blocks_ref[k]), 0) for k in range(col_blocks_ref.shape[0])]
    inner = pl.ds(8, height)

    @functools.partial(each, width // lanes_at_once)
    def start(t):
        cut = pl.ds(pl.multiple_of(t * lanes_at_once, lanes_at_once), lanes_at_once)
        current = source_ref[:, cut]
        field_ref[inner, cut] = current
        source_ref[:, cut] = weights_ref[:, cut] * current - coupling * across_lines(current)

    for step in range(STEPS):

        @functools.partial(each, chunks)
        def solve_rows(g):
            here = pl.ds(pl.multiple_of(g * chunk, chunk), chunk)
            there = pl.ds(pl.multiple_of(g * chunk + 8, 8), chunk)
            source, weights, current = source_ref[here, :], weights_ref[here, :], field_ref[there, :]
            for sweep in range(SWEEPS):
                residual = source - (weights * current + coupling * along_lines(current))
                current = current + row_blockwise(residual, pairs)
            field_ref[there, :] = current
            source_ref[here, :] = weights * current - coupling * along_lines(current)

        @functools.partial(each, width // lanes_at_once)
        def solve_cols(t):
            cut = pl.ds(pl.multiple_of(t * lanes_at_once, lanes_at_once), lanes_at_once)
            middle, weights, current = source_ref[:, cut], weights_ref[:, cut], field_ref[inner, cut]
            for sweep in range(SWEEPS):
                residual = middle - (weights * current + coupling * across_lines(current))
                current = current + col_blockwise(residual, col_blocks)
            field_ref[inner, cut] = current
            if step + 1 < STEPS:
                source_ref[:, cut] = weights * current - coupling * across_lines(current)
            else:
                field_ref[:8, cut] = jnp.broadcast_to(current[:1], (8, lanes_at_once))
                field_ref[height + 8 :, cut] = jnp.broadcast_to(current[-1:], (8, lanes_at_once))

    row0 = strip * depth
    columns = pl.ds(pl.multiple_of(part * width_part, LANES), width_part)
    base, shift = pl.multiple_of(row0 // 8 * 8, 8), 17 - row0 % 8
    final_ref[...] = pltpu.roll(field_ref[pl.ds(base, 24), columns], shift, 0)[1 : 1 + depth]

    window = pltpu.roll(field_ref[pl.ds(base, 24), :], shift, 0)
    above, centre, below = window[:8], pltpu.roll(window, 23, 0)[:8], pltpu.roll(window, 22, 0)[:8]
    left, right = beside(centre)
    scale = jnp.maximum(centre, floor_level)
    velocity_y = rounded(-(0.5 * (below - above)) / scale)
    velocity_x = rounded(-(0.5 * (right - left)) / scale)

    upper = iota((8, LANES), 0) < depth

    def stacked(values):
        stack = []
        for t in range(0, parts * tiles, 2):
            even = values[:, t * LANES : (t + 1) * LANES]
            odd = values[:, (t + 1) * LANES : (t + 2) * LANES]
            stack.append(jnp.where(upper, even, pltpu.roll(odd, depth, 0)))
        return jnp.concatenate(stack, 0)

    half = LANES // 2

    def table_of(values):
        stack = stacked(values)
        many = stack.shape[0]
        blank = jnp.zeros((LANES - many, LANES), f32)
        turned = jnp.concatenate([stack, blank], 0).T
        after = jnp.concatenate([pltpu.roll(stack, many - depth, 0), blank], 0).T[:8]
        return jnp.concatenate([turned[: half + 8], jnp.concatenate([turned[half:], after], 0)], 1)

    table = jnp.concatenate([table_of(velocity_y), table_of(velocity_x)], 0).astype(bf16)
    many = parts * tiles * depth
    rows, cols = rows_ref[...], cols_ref[...]
    joined = 2 if rows.shape[0] % 2 == 0 else 1
    blank = jnp.zeros((LANES - many, joined * LANES), bf16)
    keys, lane = iota((many, joined * LANES), 0), iota((half + 8, joined * LANES), 0)
    for j in range(0, rows.shape[0], joined):
        cut = slice(j * LANES, (j + joined) * LANES)
        fy, fx = fracs_ref[0:1, cut], fracs_ref[1:2, cut]
        col = jnp.concatenate([cols[n : n + 1] for n in range(j, j + joined)], 1)
        row = jnp.concatenate([rows[n : n + 1] for n in range(j, j + joined)], 1)
        key = (col >> 7) * depth + row
        second = (col & half) != 0
        near, far = rounded(1.0 - fy), rounded(fy)
        looks = [
            pick(keys, jnp.where(second, -8, key), near, far).astype(bf16),
            blank,
            pick(keys, jnp.where(second, key, -8), near, far).astype(bf16),
            blank,
        ]
        sampled = jnp.dot(table, jnp.concatenate(looks, 0), preferred_element_type=f32)
        share = pick(lane, col & (half - 1), rounded(1.0 - fx), rounded(fx))
        velocity_ref[0:1, cut] = jnp.sum(sampled[: half + 8] * share, 0, keepdims=True)
        velocity_ref[1:2, cut] = jnp.sum(sampled[half + 8 :] * share, 0, keepdims=True)


def local(pin_rows, pin_cols, pin_fracs, pin_weights, capacity, blockage, row_blocks, col_blocks):
    depth, width_part = capacity.shape
    parts, strips = lax.axis_size("cells"), lax.axis_size("strip")
    tiles = width_part // LANES
    height, width = depth * strips, width_part * parts
    pins = pin_rows.shape[0]
    by_lane = (pins // LANES, LANES)
    rows, cols = pin_rows.reshape(by_lane), pin_cols.reshape(by_lane)
    sizes = pin_weights.reshape(by_lane)
    vmem = pl.BlockSpec(memory_space=pltpu.VMEM)
    whole = pltpu.CompilerParams(vmem_limit_bytes=60 << 20)
    small = pltpu.CompilerParams(vmem_limit_bytes=16 * 1024 * 1024)
    grid_bytes = 4 * height * width
    large = pltpu.CompilerParams(vmem_limit_bytes=(20 << 20) + 6 * grid_bytes)

    carried = 2 * parts * depth
    terms = pl.pallas_call(
        functools.partial(splat_kernel, tiles, parts),
        out_shape=jax.ShapeDtypeStruct((carried + LANES, width_part), jnp.int16),
        in_specs=[vmem] * 7,
        out_specs=vmem,
        compiler_params=whole,
        name="splat",
    )(rows, cols, pin_fracs, sizes, capacity, blockage, row_blocks.reshape(-1, LANES))
    blocks = lax.all_gather(terms, "cells", axis=0, tiled=True)

    def terms_of(part):
        place = part * (carried + LANES) // carried
        return pl.BlockSpec((carried, width_part), lambda i: (place, 0))

    sums = pl.pallas_call(
        sum_kernel,
        grid=(1,),
        out_shape=jax.ShapeDtypeStruct((carried, width_part), jnp.int16),
        in_specs=[terms_of(part) for part in range(parts)],
        out_specs=pl.BlockSpec((carried, width_part), lambda i: (0, 0)),
        compiler_params=small,
        name="sum_terms",
    )(*[blocks] * parts)
    if strips == 8:
        sent = [sums] + [None] * 7
        for k in (6, 7, 4, 5, 2, 3, 1):
            sent[k] = lax.ppermute(sums, "strip", [(n, n ^ k) for n in range(strips)])
    else:
        sent = [lax.all_gather(sums, "strip", axis=0)]

    final, velocity = pl.pallas_call(
        functools.partial(field_kernel, (depth, tiles, parts, strips)),
        out_shape=(
            jax.ShapeDtypeStruct((depth, width_part), f32),
            jax.ShapeDtypeStruct((2, pins), f32),
        ),
        in_specs=[vmem] * (5 + len(sent)),
        out_specs=(vmem, vmem),
        scratch_shapes=[
            pltpu.VMEM((width // LANES, 2 * LANES, LANES), bf16),
            pltpu.VMEM((height, width), f32),
            pltpu.VMEM((height, width), f32),
            pltpu.VMEM((height + 16, width), f32),
            pltpu.VMEM((len(sent), carried, width_part), jnp.int16),
        ],
        compiler_params=large,
        name="field",
    )(blocks, col_blocks, rows, cols, pin_fracs, *sent)
    return final, velocity


def solution(mesh):
    placed = (
        P(("strip", "cells")),
        P(("strip", "cells")),
        P(None, ("strip", "cells")),
        P(("strip", "cells")),
        P("strip", "cells"),
        P("strip", "cells"),
        P("cells", None, None),
        P(),
    )
    return jax.shard_map(
        local,
        mesh=mesh,
        in_specs=placed,
        out_specs=(P("strip", "cells"), P(None, ("strip", "cells"))),
        check_vma=False,
    )
```

```python
import functools

import jax
import jax.numpy as jnp
from jax import lax
from jax.experimental import pallas as pl
from jax.experimental.pallas import tpu as pltpu
from jax.sharding import PartitionSpec as P

SWEEPS = 3
STEPS = 2
LANES = 128
GROUP = 8

coupling = 2.0
floor_level = 0.5
block_low, block_span = -0.002, 0.152
weight_low, weight_span = 0.5, 3.5
term_low, term_octaves = -20.0, 34.0
code_top = 65535.0
code_half = 32768.0
log_two = 0.6931471805599453

f32 = jnp.float32
bf16 = jnp.bfloat16


def iota(shape, axis):
    return lax.broadcasted_iota(jnp.int32, shape, axis)


def halves(values):
    high = values.astype(bf16)
    return high, (values - high.astype(f32)).astype(bf16)


def last_dims(left, right):
    return lax.dot_general(left, right, (((1,), (1,)), ((), ())), preferred_element_type=f32)


def pick(index, first, near, far):
    return jnp.where(index == first, near, jnp.where(index == first + 1, far, 0.0))


def rounded(values):
    return values.astype(bf16).astype(f32)


def coded(share):
    return jnp.clip(jnp.round(share * code_top), 0.0, code_top) - code_half


def stored(codes):
    return codes.astype(jnp.int32).astype(jnp.int16)


def density_codes(values):
    octave = jnp.log(jnp.maximum(values, 2.0**-40)) * (1.0 / log_two)
    return stored(coded((octave - term_low) * (1.0 / term_octaves)))


def densities(codes):
    codes = codes.astype(f32)
    octave = (codes + code_half) * (term_octaves / code_top) + term_low
    return jnp.where(codes == -code_half, 0.0, jnp.exp(octave * log_two))


def splat_kernel(
    tiles, parts, rows_ref, cols_ref, fracs_ref, pin_weights_ref, cap_ref, block_ref, row_blocks_ref, out_ref, codes_ref
):
    depth = cap_ref.shape[0]
    height = parts * depth
    rows, cols, sizes = rows_ref[...], cols_ref[...], pin_weights_ref[...]
    place = iota((height * (tiles + 1), LANES), 0)
    group, inner = place // height, place % height
    keys = ((inner // depth) * tiles + group - 1) * depth + inner % depth
    lane = iota((LANES + 8, LANES), 0)
    tables, lanes = [], []
    for j in range(rows.shape[0]):
        cut = slice(j * LANES, (j + 1) * LANES)
        fy, fx = fracs_ref[0:1, cut], fracs_ref[1:2, cut]
        size, col = sizes[j : j + 1], cols[j : j + 1]
        key = (col >> 7) * depth + rows[j : j + 1]
        tables.append(pick(keys, key, rounded(size * (1.0 - fy)), rounded(size * fy)).astype(bf16))
        lanes.append(pick(lane, col & 127, rounded(1.0 - fx), rounded(fx)).astype(bf16))
    total = last_dims(jnp.concatenate(tables, 1), jnp.concatenate(lanes, 1))
    first_lane = iota((height, LANES), 1) == 0
    for t in range(tiles):
        own = total[(t + 1) * height : (t + 2) * height, :LANES]
        spill = total[t * height : (t + 1) * height, LANES : LANES + 1]
        own = own + jnp.where(first_lane, spill, 0.0)
        cut = slice(t * LANES, (t + 1) * LANES)
        out_ref[:height, cut] = density_codes(own)
        share = (row_blocks_ref[t * LANES : (t + 1) * LANES, :] - block_low) * (1.0 / block_span)
        codes_ref[:, cut] = stored(coded(share))
    weights = cap_ref[...].astype(f32) * (1.0 - block_ref[...])
    code = coded((weights - weight_low) * (1.0 / weight_span))
    row = iota((height, weights.shape[1]), 0)
    mine = row // depth == lax.axis_index("cells")
    out_ref[height:, :] = stored(jnp.where(mine, jnp.concatenate([code] * parts, 0), 0.0))


def sum_kernel(*refs):
    sent_refs, out_ref = refs[:-1], refs[-1]
    height = out_ref.shape[0] // 2
    terms, codes = 0.0, 0.0
    for sent_ref in sent_refs:
        terms += densities(sent_ref[:height, :])
        codes += sent_ref[height:, :].astype(f32)
    out_ref[:height, :] = density_codes(terms)
    out_ref[height:, :] = stored(codes)


def beside(values):
    width = values.shape[1]
    lane = iota((values.shape[0], LANES), 1)
    left, right = pltpu.roll(values, 1, 1), pltpu.roll(values, width - 1, 1)
    first = jnp.where(lane == 0, values[:, :LANES], left[:, :LANES])
    last = jnp.where(lane == LANES - 1, values[:, width - LANES :], right[:, width - LANES :])
    return (
        jnp.concatenate([first, left[:, LANES:]], 1),
        jnp.concatenate([right[:, : width - LANES], last], 1),
    )


def along_lines(values):
    left, right = beside(values)
    return 2.0 * values - left - right


def across_lines(values):
    height = values.shape[0]
    row = iota((8, values.shape[1]), 0)
    above, below = pltpu.roll(values, 1, 0), pltpu.roll(values, height - 1, 0)
    first = jnp.where(row == 0, values[:8], above[:8])
    last = jnp.where(row == 7, values[height - 8 :], below[height - 8 :])
    above = jnp.concatenate([first, above[8:]], 0)
    below = jnp.concatenate([below[: height - 8], last], 0)
    return 2.0 * values - above - below


def row_blockwise(residual, pairs_ref):
    count = residual.shape[0]
    both = jnp.concatenate(halves(residual), 0)
    result = []
    for k in range(pairs_ref.shape[0]):
        product = last_dims(both[:, k * LANES : (k + 1) * LANES], pairs_ref[k])
        high, low = product[:count], product[count:]
        result.append(high[:, :LANES] + (high[:, LANES:] + low[:, :LANES]))
    return jnp.concatenate(result, 1)


def col_blockwise(residual, blocks):
    high, low = halves(residual)
    size = blocks[0].shape[0] // 2
    dot = functools.partial(jnp.dot, preferred_element_type=f32)
    result = []
    for k, pair in enumerate(blocks):
        cut = slice(k * size, (k + 1) * size)
        both = dot(pair, high[cut])
        result.append(both[:size] + (both[size:] + dot(pair[:size], low[cut])))
    return result[0] if len(blocks) == 1 else jnp.concatenate(result, 0)


def each(count, body):
    if count == 1:
        body(0)
    else:
        pl.loop(0, count)(body)


def field_kernel(
    sizes, block_order, sent_order, col_blocks_ref, rows_ref, cols_ref, fracs_ref, *refs,
):
    depth, tiles, parts, strips = sizes
    block_refs, sent_refs = refs[: len(block_order)], refs[len(block_order) : -7]
    (final_ref, velocity_ref, pairs, weights_ref, source_ref, field_ref, ordered) = refs[-7:]
    width_part = tiles * LANES
    width = parts * width_part
    height = strips * depth
    chunk = min(GROUP, strips) * depth
    chunks = height // chunk
    strip, part = lax.axis_index("strip"), lax.axis_index("cells")

    for offset, block_ref in zip(block_order, block_refs):
        first = (part ^ offset) * tiles
        for t in range(tiles):
            code = block_ref[:, t * LANES : (t + 1) * LANES].astype(f32)
            high, low = halves((code + code_half) * (block_span / code_top) + block_low)
            pairs[first + t, :LANES, :] = high
            pairs[first + t, LANES:, :] = low

    slots = parts * depth
    if len(sent_refs) == 1:
        sent = sent_refs[0]
    else:
        sent = ordered
        for offset, sent_ref in zip(sent_order, sent_refs):
            ordered[strip ^ offset] = sent_ref[...]
    group = chunk // depth
    target, origin = iota((parts * chunk, group * slots), 0), iota((parts * chunk, group * slots), 1)
    slot = origin % slots
    fits = (slot // depth == target // chunk) & (origin // slots * depth + slot % depth == target % chunk)
    chosen = jnp.where(fits, 1.0, 0.0).astype(bf16)

    def placed(values):
        high, low = halves(jnp.concatenate(values, 0))
        dot = functools.partial(jnp.dot, preferred_element_type=f32)
        return dot(chosen, high) + dot(chosen, low)

    @functools.partial(each, chunks)
    def place(g):
        terms, codes = [], []
        for n in range(group):
            got = sent[g * group + n]
            terms.append(densities(got[:slots]))
            codes.append(got[slots:].astype(f32))
        term = placed(terms)
        weight = (placed(codes) + code_half) * (weight_span / code_top) + weight_low
        here = pl.ds(pl.multiple_of(g * chunk, chunk), chunk)
        for p in range(parts):
            cut = slice(p * width_part, (p + 1) * width_part)
            weights_ref[here, cut] = weight[p * chunk : (p + 1) * chunk]
            source_ref[here, cut] = term[p * chunk : (p + 1) * chunk] / weight[p * chunk : (p + 1) * chunk]

    lanes_at_once = width if chunks == 1 else LANES
    col_blocks = [jnp.concatenate(halves(col_blocks_ref[k]), 0) for k in range(col_blocks_ref.shape[0])]
    inner = pl.ds(8, height)

    @functools.partial(each, width // lanes_at_once)
    def start(t):
        cut = pl.ds(pl.multiple_of(t * lanes_at_once, lanes_at_once), lanes_at_once)
        current = source_ref[:, cut]
        field_ref[inner, cut] = current
        source_ref[:, cut] = weights_ref[:, cut] * current - coupling * across_lines(current)

    for step in range(STEPS):

        @functools.partial(each, chunks)
        def solve_rows(g):
            here = pl.ds(pl.multiple_of(g * chunk, chunk), chunk)
            there = pl.ds(pl.multiple_of(g * chunk + 8, 8), chunk)
            source, weights, current = source_ref[here, :], weights_ref[here, :], field_ref[there, :]
            for sweep in range(SWEEPS):
                residual = source - (weights * current + coupling * along_lines(current))
                current = current + row_blockwise(residual, pairs)
            field_ref[there, :] = current
            source_ref[here, :] = weights * current - coupling * along_lines(current)

        @functools.partial(each, width // lanes_at_once)
        def solve_cols(t):
            cut = pl.ds(pl.multiple_of(t * lanes_at_once, lanes_at_once), lanes_at_once)
            middle, weights, current = source_ref[:, cut], weights_ref[:, cut], field_ref[inner, cut]
            for sweep in range(SWEEPS):
                residual = middle - (weights * current + coupling * across_lines(current))
                current = current + col_blockwise(residual, col_blocks)
            field_ref[inner, cut] = current
            if step + 1 < STEPS:
                source_ref[:, cut] = weights * current - coupling * across_lines(current)
            else:
                field_ref[:8, cut] = jnp.broadcast_to(current[:1], (8, lanes_at_once))
                field_ref[height + 8 :, cut] = jnp.broadcast_to(current[-1:], (8, lanes_at_once))

    row0 = strip * depth
    columns = pl.ds(pl.multiple_of(part * width_part, LANES), width_part)
    base, shift = pl.multiple_of(row0 // 8 * 8, 8), 17 - row0 % 8
    final_ref[...] = pltpu.roll(field_ref[pl.ds(base, 24), columns], shift, 0)[1 : 1 + depth]

    window = pltpu.roll(field_ref[pl.ds(base, 24), :], shift, 0)
    above, centre, below = window[:8], pltpu.roll(window, 23, 0)[:8], pltpu.roll(window, 22, 0)[:8]
    left, right = beside(centre)
    scale = jnp.maximum(centre, floor_level)
    velocity_y = rounded(-(0.5 * (below - above)) / scale)
    velocity_x = rounded(-(0.5 * (right - left)) / scale)

    upper = iota((8, LANES), 0) < depth

    def stacked(values):
        stack = []
        for t in range(0, parts * tiles, 2):
            even = values[:, t * LANES : (t + 1) * LANES]
            odd = values[:, (t + 1) * LANES : (t + 2) * LANES]
            stack.append(jnp.where(upper, even, pltpu.roll(odd, depth, 0)))
        return jnp.concatenate(stack, 0)

    half = LANES // 2

    def table_of(values):
        stack = stacked(values)
        many = stack.shape[0]
        blank = jnp.zeros((LANES - many, LANES), f32)
        turned = jnp.concatenate([stack, blank], 0).T
        after = jnp.concatenate([pltpu.roll(stack, many - depth, 0), blank], 0).T[:8]
        return jnp.concatenate([turned[: half + 8], jnp.concatenate([turned[half:], after], 0)], 1)

    table = jnp.concatenate([table_of(velocity_y), table_of(velocity_x)], 0).astype(bf16)
    many = parts * tiles * depth
    rows, cols = rows_ref[...], cols_ref[...]
    joined = 2 if rows.shape[0] % 2 == 0 else 1
    blank = jnp.zeros((LANES - many, joined * LANES), bf16)
    keys, lane = iota((many, joined * LANES), 0), iota((half + 8, joined * LANES), 0)
    for j in range(0, rows.shape[0], joined):
        cut = slice(j * LANES, (j + joined) * LANES)
        fy, fx = fracs_ref[0:1, cut], fracs_ref[1:2, cut]
        col = jnp.concatenate([cols[n : n + 1] for n in range(j, j + joined)], 1)
        row = jnp.concatenate([rows[n : n + 1] for n in range(j, j + joined)], 1)
        key = (col >> 7) * depth + row
        second = (col & half) != 0
        near, far = rounded(1.0 - fy), rounded(fy)
        looks = [
            pick(keys, jnp.where(second, -8, key), near, far).astype(bf16),
            blank,
            pick(keys, jnp.where(second, key, -8), near, far).astype(bf16),
            blank,
        ]
        sampled = jnp.dot(table, jnp.concatenate(looks, 0), preferred_element_type=f32)
        share = pick(lane, col & (half - 1), rounded(1.0 - fx), rounded(fx))
        velocity_ref[0:1, cut] = jnp.sum(sampled[: half + 8] * share, 0, keepdims=True)
        velocity_ref[1:2, cut] = jnp.sum(sampled[half + 8 :] * share, 0, keepdims=True)


def partner(values, axis, bits):
    return lax.ppermute(values, axis, [(n, n ^ bits) for n in range(lax.axis_size(axis))])


def local(pin_rows, pin_cols, pin_fracs, pin_weights, capacity, blockage, row_blocks, col_blocks):
    depth, width_part = capacity.shape
    parts, strips = lax.axis_size("cells"), lax.axis_size("strip")
    tiles = width_part // LANES
    height, width = depth * strips, width_part * parts
    pins = pin_rows.shape[0]
    by_lane = (pins // LANES, LANES)
    rows, cols = pin_rows.reshape(by_lane), pin_cols.reshape(by_lane)
    sizes = pin_weights.reshape(by_lane)
    vmem = pl.BlockSpec(memory_space=pltpu.VMEM)
    whole = pltpu.CompilerParams(vmem_limit_bytes=60 << 20)
    small = pltpu.CompilerParams(vmem_limit_bytes=16 * 1024 * 1024)
    grid_bytes = 4 * height * width
    large = pltpu.CompilerParams(vmem_limit_bytes=(20 << 20) + 6 * grid_bytes)

    carried = 2 * parts * depth
    terms, codes = pl.pallas_call(
        functools.partial(splat_kernel, tiles, parts),
        out_shape=(
            jax.ShapeDtypeStruct((carried, width_part), jnp.int16),
            jax.ShapeDtypeStruct((LANES, width_part), jnp.int16),
        ),
        in_specs=[vmem] * 7,
        out_specs=(vmem, vmem),
        compiler_params=whole,
        name="splat",
    )(rows, cols, pin_fracs, sizes, capacity, blockage, row_blocks.reshape(-1, LANES))
    gathered = lax.all_gather(terms, "cells", axis=0, tiled=True)

    def terms_of(part):
        return pl.BlockSpec((carried, width_part), lambda i: (part, 0))

    sums = pl.pallas_call(
        sum_kernel,
        grid=(1,),
        out_shape=jax.ShapeDtypeStruct((carried, width_part), jnp.int16),
        in_specs=[terms_of(part) for part in range(parts)],
        out_specs=pl.BlockSpec((carried, width_part), lambda i: (0, 0)),
        compiler_params=small,
        name="sum_terms",
    )(*[gathered] * parts)
    sums, codes = lax.optimization_barrier((sums, codes))
    sent, blocks = {0: sums}, {0: codes}
    blocks[2] = partner(codes, "cells", 2)
    blocks[1] = partner(codes, "cells", 1)
    held = blocks[2]
    if strips == 8:
        for k in (6, 4, 2):
            sent[k] = partner(sums, "strip", k)
        sent[2], sent[4], sent[6], held = lax.optimization_barrier((sent[2], sent[4], sent[6], held))
        for k in (0, 2, 4, 6):
            sent[k + 1] = partner(sent[k], "strip", 1)
    else:
        sent = {0: lax.all_gather(sums, "strip", axis=0)}
    blocks[3] = partner(held, "cells", 1)

    final, velocity = pl.pallas_call(
        functools.partial(field_kernel, (depth, tiles, parts, strips), tuple(blocks), tuple(sent)),
        out_shape=(
            jax.ShapeDtypeStruct((depth, width_part), f32),
            jax.ShapeDtypeStruct((2, pins), f32),
        ),
        in_specs=[vmem] * (4 + len(blocks) + len(sent)),
        out_specs=(vmem, vmem),
        scratch_shapes=[
            pltpu.VMEM((width // LANES, 2 * LANES, LANES), bf16),
            pltpu.VMEM((height, width), f32),
            pltpu.VMEM((height, width), f32),
            pltpu.VMEM((height + 16, width), f32),
            pltpu.VMEM((len(sent), carried, width_part), jnp.int16),
        ],
        compiler_params=large,
        name="field",
    )(col_blocks, rows, cols, pin_fracs, *blocks.values(), *sent.values())
    return final, velocity


def solution(mesh):
    placed = (
        P(("strip", "cells")),
        P(("strip", "cells")),
        P(None, ("strip", "cells")),
        P(("strip", "cells")),
        P("strip", "cells"),
        P("strip", "cells"),
        P("cells", None, None),
        P(),
    )
    return jax.shard_map(
        local,
        mesh=mesh,
        in_specs=placed,
        out_specs=(P("strip", "cells"), P(None, ("strip", "cells"))),
        check_vma=False,
    )
```

```python
import functools

import jax
import jax.numpy as jnp
from jax import lax
from jax.experimental import pallas as pl
from jax.experimental.pallas import tpu as pltpu
from jax.sharding import PartitionSpec as P

SWEEPS = 3
STEPS = 2
LANES = 128
GROUP = 8

coupling = 2.0
floor_level = 0.5
block_low, block_span = -0.002, 0.152
weight_low, weight_span = 0.5, 3.5
term_low, term_octaves = -20.0, 34.0
code_top = 65535.0
code_half = 32768.0
log_two = 0.6931471805599453

f32 = jnp.float32
bf16 = jnp.bfloat16


def iota(shape, axis):
    return lax.broadcasted_iota(jnp.int32, shape, axis)


def halves(values):
    high = values.astype(bf16)
    return high, (values - high.astype(f32)).astype(bf16)


def last_dims(left, right):
    return lax.dot_general(left, right, (((1,), (1,)), ((), ())), preferred_element_type=f32)


def pick(index, first, near, far):
    return jnp.where(index == first, near, jnp.where(index == first + 1, far, 0.0))


def rounded(values):
    return values.astype(bf16).astype(f32)


def coded(share):
    return jnp.clip(jnp.round(share * code_top), 0.0, code_top) - code_half


def stored(codes):
    return codes.astype(jnp.int32).astype(jnp.int16)


def density_codes(values):
    octave = jnp.log(jnp.maximum(values, 2.0**-40)) * (1.0 / log_two)
    return stored(coded((octave - term_low) * (1.0 / term_octaves)))


def densities(codes):
    codes = codes.astype(f32)
    octave = (codes + code_half) * (term_octaves / code_top) + term_low
    return jnp.where(codes == -code_half, 0.0, jnp.exp(octave * log_two))


def splat_kernel(
    tiles, parts, rows_ref, cols_ref, fracs_ref, pin_weights_ref, cap_ref, block_ref, row_blocks_ref, out_ref
):
    depth = cap_ref.shape[0]
    height = parts * depth
    rows, cols, sizes = rows_ref[...], cols_ref[...], pin_weights_ref[...]
    place = iota((height * (tiles + 1), LANES), 0)
    group, inner = place // height, place % height
    keys = ((inner // depth) * tiles + group - 1) * depth + inner % depth
    lane = iota((LANES + 8, LANES), 0)
    tables, lanes = [], []
    for j in range(rows.shape[0]):
        cut = slice(j * LANES, (j + 1) * LANES)
        fy, fx = fracs_ref[0:1, cut], fracs_ref[1:2, cut]
        size, col = sizes[j : j + 1], cols[j : j + 1]
        key = (col >> 7) * depth + rows[j : j + 1]
        tables.append(pick(keys, key, rounded(size * (1.0 - fy)), rounded(size * fy)).astype(bf16))
        lanes.append(pick(lane, col & 127, rounded(1.0 - fx), rounded(fx)).astype(bf16))
    total = last_dims(jnp.concatenate(tables, 1), jnp.concatenate(lanes, 1))
    first_lane = iota((height, LANES), 1) == 0
    for t in range(tiles):
        own = total[(t + 1) * height : (t + 2) * height, :LANES]
        spill = total[t * height : (t + 1) * height, LANES : LANES + 1]
        own = own + jnp.where(first_lane, spill, 0.0)
        cut = slice(t * LANES, (t + 1) * LANES)
        out_ref[:height, cut] = density_codes(own)
        share = (row_blocks_ref[t * LANES : (t + 1) * LANES, :] - block_low) * (1.0 / block_span)
        out_ref[2 * height :, cut] = stored(coded(share))
    weights = cap_ref[...].astype(f32) * (1.0 - block_ref[...])
    code = coded((weights - weight_low) * (1.0 / weight_span))
    row = iota((height, weights.shape[1]), 0)
    mine = row // depth == lax.axis_index("cells")
    out_ref[height : 2 * height, :] = stored(jnp.where(mine, jnp.concatenate([code] * parts, 0), 0.0))


def sum_kernel(*refs):
    sent_refs, out_ref = refs[:-1], refs[-1]
    height = out_ref.shape[0] // 2
    terms, codes = 0.0, 0.0
    for sent_ref in sent_refs:
        terms += densities(sent_ref[:height, :])
        codes += sent_ref[height:, :].astype(f32)
    out_ref[:height, :] = density_codes(terms)
    out_ref[height:, :] = stored(codes)


def beside(values):
    width = values.shape[1]
    lane = iota((values.shape[0], LANES), 1)
    left, right = pltpu.roll(values, 1, 1), pltpu.roll(values, width - 1, 1)
    first = jnp.where(lane == 0, values[:, :LANES], left[:, :LANES])
    last = jnp.where(lane == LANES - 1, values[:, width - LANES :], right[:, width - LANES :])
    return (
        jnp.concatenate([first, left[:, LANES:]], 1),
        jnp.concatenate([right[:, : width - LANES], last], 1),
    )


class Turned:
    def __init__(self, tiles):
        self.tiles, self.turned = tiles, {}

    def turn(self, t, shift):
        if (t, shift) not in self.turned:
            self.turned[t, shift] = pltpu.roll(self.tiles[t], shift, 1)
        return self.turned[t, shift]

    def along(self, t):
        mine, back = self.tiles[t], LANES - 1
        lane = iota(mine.shape, 1)
        before = self.turn(t - 1, 1) if t else mine
        after = self.turn(t + 1, back) if t + 1 < len(self.tiles) else mine
        left = jnp.where(lane == 0, before, self.turn(t, 1))
        right = jnp.where(lane == back, after, self.turn(t, back))
        return 2.0 * mine - left - right


def delayed(count, first, second, delay=2):
    waiting, results = [], []
    for t in range(count + delay):
        if t < count:
            waiting.append(first(t))
        if t >= delay:
            results.append(second(t - delay, waiting[t - delay]))
            waiting[t - delay] = None
    return results


def across_lines(values):
    height = values.shape[0]
    row = iota((8, values.shape[1]), 0)
    above, below = pltpu.roll(values, 1, 0), pltpu.roll(values, height - 1, 0)
    first = jnp.where(row == 0, values[:8], above[:8])
    last = jnp.where(row == 7, values[height - 8 :], below[height - 8 :])
    above = jnp.concatenate([first, above[8:]], 0)
    below = jnp.concatenate([below[: height - 8], last], 0)
    return 2.0 * values - above - below


def col_products(residual, blocks):
    high, low = halves(residual)
    size = blocks[0].shape[0] // 2
    dot = functools.partial(jnp.dot, preferred_element_type=f32)
    cuts = [slice(k * size, (k + 1) * size) for k in range(len(blocks))]
    return [(dot(pair, high[cut]), dot(pair[:size], low[cut])) for pair, cut in zip(blocks, cuts)]


def col_sum(products):
    size = products[0][1].shape[0]
    result = [both[:size] + (both[size:] + rest) for both, rest in products]
    return result[0] if len(result) == 1 else jnp.concatenate(result, 0)


def each(count, body):
    if count == 1:
        body(0)
    else:
        pl.loop(0, count)(body)


def field_kernel(
    sizes, blocks_ref, col_blocks_ref, rows_ref, cols_ref, fracs_ref, *refs,
):
    depth, tiles, parts, strips = sizes
    sent_refs, (final_ref, velocity_ref, pairs, weights_ref, source_ref, field_ref, ordered) = refs[:-7], refs[-7:]
    width_part = tiles * LANES
    width = parts * width_part
    height = strips * depth
    chunk = min(GROUP, strips) * depth
    chunks = height // chunk
    strip, part = lax.axis_index("strip"), lax.axis_index("cells")

    for k in range(pairs.shape[0]):
        base = (k // tiles) * (2 * parts * depth + LANES) + 2 * parts * depth
        code = blocks_ref[base : base + LANES, k % tiles * LANES : (k % tiles + 1) * LANES].astype(f32)
        high, low = halves((code + code_half) * (block_span / code_top) + block_low)
        pairs[k, :LANES, :] = high
        pairs[k, LANES:, :] = low

    slots = parts * depth
    if len(sent_refs) == 1:
        sent = sent_refs[0]
    else:
        sent = ordered
        for k, sent_ref in enumerate(sent_refs):
            ordered[strip ^ k] = sent_ref[...]
    group = chunk // depth
    target, origin = iota((parts * chunk, group * slots), 0), iota((parts * chunk, group * slots), 1)
    slot = origin % slots
    fits = (slot // depth == target // chunk) & (origin // slots * depth + slot % depth == target % chunk)
    chosen = jnp.where(fits, 1.0, 0.0).astype(bf16)

    def placed(values):
        high, low = halves(jnp.concatenate(values, 0))
        dot = functools.partial(jnp.dot, preferred_element_type=f32)
        return dot(chosen, high) + dot(chosen, low)

    @functools.partial(each, chunks)
    def place(g):
        terms, codes = [], []
        for n in range(group):
            got = sent[g * group + n]
            terms.append(densities(got[:slots]))
            codes.append(got[slots:].astype(f32))
        term = placed(terms)
        weight = (placed(codes) + code_half) * (weight_span / code_top) + weight_low
        here = pl.ds(pl.multiple_of(g * chunk, chunk), chunk)
        for p in range(parts):
            cut = slice(p * width_part, (p + 1) * width_part)
            weights_ref[here, cut] = weight[p * chunk : (p + 1) * chunk]
            source_ref[here, cut] = term[p * chunk : (p + 1) * chunk] / weight[p * chunk : (p + 1) * chunk]

    col_blocks = [jnp.concatenate(halves(col_blocks_ref[k]), 0) for k in range(col_blocks_ref.shape[0])]
    inner = pl.ds(8, height)
    lanes_at_once = 2 * LANES if chunks == 1 and width % (2 * LANES) == 0 else LANES
    at_once = width // lanes_at_once if chunks == 1 else 1

    def cuts_of(g):
        if at_once > 1:
            return [slice(n * lanes_at_once, (n + 1) * lanes_at_once) for n in range(at_once)]
        return [pl.ds(pl.multiple_of(g * lanes_at_once, lanes_at_once), lanes_at_once)]

    col_steps = width // lanes_at_once // at_once

    @functools.partial(each, col_steps)
    def start(g):
        for cut in cuts_of(g):
            current = source_ref[:, cut]
            field_ref[inner, cut] = current
            source_ref[:, cut] = weights_ref[:, cut] * current - coupling * across_lines(current)

    row_tiles = [slice(t * LANES, (t + 1) * LANES) for t in range(width // LANES)]
    for step in range(STEPS):

        @functools.partial(each, chunks)
        def solve_rows(g):
            here = pl.ds(pl.multiple_of(g * chunk, chunk), chunk)
            there = pl.ds(pl.multiple_of(g * chunk + 8, 8), chunk)
            current = [field_ref[there, cut] for cut in row_tiles]
            for sweep in range(SWEEPS):
                turned = Turned(current)

                def multiply(t):
                    cut = row_tiles[t]
                    now = weights_ref[here, cut] * turned.tiles[t] + coupling * turned.along(t)
                    return last_dims(jnp.concatenate(halves(source_ref[here, cut] - now), 0), pairs[t])

                def add(t, product):
                    high, low = product[:chunk], product[chunk:]
                    return turned.tiles[t] + (high[:, :LANES] + (high[:, LANES:] + low[:, :LANES]))

                current = delayed(len(current), multiply, add)
            turned = Turned(current)
            for t, cut in enumerate(row_tiles):
                field_ref[there, cut] = current[t]
                source_ref[here, cut] = weights_ref[here, cut] * current[t] - coupling * turned.along(t)

        @functools.partial(each, col_steps)
        def solve_cols(g):
            cuts = cuts_of(g)
            current = [field_ref[inner, cut] for cut in cuts]
            for sweep in range(SWEEPS):
                before = current

                def multiply(n):
                    now = weights_ref[:, cuts[n]] * before[n] + coupling * across_lines(before[n])
                    return col_products(source_ref[:, cuts[n]] - now, col_blocks)

                current = delayed(len(cuts), multiply, lambda n, products: before[n] + col_sum(products))
            for now, cut in zip(current, cuts):
                field_ref[inner, cut] = now
                if step + 1 < STEPS:
                    source_ref[:, cut] = weights_ref[:, cut] * now - coupling * across_lines(now)
                else:
                    field_ref[:8, cut] = jnp.broadcast_to(now[:1], (8, lanes_at_once))
                    field_ref[height + 8 :, cut] = jnp.broadcast_to(now[-1:], (8, lanes_at_once))

    row0 = strip * depth
    columns = pl.ds(pl.multiple_of(part * width_part, LANES), width_part)
    base, shift = pl.multiple_of(row0 // 8 * 8, 8), 17 - row0 % 8
    final_ref[...] = pltpu.roll(field_ref[pl.ds(base, 24), columns], shift, 0)[1 : 1 + depth]

    window = pltpu.roll(field_ref[pl.ds(base, 24), :], shift, 0)
    above, centre, below = window[:8], pltpu.roll(window, 23, 0)[:8], pltpu.roll(window, 22, 0)[:8]
    left, right = beside(centre)
    scale = jnp.maximum(centre, floor_level)
    velocity_y = rounded(-(0.5 * (below - above)) / scale)
    velocity_x = rounded(-(0.5 * (right - left)) / scale)

    upper = iota((8, LANES), 0) < depth

    def stacked(values):
        stack = []
        for t in range(0, parts * tiles, 2):
            even = values[:, t * LANES : (t + 1) * LANES]
            odd = values[:, (t + 1) * LANES : (t + 2) * LANES]
            stack.append(jnp.where(upper, even, pltpu.roll(odd, depth, 0)))
        return jnp.concatenate(stack, 0)

    half = LANES // 2

    def table_of(values):
        stack = stacked(values)
        many = stack.shape[0]
        blank = jnp.zeros((LANES - many, LANES), f32)
        turned = jnp.concatenate([stack, blank], 0).T
        after = jnp.concatenate([pltpu.roll(stack, many - depth, 0), blank], 0).T[:8]
        return jnp.concatenate([turned[: half + 8], jnp.concatenate([turned[half:], after], 0)], 1)

    table = jnp.concatenate([table_of(velocity_y), table_of(velocity_x)], 0).astype(bf16)
    many = parts * tiles * depth
    rows, cols = rows_ref[...], cols_ref[...]
    joined = 2 if rows.shape[0] % 2 == 0 else 1
    blank = jnp.zeros((LANES - many, joined * LANES), bf16)
    keys, lane = iota((many, joined * LANES), 0), iota((half + 8, joined * LANES), 0)
    for j in range(0, rows.shape[0], joined):
        cut = slice(j * LANES, (j + joined) * LANES)
        fy, fx = fracs_ref[0:1, cut], fracs_ref[1:2, cut]
        col = jnp.concatenate([cols[n : n + 1] for n in range(j, j + joined)], 1)
        row = jnp.concatenate([rows[n : n + 1] for n in range(j, j + joined)], 1)
        key = (col >> 7) * depth + row
        second = (col & half) != 0
        near, far = rounded(1.0 - fy), rounded(fy)
        looks = [
            pick(keys, jnp.where(second, -8, key), near, far).astype(bf16),
            blank,
            pick(keys, jnp.where(second, key, -8), near, far).astype(bf16),
            blank,
        ]
        sampled = jnp.dot(table, jnp.concatenate(looks, 0), preferred_element_type=f32)
        share = pick(lane, col & (half - 1), rounded(1.0 - fx), rounded(fx))
        velocity_ref[0:1, cut] = jnp.sum(sampled[: half + 8] * share, 0, keepdims=True)
        velocity_ref[1:2, cut] = jnp.sum(sampled[half + 8 :] * share, 0, keepdims=True)


def local(pin_rows, pin_cols, pin_fracs, pin_weights, capacity, blockage, row_blocks, col_blocks):
    depth, width_part = capacity.shape
    parts, strips = lax.axis_size("cells"), lax.axis_size("strip")
    tiles = width_part // LANES
    height, width = depth * strips, width_part * parts
    pins = pin_rows.shape[0]
    by_lane = (pins // LANES, LANES)
    rows, cols = pin_rows.reshape(by_lane), pin_cols.reshape(by_lane)
    sizes = pin_weights.reshape(by_lane)
    vmem = pl.BlockSpec(memory_space=pltpu.VMEM)
    whole = pltpu.CompilerParams(vmem_limit_bytes=60 << 20)
    small = pltpu.CompilerParams(vmem_limit_bytes=16 * 1024 * 1024)
    grid_bytes = 4 * height * width
    large = pltpu.CompilerParams(vmem_limit_bytes=(20 << 20) + 6 * grid_bytes)

    carried = 2 * parts * depth
    terms = pl.pallas_call(
        functools.partial(splat_kernel, tiles, parts),
        out_shape=jax.ShapeDtypeStruct((carried + LANES, width_part), jnp.int16),
        in_specs=[vmem] * 7,
        out_specs=vmem,
        compiler_params=whole,
        name="splat",
    )(rows, cols, pin_fracs, sizes, capacity, blockage, row_blocks.reshape(-1, LANES))
    blocks = lax.all_gather(terms, "cells", axis=0, tiled=True)

    def terms_of(part):
        place = part * (carried + LANES) // carried
        return pl.BlockSpec((carried, width_part), lambda i: (place, 0))

    sums = pl.pallas_call(
        sum_kernel,
        grid=(1,),
        out_shape=jax.ShapeDtypeStruct((carried, width_part), jnp.int16),
        in_specs=[terms_of(part) for part in range(parts)],
        out_specs=pl.BlockSpec((carried, width_part), lambda i: (0, 0)),
        compiler_params=small,
        name="sum_terms",
    )(*[blocks] * parts)
    if strips == 8:
        sent = [sums] + [None] * 7
        for k in (6, 7, 4, 5, 2, 3, 1):
            sent[k] = lax.ppermute(sums, "strip", [(n, n ^ k) for n in range(strips)])
    else:
        sent = [lax.all_gather(sums, "strip", axis=0)]

    final, velocity = pl.pallas_call(
        functools.partial(field_kernel, (depth, tiles, parts, strips)),
        out_shape=(
            jax.ShapeDtypeStruct((depth, width_part), f32),
            jax.ShapeDtypeStruct((2, pins), f32),
        ),
        in_specs=[vmem] * (5 + len(sent)),
        out_specs=(vmem, vmem),
        scratch_shapes=[
            pltpu.VMEM((width // LANES, 2 * LANES, LANES), bf16),
            pltpu.VMEM((height, width), f32),
            pltpu.VMEM((height, width), f32),
            pltpu.VMEM((height + 16, width), f32),
            pltpu.VMEM((len(sent), carried, width_part), jnp.int16),
        ],
        compiler_params=large,
        name="field",
    )(blocks, col_blocks, rows, cols, pin_fracs, *sent)
    return final, velocity


def solution(mesh):
    placed = (
        P(("strip", "cells")),
        P(("strip", "cells")),
        P(None, ("strip", "cells")),
        P(("strip", "cells")),
        P("strip", "cells"),
        P("strip", "cells"),
        P("cells", None, None),
        P(),
    )
    return jax.shard_map(
        local,
        mesh=mesh,
        in_specs=placed,
        out_specs=(P("strip", "cells"), P(None, ("strip", "cells"))),
        check_vma=False,
    )
```

```python
import functools

import jax
import jax.numpy as jnp
from jax import lax
from jax.experimental import pallas as pl
from jax.experimental.pallas import tpu as pltpu
from jax.sharding import PartitionSpec as P

SWEEPS = 3
STEPS = 2
LANES = 128
GROUP = 8

coupling = 2.0
floor_level = 0.5
block_low, block_span = -0.002, 0.152
weight_low, weight_span = 0.5, 3.5
term_low, term_octaves = -20.0, 34.0
code_top = 65535.0
code_half = 32768.0
log_two = 0.6931471805599453

f32 = jnp.float32
bf16 = jnp.bfloat16


def iota(shape, axis):
    return lax.broadcasted_iota(jnp.int32, shape, axis)


def halves(values):
    high = values.astype(bf16)
    return high, (values - high.astype(f32)).astype(bf16)


def last_dims(left, right):
    return lax.dot_general(left, right, (((1,), (1,)), ((), ())), preferred_element_type=f32)


def pick(index, first, near, far):
    return jnp.where(index == first, near, jnp.where(index == first + 1, far, 0.0))


def rounded(values):
    return values.astype(bf16).astype(f32)


def coded(share):
    return jnp.clip(jnp.round(share * code_top), 0.0, code_top) - code_half


def stored(codes):
    return codes.astype(jnp.int32).astype(jnp.int16)


def density_codes(values):
    octave = jnp.log(jnp.maximum(values, 2.0**-40)) * (1.0 / log_two)
    return stored(coded((octave - term_low) * (1.0 / term_octaves)))


def densities(codes):
    codes = codes.astype(f32)
    octave = (codes + code_half) * (term_octaves / code_top) + term_low
    return jnp.where(codes == -code_half, 0.0, jnp.exp(octave * log_two))


def splat_kernel(
    tiles, parts, rows_in, cols_in, fracs_in, pin_weights_in, row_blocks_in, cap_in, block_in, out_ref,
    rows_ref, cols_ref, fracs_ref, pin_weights_ref, row_blocks_ref, cap_ref, block_ref, arrived,
):
    depth = cap_ref.shape[0]
    height = parts * depth
    sources = (rows_in, cols_in, fracs_in, pin_weights_in, row_blocks_in, cap_in, block_in)
    places = (rows_ref, cols_ref, fracs_ref, pin_weights_ref, row_blocks_ref, cap_ref, block_ref)
    copies = [
        pltpu.make_async_copy(source, place, arrived.at[n]) for n, (source, place) in enumerate(zip(sources, places))
    ]
    for copy in copies:
        copy.start()
    for copy in copies[:4]:
        copy.wait()
    rows, cols, sizes = rows_ref[...], cols_ref[...], pin_weights_ref[...]
    place = iota((height * (tiles + 1), LANES), 0)
    group, inner = place // height, place % height
    keys = ((inner // depth) * tiles + group - 1) * depth + inner % depth
    lane = iota((LANES + 8, LANES), 0)
    tables, lanes = [], []
    for j in range(rows.shape[0]):
        cut = slice(j * LANES, (j + 1) * LANES)
        fy, fx = fracs_ref[0:1, cut], fracs_ref[1:2, cut]
        size, col = sizes[j : j + 1], cols[j : j + 1]
        key = (col >> 7) * depth + rows[j : j + 1]
        tables.append(pick(keys, key, rounded(size * (1.0 - fy)), rounded(size * fy)).astype(bf16))
        lanes.append(pick(lane, col & 127, rounded(1.0 - fx), rounded(fx)).astype(bf16))
    total = last_dims(jnp.concatenate(tables, 1), jnp.concatenate(lanes, 1))
    for copy in copies[4:]:
        copy.wait()
    first_lane = iota((height, LANES), 1) == 0
    for t in range(tiles):
        own = total[(t + 1) * height : (t + 2) * height, :LANES]
        spill = total[t * height : (t + 1) * height, LANES : LANES + 1]
        own = own + jnp.where(first_lane, spill, 0.0)
        cut = slice(t * LANES, (t + 1) * LANES)
        out_ref[:height, cut] = density_codes(own)
        share = (row_blocks_ref[t * LANES : (t + 1) * LANES, :] - block_low) * (1.0 / block_span)
        out_ref[2 * height :, cut] = stored(coded(share))
    weights = cap_ref[...].astype(f32) * (1.0 - block_ref[...])
    code = coded((weights - weight_low) * (1.0 / weight_span))
    row = iota((height, weights.shape[1]), 0)
    mine = row // depth == lax.axis_index("cells")
    out_ref[height : 2 * height, :] = stored(jnp.where(mine, jnp.concatenate([code] * parts, 0), 0.0))


def sum_kernel(*refs):
    sent_refs, out_ref = refs[:-1], refs[-1]
    height = out_ref.shape[0] // 2
    terms, codes = 0.0, 0.0
    for sent_ref in sent_refs:
        terms += densities(sent_ref[:height, :])
        codes += sent_ref[height:, :].astype(f32)
    out_ref[:height, :] = density_codes(terms)
    out_ref[height:, :] = stored(codes)


def beside(values):
    width = values.shape[1]
    lane = iota((values.shape[0], LANES), 1)
    left, right = pltpu.roll(values, 1, 1), pltpu.roll(values, width - 1, 1)
    first = jnp.where(lane == 0, values[:, :LANES], left[:, :LANES])
    last = jnp.where(lane == LANES - 1, values[:, width - LANES :], right[:, width - LANES :])
    return (
        jnp.concatenate([first, left[:, LANES:]], 1),
        jnp.concatenate([right[:, : width - LANES], last], 1),
    )


class Turned:
    def __init__(self, tiles):
        self.tiles, self.turned = tiles, {}

    def turn(self, t, shift):
        if (t, shift) not in self.turned:
            self.turned[t, shift] = pltpu.roll(self.tiles[t], shift, 1)
        return self.turned[t, shift]

    def along(self, t):
        mine, back = self.tiles[t], LANES - 1
        lane = iota(mine.shape, 1)
        before = self.turn(t - 1, 1) if t else mine
        after = self.turn(t + 1, back) if t + 1 < len(self.tiles) else mine
        left = jnp.where(lane == 0, before, self.turn(t, 1))
        right = jnp.where(lane == back, after, self.turn(t, back))
        return 2.0 * mine - left - right


def delayed(count, first, second, delay=2):
    waiting, results = [], []
    for t in range(count + delay):
        if t < count:
            waiting.append(first(t))
        if t >= delay:
            results.append(second(t - delay, waiting[t - delay]))
            waiting[t - delay] = None
    return results


def across_lines(values):
    height = values.shape[0]
    row = iota((8, values.shape[1]), 0)
    above, below = pltpu.roll(values, 1, 0), pltpu.roll(values, height - 1, 0)
    first = jnp.where(row == 0, values[:8], above[:8])
    last = jnp.where(row == 7, values[height - 8 :], below[height - 8 :])
    above = jnp.concatenate([first, above[8:]], 0)
    below = jnp.concatenate([below[: height - 8], last], 0)
    return 2.0 * values - above - below


def col_products(residual, blocks):
    high, low = halves(residual)
    size = blocks[0].shape[0] // 2
    dot = functools.partial(jnp.dot, preferred_element_type=f32)
    cuts = [slice(k * size, (k + 1) * size) for k in range(len(blocks))]
    return [(dot(pair, high[cut]), dot(pair[:size], low[cut])) for pair, cut in zip(blocks, cuts)]


def col_sum(products):
    size = products[0][1].shape[0]
    result = [both[:size] + (both[size:] + rest) for both, rest in products]
    return result[0] if len(result) == 1 else jnp.concatenate(result, 0)


def each(count, body):
    if count == 1:
        body(0)
    else:
        pl.loop(0, count)(body)


def join_kernel(*refs):
    for n, ref in enumerate(refs[:-1]):
        refs[-1][n * ref.shape[0] : (n + 1) * ref.shape[0], :] = ref[...]


def unpack_kernel(tiles, carried, codes_ref, pairs_ref):
    for k in range(pairs_ref.shape[0]):
        base = (k // tiles) * (carried + LANES) + carried
        code = codes_ref[base : base + LANES, k % tiles * LANES : (k % tiles + 1) * LANES].astype(f32)
        high, low = halves((code + code_half) * (block_span / code_top) + block_low)
        pairs_ref[k, :LANES, :] = high
        pairs_ref[k, LANES:, :] = low


def field_kernel(
    sizes, pairs, col_blocks_ref, rows_ref, cols_ref, fracs_ref, *refs,
):
    depth, tiles, parts, strips = sizes
    sent_refs, (final_ref, velocity_ref, weights_ref, source_ref, field_ref, ordered) = refs[:-6], refs[-6:]
    width_part = tiles * LANES
    width = parts * width_part
    height = strips * depth
    chunk = min(GROUP, strips) * depth
    chunks = height // chunk
    strip, part = lax.axis_index("strip"), lax.axis_index("cells")

    slots = parts * depth
    if len(sent_refs) == 1:
        sent = sent_refs[0]
    else:
        sent = ordered
        for near, sent_ref in enumerate(sent_refs):
            for n in range(strips // 2):
                ordered[strip ^ (2 * n + near)] = sent_ref[n * 2 * slots : (n + 1) * 2 * slots, :]
    group = chunk // depth
    target, origin = iota((parts * chunk, group * slots), 0), iota((parts * chunk, group * slots), 1)
    slot = origin % slots
    fits = (slot // depth == target // chunk) & (origin // slots * depth + slot % depth == target % chunk)
    chosen = jnp.where(fits, 1.0, 0.0).astype(bf16)

    def placed(values):
        high, low = halves(jnp.concatenate(values, 0))
        dot = functools.partial(jnp.dot, preferred_element_type=f32)
        return dot(chosen, high) + dot(chosen, low)

    @functools.partial(each, chunks)
    def place(g):
        terms, codes = [], []
        for n in range(group):
            got = sent[g * group + n]
            terms.append(densities(got[:slots]))
            codes.append(got[slots:].astype(f32))
        term = placed(terms)
        weight = (placed(codes) + code_half) * (weight_span / code_top) + weight_low
        here = pl.ds(pl.multiple_of(g * chunk, chunk), chunk)
        for p in range(parts):
            cut = slice(p * width_part, (p + 1) * width_part)
            weights_ref[here, cut] = weight[p * chunk : (p + 1) * chunk]
            source_ref[here, cut] = term[p * chunk : (p + 1) * chunk] / weight[p * chunk : (p + 1) * chunk]

    col_blocks = [jnp.concatenate(halves(col_blocks_ref[k]), 0) for k in range(col_blocks_ref.shape[0])]
    inner = pl.ds(8, height)
    lanes_at_once = 2 * LANES if chunks == 1 and width % (2 * LANES) == 0 else LANES
    at_once = width // lanes_at_once if chunks == 1 else 1

    def cuts_of(g):
        if at_once > 1:
            return [slice(n * lanes_at_once, (n + 1) * lanes_at_once) for n in range(at_once)]
        return [pl.ds(pl.multiple_of(g * lanes_at_once, lanes_at_once), lanes_at_once)]

    col_steps = width // lanes_at_once // at_once

    @functools.partial(each, col_steps)
    def start(g):
        for cut in cuts_of(g):
            current = source_ref[:, cut]
            field_ref[inner, cut] = current
            source_ref[:, cut] = weights_ref[:, cut] * current - coupling * across_lines(current)

    row_tiles = [slice(t * LANES, (t + 1) * LANES) for t in range(width // LANES)]
    for step in range(STEPS):

        @functools.partial(each, chunks)
        def solve_rows(g):
            here = pl.ds(pl.multiple_of(g * chunk, chunk), chunk)
            there = pl.ds(pl.multiple_of(g * chunk + 8, 8), chunk)
            current = [field_ref[there, cut] for cut in row_tiles]
            for sweep in range(SWEEPS):
                turned = Turned(current)

                def multiply(t):
                    cut = row_tiles[t]
                    now = weights_ref[here, cut] * turned.tiles[t] + coupling * turned.along(t)
                    return last_dims(jnp.concatenate(halves(source_ref[here, cut] - now), 0), pairs[t])

                def add(t, product):
                    high, low = product[:chunk], product[chunk:]
                    return turned.tiles[t] + (high[:, :LANES] + (high[:, LANES:] + low[:, :LANES]))

                current = delayed(len(current), multiply, add)
            turned = Turned(current)
            for t, cut in enumerate(row_tiles):
                field_ref[there, cut] = current[t]
                source_ref[here, cut] = weights_ref[here, cut] * current[t] - coupling * turned.along(t)

        @functools.partial(each, col_steps)
        def solve_cols(g):
            cuts = cuts_of(g)
            current = [field_ref[inner, cut] for cut in cuts]
            for sweep in range(SWEEPS):
                before = current

                def multiply(n):
                    now = weights_ref[:, cuts[n]] * before[n] + coupling * across_lines(before[n])
                    return col_products(source_ref[:, cuts[n]] - now, col_blocks)

                current = delayed(len(cuts), multiply, lambda n, products: before[n] + col_sum(products))
            for now, cut in zip(current, cuts):
                field_ref[inner, cut] = now
                if step + 1 < STEPS:
                    source_ref[:, cut] = weights_ref[:, cut] * now - coupling * across_lines(now)
                else:
                    field_ref[:8, cut] = jnp.broadcast_to(now[:1], (8, lanes_at_once))
                    field_ref[height + 8 :, cut] = jnp.broadcast_to(now[-1:], (8, lanes_at_once))

    row0 = strip * depth
    columns = pl.ds(pl.multiple_of(part * width_part, LANES), width_part)
    base, shift = pl.multiple_of(row0 // 8 * 8, 8), 17 - row0 % 8
    final_ref[...] = pltpu.roll(field_ref[pl.ds(base, 24), columns], shift, 0)[1 : 1 + depth]

    window = pltpu.roll(field_ref[pl.ds(base, 24), :], shift, 0)
    above, centre, below = window[:8], pltpu.roll(window, 23, 0)[:8], pltpu.roll(window, 22, 0)[:8]
    left, right = beside(centre)
    scale = jnp.maximum(centre, floor_level)
    velocity_y = rounded(-(0.5 * (below - above)) / scale)
    velocity_x = rounded(-(0.5 * (right - left)) / scale)

    upper = iota((8, LANES), 0) < depth

    def stacked(values):
        stack = []
        for t in range(0, parts * tiles, 2):
            even = values[:, t * LANES : (t + 1) * LANES]
            odd = values[:, (t + 1) * LANES : (t + 2) * LANES]
            stack.append(jnp.where(upper, even, pltpu.roll(odd, depth, 0)))
        return jnp.concatenate(stack, 0)

    half = LANES // 2

    def table_of(values):
        stack = stacked(values)
        many = stack.shape[0]
        blank = jnp.zeros((LANES - many, LANES), f32)
        turned = jnp.concatenate([stack, blank], 0).T
        after = jnp.concatenate([pltpu.roll(stack, many - depth, 0), blank], 0).T[:8]
        return jnp.concatenate([turned[: half + 8], jnp.concatenate([turned[half:], after], 0)], 1)

    table = jnp.concatenate([table_of(velocity_y), table_of(velocity_x)], 0).astype(bf16)
    many = parts * tiles * depth
    rows, cols = rows_ref[...], cols_ref[...]
    joined = 2 if rows.shape[0] % 2 == 0 else 1
    blank = jnp.zeros((LANES - many, joined * LANES), bf16)
    keys, lane = iota((many, joined * LANES), 0), iota((half + 8, joined * LANES), 0)
    for j in range(0, rows.shape[0], joined):
        cut = slice(j * LANES, (j + joined) * LANES)
        fy, fx = fracs_ref[0:1, cut], fracs_ref[1:2, cut]
        col = jnp.concatenate([cols[n : n + 1] for n in range(j, j + joined)], 1)
        row = jnp.concatenate([rows[n : n + 1] for n in range(j, j + joined)], 1)
        key = (col >> 7) * depth + row
        second = (col & half) != 0
        near, far = rounded(1.0 - fy), rounded(fy)
        looks = [
            pick(keys, jnp.where(second, -8, key), near, far).astype(bf16),
            blank,
            pick(keys, jnp.where(second, key, -8), near, far).astype(bf16),
            blank,
        ]
        sampled = jnp.dot(table, jnp.concatenate(looks, 0), preferred_element_type=f32)
        share = pick(lane, col & (half - 1), rounded(1.0 - fx), rounded(fx))
        velocity_ref[0:1, cut] = jnp.sum(sampled[: half + 8] * share, 0, keepdims=True)
        velocity_ref[1:2, cut] = jnp.sum(sampled[half + 8 :] * share, 0, keepdims=True)


def partner(values, axis, bits):
    return lax.ppermute(values, axis, [(n, n ^ bits) for n in range(lax.axis_size(axis))])


def local(pin_rows, pin_cols, pin_fracs, pin_weights, capacity, blockage, row_blocks, col_blocks):
    depth, width_part = capacity.shape
    parts, strips = lax.axis_size("cells"), lax.axis_size("strip")
    tiles = width_part // LANES
    height, width = depth * strips, width_part * parts
    pins = pin_rows.shape[0]
    by_lane = (pins // LANES, LANES)
    rows, cols = pin_rows.reshape(by_lane), pin_cols.reshape(by_lane)
    sizes = pin_weights.reshape(by_lane)
    vmem = pl.BlockSpec(memory_space=pltpu.VMEM)
    whole = pltpu.CompilerParams(vmem_limit_bytes=60 << 20)
    small = pltpu.CompilerParams(vmem_limit_bytes=16 * 1024 * 1024)
    grid_bytes = 4 * height * width
    large = pltpu.CompilerParams(vmem_limit_bytes=(20 << 20) + 6 * grid_bytes)

    carried = 2 * parts * depth
    read = (rows, cols, pin_fracs, sizes, row_blocks.reshape(-1, LANES), capacity, blockage)
    terms = pl.pallas_call(
        functools.partial(splat_kernel, tiles, parts),
        out_shape=jax.ShapeDtypeStruct((carried + LANES, width_part), jnp.int16),
        in_specs=[pl.BlockSpec(memory_space=pltpu.HBM)] * 7,
        out_specs=vmem,
        scratch_shapes=[pltpu.VMEM(item.shape, item.dtype) for item in read] + [pltpu.SemaphoreType.DMA((7,))],
        compiler_params=whole,
        name="splat",
    )(*read)
    blocks = lax.all_gather(terms, "cells", axis=0, tiled=True)

    def terms_of(part):
        place = part * (carried + LANES) // carried
        return pl.BlockSpec((carried, width_part), lambda i: (place, 0))

    sums = pl.pallas_call(
        sum_kernel,
        grid=(1,),
        out_shape=jax.ShapeDtypeStruct((carried, width_part), jnp.int16),
        in_specs=[terms_of(part) for part in range(parts)],
        out_specs=pl.BlockSpec((carried, width_part), lambda i: (0, 0)),
        compiler_params=small,
        name="sum_terms",
    )(*[blocks] * parts)
    if strips == 8:
        from_z = {k: partner(sums, "strip", k) for k in (6, 4, 2)}
        held = pl.pallas_call(
            join_kernel,
            out_shape=jax.ShapeDtypeStruct((strips // 2 * carried, width_part), jnp.int16),
            in_specs=[vmem] * 4,
            out_specs=vmem,
            compiler_params=small,
            name="join",
        )(sums, from_z[2], from_z[4], from_z[6])
        held, blocks = lax.optimization_barrier((held, blocks))
        sent = [held, partner(held, "strip", 1)]
    else:
        sent = [lax.all_gather(sums, "strip", axis=0)]
    pairs = pl.pallas_call(
        functools.partial(unpack_kernel, tiles, carried),
        out_shape=jax.ShapeDtypeStruct((width // LANES, 2 * LANES, LANES), bf16),
        in_specs=[vmem],
        out_specs=vmem,
        compiler_params=small,
        cost_estimate=pl.CostEstimate(flops=1 << 20, bytes_accessed=1 << 21, transcendentals=0),
        name="unpack",
    )(blocks)

    final, velocity = pl.pallas_call(
        functools.partial(field_kernel, (depth, tiles, parts, strips)),
        out_shape=(
            jax.ShapeDtypeStruct((depth, width_part), f32),
            jax.ShapeDtypeStruct((2, pins), f32),
        ),
        in_specs=[vmem] * (5 + len(sent)),
        out_specs=(vmem, vmem),
        scratch_shapes=[
            pltpu.VMEM((height, width), f32),
            pltpu.VMEM((height, width), f32),
            pltpu.VMEM((height + 16, width), f32),
            pltpu.VMEM((strips if len(sent) > 1 else 1, carried, width_part), jnp.int16),
        ],
        compiler_params=large,
        name="field",
    )(pairs, col_blocks, rows, cols, pin_fracs, *sent)
    return final, velocity


def solution(mesh):
    placed = (
        P(("strip", "cells")),
        P(("strip", "cells")),
        P(None, ("strip", "cells")),
        P(("strip", "cells")),
        P("strip", "cells"),
        P("strip", "cells"),
        P("cells", None, None),
        P(),
    )
    return jax.shard_map(
        local,
        mesh=mesh,
        in_specs=placed,
        out_specs=(P("strip", "cells"), P(None, ("strip", "cells"))),
        check_vma=False,
    )
```

```python
import functools

import jax
import jax.numpy as jnp
from jax import lax
from jax.experimental import pallas as pl
from jax.experimental.pallas import tpu as pltpu
from jax.sharding import PartitionSpec as P

SWEEPS = 3
STEPS = 2
LANES = 128
GROUP = 8

coupling = 2.0
floor_level = 0.5
block_low, block_span = -0.002, 0.152
weight_low, weight_span = 0.5, 3.5
term_low, term_octaves = -20.0, 34.0
code_top = 65535.0
code_half = 32768.0
log_two = 0.6931471805599453

f32 = jnp.float32
bf16 = jnp.bfloat16


def iota(shape, axis):
    return lax.broadcasted_iota(jnp.int32, shape, axis)


def halves(values):
    high = values.astype(bf16)
    return high, (values - high.astype(f32)).astype(bf16)


def last_dims(left, right):
    return lax.dot_general(left, right, (((1,), (1,)), ((), ())), preferred_element_type=f32)


def pick(index, first, near, far):
    return jnp.where(index == first, near, jnp.where(index == first + 1, far, 0.0))


def rounded(values):
    return values.astype(bf16).astype(f32)


def coded(share):
    return jnp.clip(jnp.round(share * code_top), 0.0, code_top) - code_half


def stored(codes):
    return codes.astype(jnp.int32).astype(jnp.int16)


def density_codes(values):
    octave = jnp.log(jnp.maximum(values, 2.0**-40)) * (1.0 / log_two)
    return coded((octave - term_low) * (1.0 / term_octaves))


def densities(codes):
    codes = codes.astype(f32)
    octave = (codes + code_half) * (term_octaves / code_top) + term_low
    return jnp.where(codes == -code_half, 0.0, jnp.exp(octave * log_two))


def splat_kernel(
    tiles, parts, rows_in, cols_in, fracs_in, pin_weights_in, row_blocks_in, cap_in, block_in, out_ref,
    rows_ref, cols_ref, fracs_ref, pin_weights_ref, row_blocks_ref, cap_ref, block_ref, arrived,
):
    depth = cap_ref.shape[0]
    height = parts * depth
    sources = (rows_in, cols_in, fracs_in, pin_weights_in, row_blocks_in, cap_in, block_in)
    places = (rows_ref, cols_ref, fracs_ref, pin_weights_ref, row_blocks_ref, cap_ref, block_ref)
    copies = [
        pltpu.make_async_copy(source, place, arrived.at[n]) for n, (source, place) in enumerate(zip(sources, places))
    ]
    for copy in copies:
        copy.start()
    for copy in copies[:4]:
        copy.wait()
    rows, cols, sizes = rows_ref[...], cols_ref[...], pin_weights_ref[...]
    place = iota((height * (tiles + 1), LANES), 0)
    group, inner = place // height, place % height
    keys = ((inner // depth) * tiles + group - 1) * depth + inner % depth
    lane = iota((LANES + 8, LANES), 0)
    tables, lanes = [], []
    for j in range(rows.shape[0]):
        cut = slice(j * LANES, (j + 1) * LANES)
        fy, fx = fracs_ref[0:1, cut], fracs_ref[1:2, cut]
        size, col = sizes[j : j + 1], cols[j : j + 1]
        key = (col >> 7) * depth + rows[j : j + 1]
        tables.append(pick(keys, key, rounded(size * (1.0 - fy)), rounded(size * fy)).astype(bf16))
        lanes.append(pick(lane, col & 127, rounded(1.0 - fx), rounded(fx)).astype(bf16))
    total = last_dims(jnp.concatenate(tables, 1), jnp.concatenate(lanes, 1))
    for copy in copies[4:]:
        copy.wait()
    first_lane = iota((height, LANES), 1) == 0
    for t in range(tiles):
        own = total[(t + 1) * height : (t + 2) * height, :LANES]
        spill = total[t * height : (t + 1) * height, LANES : LANES + 1]
        own = own + jnp.where(first_lane, spill, 0.0)
        cut = slice(t * LANES, (t + 1) * LANES)
        out_ref[:height, cut] = stored(density_codes(own))
        share = (row_blocks_ref[t * LANES : (t + 1) * LANES, :] - block_low) * (1.0 / block_span)
        out_ref[2 * height :, cut] = stored(coded(share))
    weights = cap_ref[...].astype(f32) * (1.0 - block_ref[...])
    code = coded((weights - weight_low) * (1.0 / weight_span))
    row = iota((height, weights.shape[1]), 0)
    mine = row // depth == lax.axis_index("cells")
    out_ref[height : 2 * height, :] = stored(jnp.where(mine, jnp.concatenate([code] * parts, 0), 0.0))


def sum_kernel(*refs):
    sent_refs, out_ref = refs[:-1], refs[-1]
    height = sent_refs[0].shape[0] // 2
    terms, codes = 0.0, 0.0
    for sent_ref in sent_refs:
        terms += densities(sent_ref[:height, :])
        codes += sent_ref[height:, :].astype(f32)
    if out_ref.shape[0] == height:
        out_ref[...] = stored(jnp.where(lax.axis_index("cells") % 2 == 0, density_codes(terms), codes))
    else:
        out_ref[:height, :] = stored(density_codes(terms))
        out_ref[height:, :] = stored(codes)


def beside(values):
    width = values.shape[1]
    lane = iota((values.shape[0], LANES), 1)
    left, right = pltpu.roll(values, 1, 1), pltpu.roll(values, width - 1, 1)
    first = jnp.where(lane == 0, values[:, :LANES], left[:, :LANES])
    last = jnp.where(lane == LANES - 1, values[:, width - LANES :], right[:, width - LANES :])
    return (
        jnp.concatenate([first, left[:, LANES:]], 1),
        jnp.concatenate([right[:, : width - LANES], last], 1),
    )


class Turned:
    def __init__(self, tiles):
        self.tiles, self.turned = tiles, {}

    def turn(self, t, shift):
        if (t, shift) not in self.turned:
            self.turned[t, shift] = pltpu.roll(self.tiles[t], shift, 1)
        return self.turned[t, shift]

    def along(self, t):
        mine, back = self.tiles[t], LANES - 1
        lane = iota(mine.shape, 1)
        before = self.turn(t - 1, 1) if t else mine
        after = self.turn(t + 1, back) if t + 1 < len(self.tiles) else mine
        left = jnp.where(lane == 0, before, self.turn(t, 1))
        right = jnp.where(lane == back, after, self.turn(t, back))
        return 2.0 * mine - left - right


def delayed(count, first, second, delay=2):
    waiting, results = [], []
    for t in range(count + delay):
        if t < count:
            waiting.append(first(t))
        if t >= delay:
            results.append(second(t - delay, waiting[t - delay]))
            waiting[t - delay] = None
    return results


def across_lines(values):
    height = values.shape[0]
    row = iota((8, values.shape[1]), 0)
    above, below = pltpu.roll(values, 1, 0), pltpu.roll(values, height - 1, 0)
    first = jnp.where(row == 0, values[:8], above[:8])
    last = jnp.where(row == 7, values[height - 8 :], below[height - 8 :])
    above = jnp.concatenate([first, above[8:]], 0)
    below = jnp.concatenate([below[: height - 8], last], 0)
    return 2.0 * values - above - below


def col_products(residual, blocks):
    high, low = halves(residual)
    size = blocks[0].shape[0] // 2
    dot = functools.partial(jnp.dot, preferred_element_type=f32)
    cuts = [slice(k * size, (k + 1) * size) for k in range(len(blocks))]
    return [(dot(pair, high[cut]), dot(pair[:size], low[cut])) for pair, cut in zip(blocks, cuts)]


def col_sum(products):
    size = products[0][1].shape[0]
    result = [both[:size] + (both[size:] + rest) for both, rest in products]
    return result[0] if len(result) == 1 else jnp.concatenate(result, 0)


def each(count, body):
    if count == 1:
        body(0)
    else:
        pl.loop(0, count)(body)


def join_kernel(*refs):
    for n, ref in enumerate(refs[:-1]):
        refs[-1][n * ref.shape[0] : (n + 1) * ref.shape[0], :] = ref[...]


def unpack_kernel(tiles, carried, codes_ref, pairs_ref):
    for k in range(pairs_ref.shape[0]):
        base = (k // tiles) * (carried + LANES) + carried
        code = codes_ref[base : base + LANES, k % tiles * LANES : (k % tiles + 1) * LANES].astype(f32)
        high, low = halves((code + code_half) * (block_span / code_top) + block_low)
        pairs_ref[k, :LANES, :] = high
        pairs_ref[k, LANES:, :] = low


def field_kernel(
    sizes, pairs, col_blocks_ref, rows_ref, cols_ref, fracs_ref, *refs,
):
    depth, tiles, parts, strips = sizes
    sent_refs, (final_ref, velocity_ref, weights_ref, source_ref, field_ref, ordered) = refs[:-6], refs[-6:]
    width_part = tiles * LANES
    width = parts * width_part
    height = strips * depth
    chunk = min(GROUP, strips) * depth
    chunks = height // chunk
    strip, part = lax.axis_index("strip"), lax.axis_index("cells")

    slots = parts * depth
    if len(sent_refs) == 1:
        sent = sent_refs[0]

        def half_of(n, side):
            return sent[n][side * slots : (side + 1) * slots]

    else:
        for other, sent_ref in enumerate(sent_refs):
            for n in range(strips):
                near, far = n // (strips // 2), n % (strips // 2)
                got = sent_ref[n * slots : (n + 1) * slots, :]
                ordered[strip ^ (2 * far + near), (part + other) % 2] = got

        def half_of(n, side):
            return ordered[n, side]

    group = chunk // depth
    target, origin = iota((parts * chunk, group * slots), 0), iota((parts * chunk, group * slots), 1)
    slot = origin % slots
    fits = (slot // depth == target // chunk) & (origin // slots * depth + slot % depth == target % chunk)
    chosen = jnp.where(fits, 1.0, 0.0).astype(bf16)

    def placed(values):
        high, low = halves(jnp.concatenate(values, 0))
        dot = functools.partial(jnp.dot, preferred_element_type=f32)
        return dot(chosen, high) + dot(chosen, low)

    @functools.partial(each, chunks)
    def place(g):
        terms, codes = [], []
        for n in range(group):
            terms.append(densities(half_of(g * group + n, 0)))
            codes.append(half_of(g * group + n, 1).astype(f32))
        term = placed(terms)
        weight = (placed(codes) + code_half) * (weight_span / code_top) + weight_low
        here = pl.ds(pl.multiple_of(g * chunk, chunk), chunk)
        for p in range(parts):
            cut = slice(p * width_part, (p + 1) * width_part)
            weights_ref[here, cut] = weight[p * chunk : (p + 1) * chunk]
            source_ref[here, cut] = term[p * chunk : (p + 1) * chunk] / weight[p * chunk : (p + 1) * chunk]

    col_blocks = [jnp.concatenate(halves(col_blocks_ref[k]), 0) for k in range(col_blocks_ref.shape[0])]
    inner = pl.ds(8, height)
    lanes_at_once = 2 * LANES if chunks == 1 and width % (2 * LANES) == 0 else LANES
    at_once = width // lanes_at_once if chunks == 1 else 1

    def cuts_of(g):
        if at_once > 1:
            return [slice(n * lanes_at_once, (n + 1) * lanes_at_once) for n in range(at_once)]
        return [pl.ds(pl.multiple_of(g * lanes_at_once, lanes_at_once), lanes_at_once)]

    col_steps = width // lanes_at_once // at_once

    @functools.partial(each, col_steps)
    def start(g):
        for cut in cuts_of(g):
            current = source_ref[:, cut]
            field_ref[inner, cut] = current
            source_ref[:, cut] = weights_ref[:, cut] * current - coupling * across_lines(current)

    row_tiles = [slice(t * LANES, (t + 1) * LANES) for t in range(width // LANES)]
    for step in range(STEPS):

        @functools.partial(each, chunks)
        def solve_rows(g):
            here = pl.ds(pl.multiple_of(g * chunk, chunk), chunk)
            there = pl.ds(pl.multiple_of(g * chunk + 8, 8), chunk)
            current = [field_ref[there, cut] for cut in row_tiles]
            for sweep in range(SWEEPS):
                turned = Turned(current)

                def multiply(t):
                    cut = row_tiles[t]
                    now = weights_ref[here, cut] * turned.tiles[t] + coupling * turned.along(t)
                    return last_dims(jnp.concatenate(halves(source_ref[here, cut] - now), 0), pairs[t])

                def add(t, product):
                    high, low = product[:chunk], product[chunk:]
                    return turned.tiles[t] + (high[:, :LANES] + (high[:, LANES:] + low[:, :LANES]))

                current = delayed(len(current), multiply, add)
            turned = Turned(current)
            for t, cut in enumerate(row_tiles):
                field_ref[there, cut] = current[t]
                source_ref[here, cut] = weights_ref[here, cut] * current[t] - coupling * turned.along(t)

        @functools.partial(each, col_steps)
        def solve_cols(g):
            cuts = cuts_of(g)
            current = [field_ref[inner, cut] for cut in cuts]
            for sweep in range(SWEEPS):
                before = current

                def multiply(n):
                    now = weights_ref[:, cuts[n]] * before[n] + coupling * across_lines(before[n])
                    return col_products(source_ref[:, cuts[n]] - now, col_blocks)

                current = delayed(len(cuts), multiply, lambda n, products: before[n] + col_sum(products))
            for now, cut in zip(current, cuts):
                field_ref[inner, cut] = now
                if step + 1 < STEPS:
                    source_ref[:, cut] = weights_ref[:, cut] * now - coupling * across_lines(now)
                else:
                    field_ref[:8, cut] = jnp.broadcast_to(now[:1], (8, lanes_at_once))
                    field_ref[height + 8 :, cut] = jnp.broadcast_to(now[-1:], (8, lanes_at_once))

    row0 = strip * depth
    columns = pl.ds(pl.multiple_of(part * width_part, LANES), width_part)
    base, shift = pl.multiple_of(row0 // 8 * 8, 8), 17 - row0 % 8
    final_ref[...] = pltpu.roll(field_ref[pl.ds(base, 24), columns], shift, 0)[1 : 1 + depth]

    window = pltpu.roll(field_ref[pl.ds(base, 24), :], shift, 0)
    above, centre, below = window[:8], pltpu.roll(window, 23, 0)[:8], pltpu.roll(window, 22, 0)[:8]
    left, right = beside(centre)
    scale = jnp.maximum(centre, floor_level)
    velocity_y = rounded(-(0.5 * (below - above)) / scale)
    velocity_x = rounded(-(0.5 * (right - left)) / scale)

    upper = iota((8, LANES), 0) < depth

    def stacked(values):
        stack = []
        for t in range(0, parts * tiles, 2):
            even = values[:, t * LANES : (t + 1) * LANES]
            odd = values[:, (t + 1) * LANES : (t + 2) * LANES]
            stack.append(jnp.where(upper, even, pltpu.roll(odd, depth, 0)))
        return jnp.concatenate(stack, 0)

    half = LANES // 2

    def table_of(values):
        stack = stacked(values)
        many = stack.shape[0]
        blank = jnp.zeros((LANES - many, LANES), f32)
        turned = jnp.concatenate([stack, blank], 0).T
        after = jnp.concatenate([pltpu.roll(stack, many - depth, 0), blank], 0).T[:8]
        return jnp.concatenate([turned[: half + 8], jnp.concatenate([turned[half:], after], 0)], 1)

    table = jnp.concatenate([table_of(velocity_y), table_of(velocity_x)], 0).astype(bf16)
    many = parts * tiles * depth
    rows, cols = rows_ref[...], cols_ref[...]
    joined = 2 if rows.shape[0] % 2 == 0 else 1
    blank = jnp.zeros((LANES - many, joined * LANES), bf16)
    keys, lane = iota((many, joined * LANES), 0), iota((half + 8, joined * LANES), 0)
    for j in range(0, rows.shape[0], joined):
        cut = slice(j * LANES, (j + joined) * LANES)
        fy, fx = fracs_ref[0:1, cut], fracs_ref[1:2, cut]
        col = jnp.concatenate([cols[n : n + 1] for n in range(j, j + joined)], 1)
        row = jnp.concatenate([rows[n : n + 1] for n in range(j, j + joined)], 1)
        key = (col >> 7) * depth + row
        second = (col & half) != 0
        near, far = rounded(1.0 - fy), rounded(fy)
        looks = [
            pick(keys, jnp.where(second, -8, key), near, far).astype(bf16),
            blank,
            pick(keys, jnp.where(second, key, -8), near, far).astype(bf16),
            blank,
        ]
        sampled = jnp.dot(table, jnp.concatenate(looks, 0), preferred_element_type=f32)
        share = pick(lane, col & (half - 1), rounded(1.0 - fx), rounded(fx))
        velocity_ref[0:1, cut] = jnp.sum(sampled[: half + 8] * share, 0, keepdims=True)
        velocity_ref[1:2, cut] = jnp.sum(sampled[half + 8 :] * share, 0, keepdims=True)


def partner(values, axis, bits):
    return lax.ppermute(values, axis, [(n, n ^ bits) for n in range(lax.axis_size(axis))])


def local(pin_rows, pin_cols, pin_fracs, pin_weights, capacity, blockage, row_blocks, col_blocks):
    depth, width_part = capacity.shape
    parts, strips = lax.axis_size("cells"), lax.axis_size("strip")
    tiles = width_part // LANES
    height, width = depth * strips, width_part * parts
    pins = pin_rows.shape[0]
    by_lane = (pins // LANES, LANES)
    rows, cols = pin_rows.reshape(by_lane), pin_cols.reshape(by_lane)
    sizes = pin_weights.reshape(by_lane)
    vmem = pl.BlockSpec(memory_space=pltpu.VMEM)
    whole = pltpu.CompilerParams(vmem_limit_bytes=60 << 20)
    small = pltpu.CompilerParams(vmem_limit_bytes=16 * 1024 * 1024)
    grid_bytes = 4 * height * width
    large = pltpu.CompilerParams(vmem_limit_bytes=(20 << 20) + 6 * grid_bytes)

    carried = 2 * parts * depth
    read = (rows, cols, pin_fracs, sizes, row_blocks.reshape(-1, LANES), capacity, blockage)
    terms = pl.pallas_call(
        functools.partial(splat_kernel, tiles, parts),
        out_shape=jax.ShapeDtypeStruct((carried + LANES, width_part), jnp.int16),
        in_specs=[pl.BlockSpec(memory_space=pltpu.HBM)] * 7,
        out_specs=vmem,
        scratch_shapes=[pltpu.VMEM(item.shape, item.dtype) for item in read] + [pltpu.SemaphoreType.DMA((7,))],
        compiler_params=whole,
        name="splat",
    )(*read)
    blocks = lax.all_gather(terms, "cells", axis=0, tiled=True)

    def terms_of(part):
        place = part * (carried + LANES) // carried
        return pl.BlockSpec((carried, width_part), lambda i: (place, 0))

    split = strips == 8 and parts % 2 == 0
    handed = carried // 2 if split else carried
    sums = pl.pallas_call(
        sum_kernel,
        grid=(1,),
        out_shape=jax.ShapeDtypeStruct((handed, width_part), jnp.int16),
        in_specs=[terms_of(part) for part in range(parts)],
        out_specs=pl.BlockSpec((handed, width_part), lambda i: (0, 0)),
        compiler_params=small,
        name="sum_terms",
    )(*[blocks] * parts)
    if split:

        def joined(*items):
            return pl.pallas_call(
                join_kernel,
                out_shape=jax.ShapeDtypeStruct((len(items) * items[0].shape[0], width_part), jnp.int16),
                in_specs=[vmem] * len(items),
                out_specs=vmem,
                compiler_params=small,
                name="join",
            )(*items)

        from_z = {k: partner(sums, "strip", k) for k in (6, 4, 2)}
        held = joined(sums, from_z[2], from_z[4], from_z[6])
        held, blocks = lax.optimization_barrier((held, blocks))
        held = joined(held, partner(held, "strip", 1))
        sent = [held, partner(held, "cells", 1)]
    else:
        sent = [lax.all_gather(sums, "strip", axis=0)]
    pairs = pl.pallas_call(
        functools.partial(unpack_kernel, tiles, carried),
        out_shape=jax.ShapeDtypeStruct((width // LANES, 2 * LANES, LANES), bf16),
        in_specs=[vmem],
        out_specs=vmem,
        compiler_params=small,
        cost_estimate=pl.CostEstimate(flops=1 << 20, bytes_accessed=1 << 21, transcendentals=0),
        name="unpack",
    )(blocks)

    final, velocity = pl.pallas_call(
        functools.partial(field_kernel, (depth, tiles, parts, strips)),
        out_shape=(
            jax.ShapeDtypeStruct((depth, width_part), f32),
            jax.ShapeDtypeStruct((2, pins), f32),
        ),
        in_specs=[vmem] * (5 + len(sent)),
        out_specs=(vmem, vmem),
        scratch_shapes=[
            pltpu.VMEM((height, width), f32),
            pltpu.VMEM((height, width), f32),
            pltpu.VMEM((height + 16, width), f32),
            pltpu.VMEM((strips if split else 1, 2, carried // 2, width_part), jnp.int16),
        ],
        compiler_params=large,
        name="field",
    )(pairs, col_blocks, rows, cols, pin_fracs, *sent)
    return final, velocity


def solution(mesh):
    placed = (
        P(("strip", "cells")),
        P(("strip", "cells")),
        P(None, ("strip", "cells")),
        P(("strip", "cells")),
        P("strip", "cells"),
        P("strip", "cells"),
        P("cells", None, None),
        P(),
    )
    return jax.shard_map(
        local,
        mesh=mesh,
        in_specs=placed,
        out_specs=(P("strip", "cells"), P(None, ("strip", "cells"))),
        check_vma=False,
    )
```

```python
import functools

import jax
import jax.numpy as jnp
from jax import lax
from jax.experimental import pallas as pl
from jax.experimental.pallas import tpu as pltpu
from jax.sharding import PartitionSpec as P

SWEEPS = 3
STEPS = 2
LANES = 128
GROUP = 8

coupling = 2.0
floor_level = 0.5
block_low, block_span = -0.002, 0.152
weight_low, weight_span = 0.5, 3.5
term_low, term_octaves = -20.0, 34.0
code_top = 65535.0
code_half = 32768.0
log_two = 0.6931471805599453

f32 = jnp.float32
bf16 = jnp.bfloat16


def iota(shape, axis):
    return lax.broadcasted_iota(jnp.int32, shape, axis)


def halves(values):
    high = values.astype(bf16)
    return high, (values - high.astype(f32)).astype(bf16)


def last_dims(left, right):
    return lax.dot_general(left, right, (((1,), (1,)), ((), ())), preferred_element_type=f32)


def pick(index, first, near, far):
    return jnp.where(index == first, near, jnp.where(index == first + 1, far, 0.0))


def rounded(values):
    return values.astype(bf16).astype(f32)


def coded(share):
    return jnp.clip(jnp.round(share * code_top), 0.0, code_top) - code_half


def stored(codes):
    return codes.astype(jnp.int32).astype(jnp.int16)


def density_codes(values):
    octave = jnp.log(jnp.maximum(values, 2.0**-40)) * (1.0 / log_two)
    return stored(coded((octave - term_low) * (1.0 / term_octaves)))


def densities(codes):
    codes = codes.astype(f32)
    octave = (codes + code_half) * (term_octaves / code_top) + term_low
    return jnp.where(codes == -code_half, 0.0, jnp.exp(octave * log_two))


def splat_kernel(
    tiles, parts, rows_in, cols_in, fracs_in, pin_weights_in, row_blocks_in, cap_in, block_in, out_ref,
    rows_ref, cols_ref, fracs_ref, pin_weights_ref, row_blocks_ref, cap_ref, block_ref, arrived,
):
    depth = cap_ref.shape[0]
    height = parts * depth
    sources = (rows_in, cols_in, fracs_in, pin_weights_in, row_blocks_in, cap_in, block_in)
    places = (rows_ref, cols_ref, fracs_ref, pin_weights_ref, row_blocks_ref, cap_ref, block_ref)
    copies = [
        pltpu.make_async_copy(source, place, arrived.at[n]) for n, (source, place) in enumerate(zip(sources, places))
    ]
    for copy in copies:
        copy.start()
    for copy in copies[:4]:
        copy.wait()
    rows, cols, sizes = rows_ref[...], cols_ref[...], pin_weights_ref[...]
    place = iota((height * (tiles + 1), LANES), 0)
    group, inner = place // height, place % height
    keys = ((inner // depth) * tiles + group - 1) * depth + inner % depth
    lane = iota((LANES + 8, LANES), 0)
    tables, lanes = [], []
    for j in range(rows.shape[0]):
        cut = slice(j * LANES, (j + 1) * LANES)
        fy, fx = fracs_ref[0:1, cut], fracs_ref[1:2, cut]
        size, col = sizes[j : j + 1], cols[j : j + 1]
        key = (col >> 7) * depth + rows[j : j + 1]
        tables.append(pick(keys, key, rounded(size * (1.0 - fy)), rounded(size * fy)).astype(bf16))
        lanes.append(pick(lane, col & 127, rounded(1.0 - fx), rounded(fx)).astype(bf16))
    total = last_dims(jnp.concatenate(tables, 1), jnp.concatenate(lanes, 1))
    for copy in copies[4:]:
        copy.wait()
    first_lane = iota((height, LANES), 1) == 0
    for t in range(tiles):
        own = total[(t + 1) * height : (t + 2) * height, :LANES]
        spill = total[t * height : (t + 1) * height, LANES : LANES + 1]
        own = own + jnp.where(first_lane, spill, 0.0)
        cut = slice(t * LANES, (t + 1) * LANES)
        out_ref[:height, cut] = density_codes(own)
        share = (row_blocks_ref[t * LANES : (t + 1) * LANES, :] - block_low) * (1.0 / block_span)
        out_ref[2 * height :, cut] = stored(coded(share))
    weights = cap_ref[...].astype(f32) * (1.0 - block_ref[...])
    code = coded((weights - weight_low) * (1.0 / weight_span))
    row = iota((height, weights.shape[1]), 0)
    mine = row // depth == lax.axis_index("cells")
    out_ref[height : 2 * height, :] = stored(jnp.where(mine, jnp.concatenate([code] * parts, 0), 0.0))


def sum_kernel(*refs):
    sent_refs, out_ref = refs[:-1], refs[-1]
    height = out_ref.shape[0] // 2
    terms, codes = 0.0, 0.0
    for sent_ref in sent_refs:
        terms += densities(sent_ref[:height, :])
        codes += sent_ref[height:, :].astype(f32)
    out_ref[:height, :] = density_codes(terms)
    out_ref[height:, :] = stored(codes)


def beside(values):
    width = values.shape[1]
    lane = iota((values.shape[0], LANES), 1)
    left, right = pltpu.roll(values, 1, 1), pltpu.roll(values, width - 1, 1)
    first = jnp.where(lane == 0, values[:, :LANES], left[:, :LANES])
    last = jnp.where(lane == LANES - 1, values[:, width - LANES :], right[:, width - LANES :])
    return (
        jnp.concatenate([first, left[:, LANES:]], 1),
        jnp.concatenate([right[:, : width - LANES], last], 1),
    )


class Turned:
    def __init__(self, tiles):
        self.tiles, self.turned = tiles, {}

    def turn(self, t, shift):
        if (t, shift) not in self.turned:
            self.turned[t, shift] = pltpu.roll(self.tiles[t], shift, 1)
        return self.turned[t, shift]

    def along(self, t):
        mine, back = self.tiles[t], LANES - 1
        lane = iota(mine.shape, 1)
        before = self.turn(t - 1, 1) if t else mine
        after = self.turn(t + 1, back) if t + 1 < len(self.tiles) else mine
        left = jnp.where(lane == 0, before, self.turn(t, 1))
        right = jnp.where(lane == back, after, self.turn(t, back))
        return 2.0 * mine - left - right


def delayed(count, first, second, delay=2):
    waiting, results = [], []
    for t in range(count + delay):
        if t < count:
            waiting.append(first(t))
        if t >= delay:
            results.append(second(t - delay, waiting[t - delay]))
            waiting[t - delay] = None
    return results


def across_lines(values):
    height = values.shape[0]
    row = iota((8, values.shape[1]), 0)
    above, below = pltpu.roll(values, 1, 0), pltpu.roll(values, height - 1, 0)
    first = jnp.where(row == 0, values[:8], above[:8])
    last = jnp.where(row == 7, values[height - 8 :], below[height - 8 :])
    above = jnp.concatenate([first, above[8:]], 0)
    below = jnp.concatenate([below[: height - 8], last], 0)
    return 2.0 * values - above - below


def col_products(residual, blocks):
    high, low = halves(residual)
    size = blocks[0].shape[0] // 2
    dot = functools.partial(jnp.dot, preferred_element_type=f32)
    cuts = [slice(k * size, (k + 1) * size) for k in range(len(blocks))]
    return [(dot(pair, high[cut]), dot(pair[:size], low[cut])) for pair, cut in zip(blocks, cuts)]


def col_sum(products):
    size = products[0][1].shape[0]
    result = [both[:size] + (both[size:] + rest) for both, rest in products]
    return result[0] if len(result) == 1 else jnp.concatenate(result, 0)


def each(count, body):
    if count == 1:
        body(0)
    else:
        pl.loop(0, count)(body)


def join_kernel(*refs):
    for n, ref in enumerate(refs[:-1]):
        refs[-1][n * ref.shape[0] : (n + 1) * ref.shape[0], :] = ref[...]


def unpack_kernel(tiles, carried, codes_ref, pairs_ref):
    for k in range(pairs_ref.shape[0]):
        base = (k // tiles) * (carried + LANES) + carried
        code = codes_ref[base : base + LANES, k % tiles * LANES : (k % tiles + 1) * LANES].astype(f32)
        high, low = halves(((code + code_half) * (block_span / code_top) + block_low).T)
        pairs_ref[k, :, :LANES] = high
        pairs_ref[k, :, LANES:] = low


def field_kernel(
    sizes, orders, pairs, col_blocks_ref, rows_ref, cols_ref, fracs_ref, *refs,
):
    depth, tiles, parts, strips = sizes
    sent_refs, (final_ref, velocity_ref, weights_ref, source_ref, field_ref, ordered) = refs[:-6], refs[-6:]
    width_part = tiles * LANES
    width = parts * width_part
    height = strips * depth
    chunk = min(GROUP, strips) * depth
    chunks = height // chunk
    strip, part = lax.axis_index("strip"), lax.axis_index("cells")

    slots = parts * depth
    if len(sent_refs) == 1:
        sent = sent_refs[0]
    else:
        sent = ordered
        for order, sent_ref in zip(orders, sent_refs):
            for n, bits in enumerate(order):
                ordered[strip ^ bits] = sent_ref[n * 2 * slots : (n + 1) * 2 * slots, :]
    group = chunk // depth
    target, origin = iota((parts * chunk, group * slots), 0), iota((parts * chunk, group * slots), 1)
    slot = origin % slots
    fits = (slot // depth == target // chunk) & (origin // slots * depth + slot % depth == target % chunk)
    chosen = jnp.where(fits, 1.0, 0.0).astype(bf16)

    def placed(values):
        high, low = halves(jnp.concatenate(values, 0))
        dot = functools.partial(jnp.dot, preferred_element_type=f32)
        return dot(chosen, high) + dot(chosen, low)

    @functools.partial(each, chunks)
    def place(g):
        terms, codes = [], []
        for n in range(group):
            got = sent[g * group + n]
            terms.append(densities(got[:slots]))
            codes.append(got[slots:].astype(f32))
        term = placed(terms)
        weight = (placed(codes) + code_half) * (weight_span / code_top) + weight_low
        here = pl.ds(pl.multiple_of(g * chunk, chunk), chunk)
        for p in range(parts):
            cut = slice(p * width_part, (p + 1) * width_part)
            weights_ref[here, cut] = weight[p * chunk : (p + 1) * chunk]
            source_ref[here, cut] = term[p * chunk : (p + 1) * chunk] / weight[p * chunk : (p + 1) * chunk]

    col_blocks = [jnp.concatenate(halves(col_blocks_ref[k]), 0) for k in range(col_blocks_ref.shape[0])]
    inner = pl.ds(8, height)
    lanes_at_once = 2 * LANES if chunks == 1 and width % (2 * LANES) == 0 else LANES
    at_once = width // lanes_at_once if chunks == 1 else 1

    def cuts_of(g):
        if at_once > 1:
            return [slice(n * lanes_at_once, (n + 1) * lanes_at_once) for n in range(at_once)]
        return [pl.ds(pl.multiple_of(g * lanes_at_once, lanes_at_once), lanes_at_once)]

    col_steps = width // lanes_at_once // at_once

    @functools.partial(each, col_steps)
    def start(g):
        for cut in cuts_of(g):
            current = source_ref[:, cut]
            field_ref[inner, cut] = current
            source_ref[:, cut] = weights_ref[:, cut] * current - coupling * across_lines(current)

    row_tiles = [slice(t * LANES, (t + 1) * LANES) for t in range(width // LANES)]
    for step in range(STEPS):

        @functools.partial(each, chunks)
        def solve_rows(g):
            here = pl.ds(pl.multiple_of(g * chunk, chunk), chunk)
            there = pl.ds(pl.multiple_of(g * chunk + 8, 8), chunk)
            current = [field_ref[there, cut] for cut in row_tiles]
            for sweep in range(SWEEPS):
                turned = Turned(current)

                def multiply(t):
                    cut = row_tiles[t]
                    now = weights_ref[here, cut] * turned.tiles[t] + coupling * turned.along(t)
                    both = jnp.concatenate(halves(source_ref[here, cut] - now), 0)
                    return jnp.dot(both, pairs[t], preferred_element_type=f32)

                def add(t, product):
                    high, low = product[:chunk], product[chunk:]
                    return turned.tiles[t] + (high[:, :LANES] + (high[:, LANES:] + low[:, :LANES]))

                current = delayed(len(current), multiply, add)
            turned = Turned(current)
            for t, cut in enumerate(row_tiles):
                field_ref[there, cut] = current[t]
                source_ref[here, cut] = weights_ref[here, cut] * current[t] - coupling * turned.along(t)

        @functools.partial(each, col_steps)
        def solve_cols(g):
            cuts = cuts_of(g)
            current = [field_ref[inner, cut] for cut in cuts]
            for sweep in range(SWEEPS):
                before = current

                def multiply(n):
                    now = weights_ref[:, cuts[n]] * before[n] + coupling * across_lines(before[n])
                    return col_products(source_ref[:, cuts[n]] - now, col_blocks)

                current = delayed(len(cuts), multiply, lambda n, products: before[n] + col_sum(products))
            for now, cut in zip(current, cuts):
                field_ref[inner, cut] = now
                if step + 1 < STEPS:
                    source_ref[:, cut] = weights_ref[:, cut] * now - coupling * across_lines(now)
                else:
                    field_ref[:8, cut] = jnp.broadcast_to(now[:1], (8, lanes_at_once))
                    field_ref[height + 8 :, cut] = jnp.broadcast_to(now[-1:], (8, lanes_at_once))

    row0 = strip * depth
    columns = pl.ds(pl.multiple_of(part * width_part, LANES), width_part)
    base, shift = pl.multiple_of(row0 // 8 * 8, 8), 17 - row0 % 8
    final_ref[...] = pltpu.roll(field_ref[pl.ds(base, 24), columns], shift, 0)[1 : 1 + depth]

    window = pltpu.roll(field_ref[pl.ds(base, 24), :], shift, 0)
    above, centre, below = window[:8], pltpu.roll(window, 23, 0)[:8], pltpu.roll(window, 22, 0)[:8]
    left, right = beside(centre)
    scale = jnp.maximum(centre, floor_level)
    velocity_y = rounded(-(0.5 * (below - above)) / scale)
    velocity_x = rounded(-(0.5 * (right - left)) / scale)

    upper = iota((8, LANES), 0) < depth

    def stacked(values):
        stack = []
        for t in range(0, parts * tiles, 2):
            even = values[:, t * LANES : (t + 1) * LANES]
            odd = values[:, (t + 1) * LANES : (t + 2) * LANES]
            stack.append(jnp.where(upper, even, pltpu.roll(odd, depth, 0)))
        return jnp.concatenate(stack, 0)

    half = LANES // 2

    def table_of(values):
        stack = stacked(values)
        many = stack.shape[0]
        blank = jnp.zeros((LANES - many, LANES), f32)
        turned = jnp.concatenate([stack, blank], 0).T
        after = jnp.concatenate([pltpu.roll(stack, many - depth, 0), blank], 0).T[:8]
        return jnp.concatenate([turned[: half + 8], jnp.concatenate([turned[half:], after], 0)], 1)

    table = jnp.concatenate([table_of(velocity_y), table_of(velocity_x)], 0).astype(bf16)
    many = parts * tiles * depth
    rows, cols = rows_ref[...], cols_ref[...]
    joined = 2 if rows.shape[0] % 2 == 0 else 1
    blank = jnp.zeros((LANES - many, joined * LANES), bf16)
    keys, lane = iota((many, joined * LANES), 0), iota((half + 8, joined * LANES), 0)
    for j in range(0, rows.shape[0], joined):
        cut = slice(j * LANES, (j + joined) * LANES)
        fy, fx = fracs_ref[0:1, cut], fracs_ref[1:2, cut]
        col = jnp.concatenate([cols[n : n + 1] for n in range(j, j + joined)], 1)
        row = jnp.concatenate([rows[n : n + 1] for n in range(j, j + joined)], 1)
        key = (col >> 7) * depth + row
        second = (col & half) != 0
        near, far = rounded(1.0 - fy), rounded(fy)
        looks = [
            pick(keys, jnp.where(second, -8, key), near, far).astype(bf16),
            blank,
            pick(keys, jnp.where(second, key, -8), near, far).astype(bf16),
            blank,
        ]
        sampled = jnp.dot(table, jnp.concatenate(looks, 0), preferred_element_type=f32)
        share = pick(lane, col & (half - 1), rounded(1.0 - fx), rounded(fx))
        velocity_ref[0:1, cut] = jnp.sum(sampled[: half + 8] * share, 0, keepdims=True)
        velocity_ref[1:2, cut] = jnp.sum(sampled[half + 8 :] * share, 0, keepdims=True)


def partner(values, axis, bits):
    return lax.ppermute(values, axis, [(n, n ^ bits) for n in range(lax.axis_size(axis))])


def local(pin_rows, pin_cols, pin_fracs, pin_weights, capacity, blockage, row_blocks, col_blocks):
    depth, width_part = capacity.shape
    parts, strips = lax.axis_size("cells"), lax.axis_size("strip")
    tiles = width_part // LANES
    height, width = depth * strips, width_part * parts
    pins = pin_rows.shape[0]
    by_lane = (pins // LANES, LANES)
    rows, cols = pin_rows.reshape(by_lane), pin_cols.reshape(by_lane)
    sizes = pin_weights.reshape(by_lane)
    vmem = pl.BlockSpec(memory_space=pltpu.VMEM)
    whole = pltpu.CompilerParams(vmem_limit_bytes=60 << 20)
    small = pltpu.CompilerParams(vmem_limit_bytes=16 * 1024 * 1024)
    grid_bytes = 4 * height * width
    large = pltpu.CompilerParams(vmem_limit_bytes=(20 << 20) + 6 * grid_bytes)

    carried = 2 * parts * depth
    read = (rows, cols, pin_fracs, sizes, row_blocks.reshape(-1, LANES), capacity, blockage)
    terms = pl.pallas_call(
        functools.partial(splat_kernel, tiles, parts),
        out_shape=jax.ShapeDtypeStruct((carried + LANES, width_part), jnp.int16),
        in_specs=[pl.BlockSpec(memory_space=pltpu.HBM)] * 7,
        out_specs=vmem,
        scratch_shapes=[pltpu.VMEM(item.shape, item.dtype) for item in read] + [pltpu.SemaphoreType.DMA((7,))],
        compiler_params=whole,
        name="splat",
    )(*read)
    blocks = lax.all_gather(terms, "cells", axis=0, tiled=True)

    def terms_of(part):
        place = part * (carried + LANES) // carried
        return pl.BlockSpec((carried, width_part), lambda i: (place, 0))

    sums = pl.pallas_call(
        sum_kernel,
        grid=(1,),
        out_shape=jax.ShapeDtypeStruct((carried, width_part), jnp.int16),
        in_specs=[terms_of(part) for part in range(parts)],
        out_specs=pl.BlockSpec((carried, width_part), lambda i: (0, 0)),
        compiler_params=small,
        name="sum_terms",
    )(*[blocks] * parts)
    if strips == 8:
        orders = ((0,), (1,), (6, 4, 2), (7, 5, 3))
        from_z = [partner(sums, "strip", bits) for bits in (6, 4, 2)]
        *from_z, near = lax.optimization_barrier((*from_z, partner(sums, "strip", 1)))
        held = pl.pallas_call(
            join_kernel,
            out_shape=jax.ShapeDtypeStruct((3 * carried, width_part), jnp.int16),
            in_specs=[vmem] * 3,
            out_specs=vmem,
            compiler_params=small,
            name="join",
        )(*from_z)
        held, blocks = lax.optimization_barrier((held, blocks))
        sent = [sums, near, held, partner(held, "strip", 1)]
    else:
        orders, sent = (), [lax.all_gather(sums, "strip", axis=0)]
    pairs = pl.pallas_call(
        functools.partial(unpack_kernel, tiles, carried),
        out_shape=jax.ShapeDtypeStruct((width // LANES, LANES, 2 * LANES), bf16),
        in_specs=[vmem],
        out_specs=vmem,
        compiler_params=small,
        cost_estimate=pl.CostEstimate(flops=1 << 20, bytes_accessed=1 << 21, transcendentals=0),
        name="unpack",
    )(blocks)

    final, velocity = pl.pallas_call(
        functools.partial(field_kernel, (depth, tiles, parts, strips), orders),
        out_shape=(
            jax.ShapeDtypeStruct((depth, width_part), f32),
            jax.ShapeDtypeStruct((2, pins), f32),
        ),
        in_specs=[vmem] * (5 + len(sent)),
        out_specs=(vmem, vmem),
        scratch_shapes=[
            pltpu.VMEM((height, width), f32),
            pltpu.VMEM((height, width), f32),
            pltpu.VMEM((height + 16, width), f32),
            pltpu.VMEM((strips if len(sent) > 1 else 1, carried, width_part), jnp.int16),
        ],
        compiler_params=large,
        name="field",
    )(pairs, col_blocks, rows, cols, pin_fracs, *sent)
    return final, velocity


def solution(mesh):
    placed = (
        P(("strip", "cells")),
        P(("strip", "cells")),
        P(None, ("strip", "cells")),
        P(("strip", "cells")),
        P("strip", "cells"),
        P("strip", "cells"),
        P("cells", None, None),
        P(),
    )
    return jax.shard_map(
        local,
        mesh=mesh,
        in_specs=placed,
        out_specs=(P("strip", "cells"), P(None, ("strip", "cells"))),
        check_vma=False,
    )
```

```python
import functools

import jax
import jax.numpy as jnp
from jax import lax
from jax.experimental import pallas as pl
from jax.experimental.pallas import tpu as pltpu
from jax.sharding import PartitionSpec as P

SWEEPS = 3
STEPS = 2
LANES = 128
GROUP = 8

coupling = 2.0
floor_level = 0.5
block_low, block_span = -0.002, 0.152
weight_low, weight_span = 0.5, 3.5
term_low, term_octaves = -20.0, 34.0
code_top = 65535.0
code_half = 32768.0
log_two = 0.6931471805599453

f32 = jnp.float32
bf16 = jnp.bfloat16


def iota(shape, axis):
    return lax.broadcasted_iota(jnp.int32, shape, axis)


def halves(values):
    high = values.astype(bf16)
    return high, (values - high.astype(f32)).astype(bf16)


def last_dims(left, right):
    return lax.dot_general(left, right, (((1,), (1,)), ((), ())), preferred_element_type=f32)


def pick(index, first, near, far):
    return jnp.where(index == first, near, jnp.where(index == first + 1, far, 0.0))


def rounded(values):
    return values.astype(bf16).astype(f32)


def coded(share):
    return jnp.clip(jnp.round(share * code_top), 0.0, code_top) - code_half


def stored(codes):
    return codes.astype(jnp.int32).astype(jnp.int16)


def density_codes(values):
    octave = jnp.log(jnp.maximum(values, 2.0**-40)) * (1.0 / log_two)
    return stored(coded((octave - term_low) * (1.0 / term_octaves)))


def densities(codes):
    codes = codes.astype(f32)
    octave = (codes + code_half) * (term_octaves / code_top) + term_low
    return jnp.where(codes == -code_half, 0.0, jnp.exp(octave * log_two))


def splat_kernel(
    tiles, parts, rows_in, cols_in, fracs_in, pin_weights_in, row_blocks_in, cap_in, block_in, out_ref,
    rows_ref, cols_ref, fracs_ref, pin_weights_ref, row_blocks_ref, cap_ref, block_ref, arrived,
):
    depth = cap_ref.shape[0]
    height = parts * depth
    sources = (rows_in, cols_in, fracs_in, pin_weights_in, row_blocks_in, cap_in, block_in)
    places = (rows_ref, cols_ref, fracs_ref, pin_weights_ref, row_blocks_ref, cap_ref, block_ref)
    copies = [
        pltpu.make_async_copy(source, place, arrived.at[n]) for n, (source, place) in enumerate(zip(sources, places))
    ]
    for copy in copies:
        copy.start()
    for copy in copies[:4]:
        copy.wait()
    rows, cols, sizes = rows_ref[...], cols_ref[...], pin_weights_ref[...]
    place = iota((height * (tiles + 1), LANES), 0)
    group, inner = place // height, place % height
    keys = ((inner // depth) * tiles + group - 1) * depth + inner % depth
    lane = iota((LANES + 8, LANES), 0)
    tables, lanes = [], []
    for j in range(rows.shape[0]):
        cut = slice(j * LANES, (j + 1) * LANES)
        fy, fx = fracs_ref[0:1, cut], fracs_ref[1:2, cut]
        size, col = sizes[j : j + 1], cols[j : j + 1]
        key = (col >> 7) * depth + rows[j : j + 1]
        tables.append(pick(keys, key, rounded(size * (1.0 - fy)), rounded(size * fy)).astype(bf16))
        lanes.append(pick(lane, col & 127, rounded(1.0 - fx), rounded(fx)).astype(bf16))
    total = last_dims(jnp.concatenate(tables, 1), jnp.concatenate(lanes, 1))
    for copy in copies[4:]:
        copy.wait()
    first_lane = iota((height, LANES), 1) == 0
    for t in range(tiles):
        own = total[(t + 1) * height : (t + 2) * height, :LANES]
        spill = total[t * height : (t + 1) * height, LANES : LANES + 1]
        own = own + jnp.where(first_lane, spill, 0.0)
        cut = slice(t * LANES, (t + 1) * LANES)
        out_ref[:height, cut] = density_codes(own)
        share = (row_blocks_ref[t * LANES : (t + 1) * LANES, :] - block_low) * (1.0 / block_span)
        out_ref[2 * height :, cut] = stored(coded(share))
    weights = cap_ref[...].astype(f32) * (1.0 - block_ref[...])
    code = coded((weights - weight_low) * (1.0 / weight_span))
    row = iota((height, weights.shape[1]), 0)
    mine = row // depth == lax.axis_index("cells")
    out_ref[height : 2 * height, :] = stored(jnp.where(mine, jnp.concatenate([code] * parts, 0), 0.0))


def sum_kernel(*refs):
    sent_refs, out_ref = refs[:-1], refs[-1]
    height = out_ref.shape[0] // 2
    terms, codes = 0.0, 0.0
    for sent_ref in sent_refs:
        terms += densities(sent_ref[:height, :])
        codes += sent_ref[height:, :].astype(f32)
    out_ref[:height, :] = density_codes(terms)
    out_ref[height:, :] = stored(codes)


def beside(values):
    width = values.shape[1]
    lane = iota((values.shape[0], LANES), 1)
    left, right = pltpu.roll(values, 1, 1), pltpu.roll(values, width - 1, 1)
    first = jnp.where(lane == 0, values[:, :LANES], left[:, :LANES])
    last = jnp.where(lane == LANES - 1, values[:, width - LANES :], right[:, width - LANES :])
    return (
        jnp.concatenate([first, left[:, LANES:]], 1),
        jnp.concatenate([right[:, : width - LANES], last], 1),
    )


class Turned:
    def __init__(self, tiles):
        self.tiles, self.turned = tiles, {}

    def turn(self, t, shift):
        if (t, shift) not in self.turned:
            self.turned[t, shift] = pltpu.roll(self.tiles[t], shift, 1)
        return self.turned[t, shift]

    def along(self, t):
        mine, back = self.tiles[t], LANES - 1
        lane = iota(mine.shape, 1)
        before = self.turn(t - 1, 1) if t else mine
        after = self.turn(t + 1, back) if t + 1 < len(self.tiles) else mine
        left = jnp.where(lane == 0, before, self.turn(t, 1))
        right = jnp.where(lane == back, after, self.turn(t, back))
        return 2.0 * mine - left - right


def delayed(count, first, second, delay=2):
    waiting, results = [], []
    for t in range(count + delay):
        if t < count:
            waiting.append(first(t))
        if t >= delay:
            results.append(second(t - delay, waiting[t - delay]))
            waiting[t - delay] = None
    return results


def across_lines(values):
    height = values.shape[0]
    row = iota((8, values.shape[1]), 0)
    above, below = pltpu.roll(values, 1, 0), pltpu.roll(values, height - 1, 0)
    first = jnp.where(row == 0, values[:8], above[:8])
    last = jnp.where(row == 7, values[height - 8 :], below[height - 8 :])
    above = jnp.concatenate([first, above[8:]], 0)
    below = jnp.concatenate([below[: height - 8], last], 0)
    return 2.0 * values - above - below


def col_products(residual, blocks):
    high, low = halves(residual)
    size = blocks[0].shape[0] // 2
    dot = functools.partial(jnp.dot, preferred_element_type=f32)
    cuts = [slice(k * size, (k + 1) * size) for k in range(len(blocks))]
    return [(dot(pair, high[cut]), dot(pair[:size], low[cut])) for pair, cut in zip(blocks, cuts)]


def col_sum(products):
    size = products[0][1].shape[0]
    result = [both[:size] + (both[size:] + rest) for both, rest in products]
    return result[0] if len(result) == 1 else jnp.concatenate(result, 0)


def each(count, body):
    if count == 1:
        body(0)
    else:
        pl.loop(0, count)(body)


def join_kernel(*refs):
    for n, ref in enumerate(refs[:-1]):
        refs[-1][n * ref.shape[0] : (n + 1) * ref.shape[0], :] = ref[...]


def tables_kernel(sizes, codes_ref, rows_ref, cols_ref, fracs_ref, pairs_ref, look_ref, share_ref):
    depth, tiles, parts, carried = sizes
    for k in range(pairs_ref.shape[0]):
        base = (k // tiles) * (carried + LANES) + carried
        code = codes_ref[base : base + LANES, k % tiles * LANES : (k % tiles + 1) * LANES].astype(f32)
        high, low = halves(((code + code_half) * (block_span / code_top) + block_low).T)
        pairs_ref[k, :, :LANES] = high
        pairs_ref[k, :, LANES:] = low
    half = LANES // 2
    many = parts * tiles * depth
    rows, cols = rows_ref[...], cols_ref[...]
    blank = jnp.zeros((LANES - many, LANES), bf16)
    keys, lane = iota((many, LANES), 0), iota((half + 8, LANES), 0)
    for j in range(rows.shape[0]):
        cut = slice(j * LANES, (j + 1) * LANES)
        fy, fx = fracs_ref[0:1, cut], fracs_ref[1:2, cut]
        col = cols[j : j + 1]
        key = (col >> 7) * depth + rows[j : j + 1]
        second = (col & half) != 0
        near, far = rounded(1.0 - fy), rounded(fy)
        looks = [
            pick(keys, jnp.where(second, -8, key), near, far).astype(bf16),
            blank,
            pick(keys, jnp.where(second, key, -8), near, far).astype(bf16),
            blank,
        ]
        look_ref[:, cut] = jnp.concatenate(looks, 0)
        share_ref[:, cut] = pick(lane, col & (half - 1), rounded(1.0 - fx), rounded(fx))


def field_kernel(
    sizes, orders, pairs, look_ref, share_ref, col_blocks_ref, *refs,
):
    depth, tiles, parts, strips = sizes
    sent_refs, (final_ref, velocity_ref, weights_ref, source_ref, field_ref, ordered) = refs[:-6], refs[-6:]
    width_part = tiles * LANES
    width = parts * width_part
    height = strips * depth
    chunk = min(GROUP, strips) * depth
    chunks = height // chunk
    strip, part = lax.axis_index("strip"), lax.axis_index("cells")

    slots = parts * depth
    if len(sent_refs) == 1:
        sent = sent_refs[0]
    else:
        sent = ordered
        for order, sent_ref in zip(orders, sent_refs):
            for n, bits in enumerate(order):
                ordered[strip ^ bits] = sent_ref[n * 2 * slots : (n + 1) * 2 * slots, :]
    group = chunk // depth
    target, origin = iota((parts * chunk, group * slots), 0), iota((parts * chunk, group * slots), 1)
    slot = origin % slots
    fits = (slot // depth == target // chunk) & (origin // slots * depth + slot % depth == target % chunk)
    chosen = jnp.where(fits, 1.0, 0.0).astype(bf16)

    def placed(values):
        high, low = halves(jnp.concatenate(values, 0))
        dot = functools.partial(jnp.dot, preferred_element_type=f32)
        return dot(chosen, high) + dot(chosen, low)

    @functools.partial(each, chunks)
    def place(g):
        terms, codes = [], []
        for n in range(group):
            got = sent[g * group + n]
            terms.append(densities(got[:slots]))
            codes.append(got[slots:].astype(f32))
        term = placed(terms)
        weight = (placed(codes) + code_half) * (weight_span / code_top) + weight_low
        here = pl.ds(pl.multiple_of(g * chunk, chunk), chunk)
        for p in range(parts):
            cut = slice(p * width_part, (p + 1) * width_part)
            weights_ref[here, cut] = weight[p * chunk : (p + 1) * chunk]
            source_ref[here, cut] = term[p * chunk : (p + 1) * chunk] / weight[p * chunk : (p + 1) * chunk]

    col_blocks = [jnp.concatenate(halves(col_blocks_ref[k]), 0) for k in range(col_blocks_ref.shape[0])]
    inner = pl.ds(8, height)
    lanes_at_once = 2 * LANES if chunks == 1 and width % (2 * LANES) == 0 else LANES
    at_once = width // lanes_at_once if chunks == 1 else 1

    def cuts_of(g):
        if at_once > 1:
            return [slice(n * lanes_at_once, (n + 1) * lanes_at_once) for n in range(at_once)]
        return [pl.ds(pl.multiple_of(g * lanes_at_once, lanes_at_once), lanes_at_once)]

    col_steps = width // lanes_at_once // at_once

    @functools.partial(each, col_steps)
    def start(g):
        for cut in cuts_of(g):
            current = source_ref[:, cut]
            field_ref[inner, cut] = current
            source_ref[:, cut] = weights_ref[:, cut] * current - coupling * across_lines(current)

    row_tiles = [slice(t * LANES, (t + 1) * LANES) for t in range(width // LANES)]
    for step in range(STEPS):

        @functools.partial(each, chunks)
        def solve_rows(g):
            here = pl.ds(pl.multiple_of(g * chunk, chunk), chunk)
            there = pl.ds(pl.multiple_of(g * chunk + 8, 8), chunk)
            current = [field_ref[there, cut] for cut in row_tiles]
            for sweep in range(SWEEPS):
                turned = Turned(current)

                def multiply(t):
                    cut = row_tiles[t]
                    now = weights_ref[here, cut] * turned.tiles[t] + coupling * turned.along(t)
                    both = jnp.concatenate(halves(source_ref[here, cut] - now), 0)
                    return jnp.dot(both, pairs[t], preferred_element_type=f32)

                def add(t, product):
                    high, low = product[:chunk], product[chunk:]
                    return turned.tiles[t] + (high[:, :LANES] + (high[:, LANES:] + low[:, :LANES]))

                current = delayed(len(current), multiply, add)
            turned = Turned(current)
            for t, cut in enumerate(row_tiles):
                field_ref[there, cut] = current[t]
                source_ref[here, cut] = weights_ref[here, cut] * current[t] - coupling * turned.along(t)

        @functools.partial(each, col_steps)
        def solve_cols(g):
            cuts = cuts_of(g)
            current = [field_ref[inner, cut] for cut in cuts]
            for sweep in range(SWEEPS):
                before = current

                def multiply(n):
                    now = weights_ref[:, cuts[n]] * before[n] + coupling * across_lines(before[n])
                    return col_products(source_ref[:, cuts[n]] - now, col_blocks)

                current = delayed(len(cuts), multiply, lambda n, products: before[n] + col_sum(products))
            for now, cut in zip(current, cuts):
                field_ref[inner, cut] = now
                if step + 1 < STEPS:
                    source_ref[:, cut] = weights_ref[:, cut] * now - coupling * across_lines(now)
                else:
                    field_ref[:8, cut] = jnp.broadcast_to(now[:1], (8, lanes_at_once))
                    field_ref[height + 8 :, cut] = jnp.broadcast_to(now[-1:], (8, lanes_at_once))

    row0 = strip * depth
    columns = pl.ds(pl.multiple_of(part * width_part, LANES), width_part)
    base, shift = pl.multiple_of(row0 // 8 * 8, 8), 17 - row0 % 8
    final_ref[...] = pltpu.roll(field_ref[pl.ds(base, 24), columns], shift, 0)[1 : 1 + depth]

    window = pltpu.roll(field_ref[pl.ds(base, 24), :], shift, 0)
    above, centre, below = window[:8], pltpu.roll(window, 23, 0)[:8], pltpu.roll(window, 22, 0)[:8]
    left, right = beside(centre)
    scale = jnp.maximum(centre, floor_level)
    velocity_y = rounded(-(0.5 * (below - above)) / scale)
    velocity_x = rounded(-(0.5 * (right - left)) / scale)

    upper = iota((8, LANES), 0) < depth

    def stacked(values):
        stack = []
        for t in range(0, parts * tiles, 2):
            even = values[:, t * LANES : (t + 1) * LANES]
            odd = values[:, (t + 1) * LANES : (t + 2) * LANES]
            stack.append(jnp.where(upper, even, pltpu.roll(odd, depth, 0)))
        return jnp.concatenate(stack, 0)

    half = LANES // 2

    def table_of(values):
        stack = stacked(values)
        many = stack.shape[0]
        blank = jnp.zeros((LANES - many, LANES), f32)
        turned = jnp.concatenate([stack, blank], 0).T
        after = jnp.concatenate([pltpu.roll(stack, many - depth, 0), blank], 0).T[:8]
        return jnp.concatenate([turned[: half + 8], jnp.concatenate([turned[half:], after], 0)], 1)

    table = jnp.concatenate([table_of(velocity_y), table_of(velocity_x)], 0).astype(bf16)
    pins = share_ref.shape[1]
    at_once = 2 * LANES if pins % (2 * LANES) == 0 else LANES
    for j in range(0, pins, at_once):
        cut = slice(j, j + at_once)
        sampled = jnp.dot(table, look_ref[:, cut], preferred_element_type=f32)
        share = share_ref[:, cut]
        velocity_ref[0:1, cut] = jnp.sum(sampled[: half + 8] * share, 0, keepdims=True)
        velocity_ref[1:2, cut] = jnp.sum(sampled[half + 8 :] * share, 0, keepdims=True)


def partner(values, axis, bits):
    return lax.ppermute(values, axis, [(n, n ^ bits) for n in range(lax.axis_size(axis))])


def local(pin_rows, pin_cols, pin_fracs, pin_weights, capacity, blockage, row_blocks, col_blocks):
    depth, width_part = capacity.shape
    parts, strips = lax.axis_size("cells"), lax.axis_size("strip")
    tiles = width_part // LANES
    height, width = depth * strips, width_part * parts
    pins = pin_rows.shape[0]
    by_lane = (pins // LANES, LANES)
    rows, cols = pin_rows.reshape(by_lane), pin_cols.reshape(by_lane)
    sizes = pin_weights.reshape(by_lane)
    vmem = pl.BlockSpec(memory_space=pltpu.VMEM)
    whole = pltpu.CompilerParams(vmem_limit_bytes=60 << 20)
    small = pltpu.CompilerParams(vmem_limit_bytes=16 * 1024 * 1024)
    grid_bytes = 4 * height * width
    large = pltpu.CompilerParams(vmem_limit_bytes=(20 << 20) + 6 * grid_bytes)

    carried = 2 * parts * depth
    read = (rows, cols, pin_fracs, sizes, row_blocks.reshape(-1, LANES), capacity, blockage)
    terms = pl.pallas_call(
        functools.partial(splat_kernel, tiles, parts),
        out_shape=jax.ShapeDtypeStruct((carried + LANES, width_part), jnp.int16),
        in_specs=[pl.BlockSpec(memory_space=pltpu.HBM)] * 7,
        out_specs=vmem,
        scratch_shapes=[pltpu.VMEM(item.shape, item.dtype) for item in read] + [pltpu.SemaphoreType.DMA((7,))],
        compiler_params=whole,
        name="splat",
    )(*read)
    blocks = lax.all_gather(terms, "cells", axis=0, tiled=True)

    def terms_of(part):
        place = part * (carried + LANES) // carried
        return pl.BlockSpec((carried, width_part), lambda i: (place, 0))

    sums = pl.pallas_call(
        sum_kernel,
        grid=(1,),
        out_shape=jax.ShapeDtypeStruct((carried, width_part), jnp.int16),
        in_specs=[terms_of(part) for part in range(parts)],
        out_specs=pl.BlockSpec((carried, width_part), lambda i: (0, 0)),
        compiler_params=small,
        name="sum_terms",
    )(*[blocks] * parts)
    if strips == 8:
        orders = ((0,), (1,), (6, 4, 2), (7, 5, 3))
        from_z = [partner(sums, "strip", bits) for bits in (6, 4, 2)]
        *from_z, near = lax.optimization_barrier((*from_z, partner(sums, "strip", 1)))
        held = pl.pallas_call(
            join_kernel,
            out_shape=jax.ShapeDtypeStruct((3 * carried, width_part), jnp.int16),
            in_specs=[vmem] * 3,
            out_specs=vmem,
            compiler_params=small,
            name="join",
        )(*from_z)
        held, blocks = lax.optimization_barrier((held, blocks))
        sent = [sums, near, held, partner(held, "strip", 1)]
    else:
        orders, sent = (), [lax.all_gather(sums, "strip", axis=0)]
    pairs, look, share = pl.pallas_call(
        functools.partial(tables_kernel, (depth, tiles, parts, carried)),
        out_shape=(
            jax.ShapeDtypeStruct((width // LANES, LANES, 2 * LANES), bf16),
            jax.ShapeDtypeStruct((2 * LANES, pins), bf16),
            jax.ShapeDtypeStruct((LANES // 2 + 8, pins), f32),
        ),
        in_specs=[vmem] * 4,
        out_specs=(vmem,) * 3,
        compiler_params=small,
        cost_estimate=pl.CostEstimate(flops=1 << 20, bytes_accessed=1 << 21, transcendentals=0),
        name="tables",
    )(blocks, rows, cols, pin_fracs)

    final, velocity = pl.pallas_call(
        functools.partial(field_kernel, (depth, tiles, parts, strips), orders),
        out_shape=(
            jax.ShapeDtypeStruct((depth, width_part), f32),
            jax.ShapeDtypeStruct((2, pins), f32),
        ),
        in_specs=[vmem] * (4 + len(sent)),
        out_specs=(vmem, vmem),
        scratch_shapes=[
            pltpu.VMEM((height, width), f32),
            pltpu.VMEM((height, width), f32),
            pltpu.VMEM((height + 16, width), f32),
            pltpu.VMEM((strips if len(sent) > 1 else 1, carried, width_part), jnp.int16),
        ],
        compiler_params=large,
        name="field",
    )(pairs, look, share, col_blocks, *sent)
    return final, velocity


def solution(mesh):
    placed = (
        P(("strip", "cells")),
        P(("strip", "cells")),
        P(None, ("strip", "cells")),
        P(("strip", "cells")),
        P("strip", "cells"),
        P("strip", "cells"),
        P("cells", None, None),
        P(),
    )
    return jax.shard_map(
        local,
        mesh=mesh,
        in_specs=placed,
        out_specs=(P("strip", "cells"), P(None, ("strip", "cells"))),
        check_vma=False,
    )
```

```python
import functools

import jax
import jax.numpy as jnp
from jax import lax
from jax.experimental import pallas as pl
from jax.experimental.pallas import tpu as pltpu
from jax.sharding import PartitionSpec as P

SWEEPS = 3
STEPS = 2
LANES = 128
GROUP = 8

coupling = 2.0
floor_level = 0.5
block_low, block_span = -0.002, 0.152
weight_low, weight_span = 0.5, 3.5
term_low, term_octaves = -20.0, 34.0
code_top = 65535.0
code_half = 32768.0
log_two = 0.6931471805599453

f32 = jnp.float32
bf16 = jnp.bfloat16


def iota(shape, axis):
    return lax.broadcasted_iota(jnp.int32, shape, axis)


def halves(values):
    high = values.astype(bf16)
    return high, (values - high.astype(f32)).astype(bf16)


def last_dims(left, right):
    return lax.dot_general(left, right, (((1,), (1,)), ((), ())), preferred_element_type=f32)


def pick(index, first, near, far):
    return jnp.where(index == first, near, jnp.where(index == first + 1, far, 0.0))


def rounded(values):
    return values.astype(bf16).astype(f32)


def coded(share):
    return jnp.clip(jnp.round(share * code_top), 0.0, code_top) - code_half


def stored(codes):
    return codes.astype(jnp.int32).astype(jnp.int16)


def density_codes(values):
    octave = jnp.log(jnp.maximum(values, 2.0**-40)) * (1.0 / log_two)
    return stored(coded((octave - term_low) * (1.0 / term_octaves)))


def densities(codes):
    codes = codes.astype(f32)
    octave = (codes + code_half) * (term_octaves / code_top) + term_low
    return jnp.where(codes == -code_half, 0.0, jnp.exp(octave * log_two))


def splat_kernel(
    tiles, parts, rows_in, cols_in, fracs_in, pin_weights_in, row_blocks_in, cap_in, block_in, out_ref,
    rows_ref, cols_ref, fracs_ref, pin_weights_ref, row_blocks_ref, cap_ref, block_ref, arrived,
):
    depth = cap_ref.shape[0]
    height = parts * depth
    sources = (rows_in, cols_in, fracs_in, pin_weights_in, row_blocks_in, cap_in, block_in)
    places = (rows_ref, cols_ref, fracs_ref, pin_weights_ref, row_blocks_ref, cap_ref, block_ref)
    copies = [
        pltpu.make_async_copy(source, place, arrived.at[n]) for n, (source, place) in enumerate(zip(sources, places))
    ]
    for copy in copies:
        copy.start()
    for copy in copies[:4]:
        copy.wait()
    rows, cols, sizes = rows_ref[...], cols_ref[...], pin_weights_ref[...]
    place = iota((height * (tiles + 1), LANES), 0)
    group, inner = place // height, place % height
    keys = ((inner // depth) * tiles + group - 1) * depth + inner % depth
    lane = iota((LANES + 8, LANES), 0)
    tables, lanes = [], []
    for j in range(rows.shape[0]):
        cut = slice(j * LANES, (j + 1) * LANES)
        fy, fx = fracs_ref[0:1, cut], fracs_ref[1:2, cut]
        size, col = sizes[j : j + 1], cols[j : j + 1]
        key = (col >> 7) * depth + rows[j : j + 1]
        tables.append(pick(keys, key, rounded(size * (1.0 - fy)), rounded(size * fy)).astype(bf16))
        lanes.append(pick(lane, col & 127, rounded(1.0 - fx), rounded(fx)).astype(bf16))
    total = last_dims(jnp.concatenate(tables, 1), jnp.concatenate(lanes, 1))
    for copy in copies[4:]:
        copy.wait()
    first_lane = iota((height, LANES), 1) == 0
    for t in range(tiles):
        own = total[(t + 1) * height : (t + 2) * height, :LANES]
        spill = total[t * height : (t + 1) * height, LANES : LANES + 1]
        own = own + jnp.where(first_lane, spill, 0.0)
        cut = slice(t * LANES, (t + 1) * LANES)
        out_ref[:height, cut] = density_codes(own)
        share = (row_blocks_ref[t * LANES : (t + 1) * LANES, :] - block_low) * (1.0 / block_span)
        out_ref[2 * height :, cut] = stored(coded(share))
    weights = cap_ref[...].astype(f32) * (1.0 - block_ref[...])
    code = coded((weights - weight_low) * (1.0 / weight_span))
    row = iota((height, weights.shape[1]), 0)
    mine = row // depth == lax.axis_index("cells")
    out_ref[height : 2 * height, :] = stored(jnp.where(mine, jnp.concatenate([code] * parts, 0), 0.0))


def sum_kernel(*refs):
    sent_refs, out_ref = refs[:-1], refs[-1]
    height = out_ref.shape[0] // 2
    terms, codes = 0.0, 0.0
    for sent_ref in sent_refs:
        terms += densities(sent_ref[:height, :])
        codes += sent_ref[height:, :].astype(f32)
    out_ref[:height, :] = density_codes(terms)
    out_ref[height:, :] = stored(codes)


def beside(values):
    width = values.shape[1]
    lane = iota((values.shape[0], LANES), 1)
    left, right = pltpu.roll(values, 1, 1), pltpu.roll(values, width - 1, 1)
    first = jnp.where(lane == 0, values[:, :LANES], left[:, :LANES])
    last = jnp.where(lane == LANES - 1, values[:, width - LANES :], right[:, width - LANES :])
    return (
        jnp.concatenate([first, left[:, LANES:]], 1),
        jnp.concatenate([right[:, : width - LANES], last], 1),
    )


class Turned:
    def __init__(self, tiles):
        self.tiles, self.turned = tiles, {}

    def turn(self, t, shift):
        if (t, shift) not in self.turned:
            self.turned[t, shift] = pltpu.roll(self.tiles[t], shift, 1)
        return self.turned[t, shift]

    def along(self, t):
        mine, back = self.tiles[t], LANES - 1
        lane = iota(mine.shape, 1)
        before = self.turn(t - 1, 1) if t else mine
        after = self.turn(t + 1, back) if t + 1 < len(self.tiles) else mine
        left = jnp.where(lane == 0, before, self.turn(t, 1))
        right = jnp.where(lane == back, after, self.turn(t, back))
        return 2.0 * mine - left - right


def delayed(count, first, second, delay=2):
    waiting, results = [], []
    for t in range(count + delay):
        if t < count:
            waiting.append(first(t))
        if t >= delay:
            results.append(second(t - delay, waiting[t - delay]))
            waiting[t - delay] = None
    return results


def across_lines(values):
    height = values.shape[0]
    row = iota((8, values.shape[1]), 0)
    above, below = pltpu.roll(values, 1, 0), pltpu.roll(values, height - 1, 0)
    first = jnp.where(row == 0, values[:8], above[:8])
    last = jnp.where(row == 7, values[height - 8 :], below[height - 8 :])
    above = jnp.concatenate([first, above[8:]], 0)
    below = jnp.concatenate([below[: height - 8], last], 0)
    return 2.0 * values - above - below


def col_products(residual, blocks):
    high, low = halves(residual)
    size = blocks[0].shape[0] // 2
    dot = functools.partial(jnp.dot, preferred_element_type=f32)
    cuts = [slice(k * size, (k + 1) * size) for k in range(len(blocks))]
    return [(dot(pair, high[cut]), dot(pair[:size], low[cut])) for pair, cut in zip(blocks, cuts)]


def col_sum(products):
    size = products[0][1].shape[0]
    result = [both[:size] + (both[size:] + rest) for both, rest in products]
    return result[0] if len(result) == 1 else jnp.concatenate(result, 0)


def each(count, body):
    if count == 1:
        body(0)
    else:
        pl.loop(0, count)(body)


def join_kernel(*refs):
    for n, ref in enumerate(refs[:-1]):
        refs[-1][n * ref.shape[0] : (n + 1) * ref.shape[0], :] = ref[...]


def tables_kernel(sizes, codes_ref, rows_ref, cols_ref, fracs_ref, pairs_ref, look_ref, share_ref):
    depth, tiles, parts, carried = sizes
    for k in range(pairs_ref.shape[0]):
        base = (k // tiles) * (carried + LANES) + carried
        code = codes_ref[base : base + LANES, k % tiles * LANES : (k % tiles + 1) * LANES].astype(f32)
        high, low = halves(((code + code_half) * (block_span / code_top) + block_low).T)
        pairs_ref[k, :, :LANES] = high
        pairs_ref[k, :, LANES:] = low
    half = LANES // 2
    many = parts * tiles * depth
    rows, cols = rows_ref[...], cols_ref[...]
    blank = jnp.zeros((LANES - many, LANES), bf16)
    keys, lane = iota((many, LANES), 0), iota((half + 8, LANES), 0)
    for j in range(rows.shape[0]):
        cut = slice(j * LANES, (j + 1) * LANES)
        fy, fx = fracs_ref[0:1, cut], fracs_ref[1:2, cut]
        col = cols[j : j + 1]
        key = (col >> 7) * depth + rows[j : j + 1]
        second = (col & half) != 0
        near, far = rounded(1.0 - fy), rounded(fy)
        looks = [
            pick(keys, jnp.where(second, -8, key), near, far).astype(bf16),
            blank,
            pick(keys, jnp.where(second, key, -8), near, far).astype(bf16),
            blank,
        ]
        look_ref[:, cut] = jnp.concatenate(looks, 0)
        share_ref[:, cut] = pick(lane, col & (half - 1), rounded(1.0 - fx), rounded(fx))


def field_kernel(
    sizes, orders, pairs, look_ref, share_ref, col_blocks_ref, *refs,
):
    depth, tiles, parts, strips = sizes
    sent_refs, (final_ref, velocity_ref, weights_ref, source_ref, field_ref, ordered) = refs[:-6], refs[-6:]
    width_part = tiles * LANES
    width = parts * width_part
    height = strips * depth
    chunk = min(GROUP, strips) * depth
    chunks = height // chunk
    strip, part = lax.axis_index("strip"), lax.axis_index("cells")

    slots = parts * depth
    if len(sent_refs) == 1:
        sent = sent_refs[0]
    else:
        sent = ordered
        for order, sent_ref in zip(orders, sent_refs):
            for n, bits in enumerate(order):
                ordered[strip ^ bits] = sent_ref[n * 2 * slots : (n + 1) * 2 * slots, :]
    group = chunk // depth
    target, origin = iota((parts * chunk, group * slots), 0), iota((parts * chunk, group * slots), 1)
    slot = origin % slots
    fits = (slot // depth == target // chunk) & (origin // slots * depth + slot % depth == target % chunk)
    chosen = jnp.where(fits, 1.0, 0.0).astype(bf16)

    def placed(values):
        high, low = halves(jnp.concatenate(values, 0))
        dot = functools.partial(jnp.dot, preferred_element_type=f32)
        return dot(chosen, high) + dot(chosen, low)

    @functools.partial(each, chunks)
    def place(g):
        terms, codes = [], []
        for n in range(group):
            got = sent[g * group + n]
            terms.append(densities(got[:slots]))
            codes.append(got[slots:].astype(f32))
        term = placed(terms)
        weight = (placed(codes) + code_half) * (weight_span / code_top) + weight_low
        here = pl.ds(pl.multiple_of(g * chunk, chunk), chunk)
        for p in range(parts):
            cut = slice(p * width_part, (p + 1) * width_part)
            weights_ref[here, cut] = weight[p * chunk : (p + 1) * chunk]
            source_ref[here, cut] = term[p * chunk : (p + 1) * chunk] / weight[p * chunk : (p + 1) * chunk]

    col_blocks = [jnp.concatenate(halves(col_blocks_ref[k]), 0) for k in range(col_blocks_ref.shape[0])]
    inner = pl.ds(8, height)
    lanes_at_once = 2 * LANES if chunks == 1 and width % (2 * LANES) == 0 else LANES
    at_once = width // lanes_at_once if chunks == 1 else 1

    def cuts_of(g):
        if at_once > 1:
            return [slice(n * lanes_at_once, (n + 1) * lanes_at_once) for n in range(at_once)]
        return [pl.ds(pl.multiple_of(g * lanes_at_once, lanes_at_once), lanes_at_once)]

    col_steps = width // lanes_at_once // at_once

    @functools.partial(each, col_steps)
    def start(g):
        for cut in cuts_of(g):
            current = source_ref[:, cut]
            field_ref[inner, cut] = current
            source_ref[:, cut] = weights_ref[:, cut] * current - coupling * across_lines(current)

    row_tiles = [slice(t * LANES, (t + 1) * LANES) for t in range(width // LANES)]
    for step in range(STEPS):

        @functools.partial(each, chunks)
        def solve_rows(g):
            here = pl.ds(pl.multiple_of(g * chunk, chunk), chunk)
            there = pl.ds(pl.multiple_of(g * chunk + 8, 8), chunk)
            current = [field_ref[there, cut] for cut in row_tiles]
            for sweep in range(SWEEPS):
                turned = Turned(current)

                def multiply(t):
                    cut = row_tiles[t]
                    now = weights_ref[here, cut] * turned.tiles[t] + coupling * turned.along(t)
                    both = jnp.concatenate(halves(source_ref[here, cut] - now), 0)
                    return jnp.dot(both, pairs[t], preferred_element_type=f32)

                def add(t, product):
                    high, low = product[:chunk], product[chunk:]
                    return turned.tiles[t] + (high[:, :LANES] + (high[:, LANES:] + low[:, :LANES]))

                current = delayed(len(current), multiply, add)
            turned = Turned(current)
            for t, cut in enumerate(row_tiles):
                field_ref[there, cut] = current[t]
                source_ref[here, cut] = weights_ref[here, cut] * current[t] - coupling * turned.along(t)

        @functools.partial(each, col_steps)
        def solve_cols(g):
            cuts = cuts_of(g)
            current = [field_ref[inner, cut] for cut in cuts]
            for sweep in range(SWEEPS):
                before = current

                def multiply(n):
                    now = weights_ref[:, cuts[n]] * before[n] + coupling * across_lines(before[n])
                    return col_products(source_ref[:, cuts[n]] - now, col_blocks)

                current = delayed(len(cuts), multiply, lambda n, products: before[n] + col_sum(products))
            for now, cut in zip(current, cuts):
                field_ref[inner, cut] = now
                if step + 1 < STEPS:
                    source_ref[:, cut] = weights_ref[:, cut] * now - coupling * across_lines(now)
                else:
                    field_ref[:8, cut] = jnp.broadcast_to(now[:1], (8, lanes_at_once))
                    field_ref[height + 8 :, cut] = jnp.broadcast_to(now[-1:], (8, lanes_at_once))

    row0 = strip * depth
    columns = pl.ds(pl.multiple_of(part * width_part, LANES), width_part)
    base, shift = pl.multiple_of(row0 // 8 * 8, 8), 17 - row0 % 8
    final_ref[...] = pltpu.roll(field_ref[pl.ds(base, 24), columns], shift, 0)[1 : 1 + depth]

    window = pltpu.roll(field_ref[pl.ds(base, 24), :], shift, 0)
    above, centre, below = window[:8], pltpu.roll(window, 23, 0)[:8], pltpu.roll(window, 22, 0)[:8]
    left, right = beside(centre)
    scale = jnp.maximum(centre, floor_level)
    velocity_y = rounded(-(0.5 * (below - above)) / scale)
    velocity_x = rounded(-(0.5 * (right - left)) / scale)

    upper = iota((8, LANES), 0) < depth

    def stacked(values):
        stack = []
        for t in range(0, parts * tiles, 2):
            even = values[:, t * LANES : (t + 1) * LANES]
            odd = values[:, (t + 1) * LANES : (t + 2) * LANES]
            stack.append(jnp.where(upper, even, pltpu.roll(odd, depth, 0)))
        return jnp.concatenate(stack, 0)

    half = LANES // 2

    def table_of(values):
        stack = stacked(values)
        many = stack.shape[0]
        blank = jnp.zeros((LANES - many, LANES), f32)
        turned = jnp.concatenate([stack, blank], 0).T
        after = jnp.concatenate([pltpu.roll(stack, many - depth, 0), blank], 0).T[:8]
        return jnp.concatenate([turned[: half + 8], jnp.concatenate([turned[half:], after], 0)], 1)

    table = jnp.concatenate([table_of(velocity_y), table_of(velocity_x)], 0).astype(bf16)
    pins = share_ref.shape[1]
    at_once = 2 * LANES if pins % (2 * LANES) == 0 else LANES
    for j in range(0, pins, at_once):
        cut = slice(j, j + at_once)
        sampled = jnp.dot(table, look_ref[:, cut], preferred_element_type=f32)
        share = share_ref[:, cut]
        velocity_ref[0:1, cut] = jnp.sum(sampled[: half + 8] * share, 0, keepdims=True)
        velocity_ref[1:2, cut] = jnp.sum(sampled[half + 8 :] * share, 0, keepdims=True)


def partner(values, axis, bits):
    return lax.ppermute(values, axis, [(n, n ^ bits) for n in range(lax.axis_size(axis))])


def local(pin_rows, pin_cols, pin_fracs, pin_weights, capacity, blockage, row_blocks, col_blocks):
    depth, width_part = capacity.shape
    parts, strips = lax.axis_size("cells"), lax.axis_size("strip")
    tiles = width_part // LANES
    height, width = depth * strips, width_part * parts
    pins = pin_rows.shape[0]
    by_lane = (pins // LANES, LANES)
    rows, cols = pin_rows.reshape(by_lane), pin_cols.reshape(by_lane)
    sizes = pin_weights.reshape(by_lane)
    vmem = pl.BlockSpec(memory_space=pltpu.VMEM)
    whole = pltpu.CompilerParams(vmem_limit_bytes=60 << 20)
    small = pltpu.CompilerParams(vmem_limit_bytes=16 * 1024 * 1024)
    grid_bytes = 4 * height * width
    large = pltpu.CompilerParams(vmem_limit_bytes=(20 << 20) + 6 * grid_bytes)

    carried = 2 * parts * depth
    read = (rows, cols, pin_fracs, sizes, row_blocks.reshape(-1, LANES), capacity, blockage)
    terms = pl.pallas_call(
        functools.partial(splat_kernel, tiles, parts),
        out_shape=jax.ShapeDtypeStruct((carried + LANES, width_part), jnp.int16),
        in_specs=[pl.BlockSpec(memory_space=pltpu.HBM)] * 7,
        out_specs=vmem,
        scratch_shapes=[pltpu.VMEM(item.shape, item.dtype) for item in read] + [pltpu.SemaphoreType.DMA((7,))],
        compiler_params=whole,
        name="splat",
    )(*read)
    blocks = lax.all_gather(terms, "cells", axis=0, tiled=True)

    def terms_of(part):
        place = part * (carried + LANES) // carried
        return pl.BlockSpec((carried, width_part), lambda i: (place, 0))

    sums = pl.pallas_call(
        sum_kernel,
        grid=(1,),
        out_shape=jax.ShapeDtypeStruct((carried, width_part), jnp.int16),
        in_specs=[terms_of(part) for part in range(parts)],
        out_specs=pl.BlockSpec((carried, width_part), lambda i: (0, 0)),
        compiler_params=small,
        name="sum_terms",
    )(*[blocks] * parts)
    if strips == 8:
        orders = ((0, 6, 4, 2), (1, 7, 5, 3))
        from_z = lax.optimization_barrier([partner(sums, "strip", bits) for bits in (6, 4, 2)])
        held = pl.pallas_call(
            join_kernel,
            out_shape=jax.ShapeDtypeStruct((4 * carried, width_part), jnp.int16),
            in_specs=[vmem] * 4,
            out_specs=vmem,
            compiler_params=small,
            name="join",
        )(sums, *from_z)
        held, blocks = lax.optimization_barrier((held, blocks))
        sent = [held, partner(held, "strip", 1)]
    else:
        orders, sent = (), [lax.all_gather(sums, "strip", axis=0)]
    pairs, look, share = pl.pallas_call(
        functools.partial(tables_kernel, (depth, tiles, parts, carried)),
        out_shape=(
            jax.ShapeDtypeStruct((width // LANES, LANES, 2 * LANES), bf16),
            jax.ShapeDtypeStruct((2 * LANES, pins), bf16),
            jax.ShapeDtypeStruct((LANES // 2 + 8, pins), f32),
        ),
        in_specs=[vmem] * 4,
        out_specs=(vmem,) * 3,
        compiler_params=small,
        cost_estimate=pl.CostEstimate(flops=1 << 20, bytes_accessed=1 << 21, transcendentals=0),
        name="tables",
    )(blocks, rows, cols, pin_fracs)

    final, velocity = pl.pallas_call(
        functools.partial(field_kernel, (depth, tiles, parts, strips), orders),
        out_shape=(
            jax.ShapeDtypeStruct((depth, width_part), f32),
            jax.ShapeDtypeStruct((2, pins), f32),
        ),
        in_specs=[vmem] * (4 + len(sent)),
        out_specs=(vmem, vmem),
        scratch_shapes=[
            pltpu.VMEM((height, width), f32),
            pltpu.VMEM((height, width), f32),
            pltpu.VMEM((height + 16, width), f32),
            pltpu.VMEM((strips if len(sent) > 1 else 1, carried, width_part), jnp.int16),
        ],
        compiler_params=large,
        name="field",
    )(pairs, look, share, col_blocks, *sent)
    return final, velocity


def solution(mesh):
    placed = (
        P(("strip", "cells")),
        P(("strip", "cells")),
        P(None, ("strip", "cells")),
        P(("strip", "cells")),
        P("strip", "cells"),
        P("strip", "cells"),
        P("cells", None, None),
        P(),
    )
    return jax.shard_map(
        local,
        mesh=mesh,
        in_specs=placed,
        out_specs=(P("strip", "cells"), P(None, ("strip", "cells"))),
        check_vma=False,
    )
```

```python
import functools

import jax
import jax.numpy as jnp
from jax import lax
from jax.experimental import pallas as pl
from jax.experimental.pallas import tpu as pltpu
from jax.sharding import PartitionSpec as P

SWEEPS = 3
STEPS = 2
LANES = 128
GROUP = 8

coupling = 2.0
floor_level = 0.5
block_low, block_span = -0.002, 0.152
weight_low, weight_span = 0.5, 3.5
term_low, term_octaves = -20.0, 34.0
code_top = 65535.0
code_half = 32768.0
log_two = 0.6931471805599453

f32 = jnp.float32
bf16 = jnp.bfloat16


def iota(shape, axis):
    return lax.broadcasted_iota(jnp.int32, shape, axis)


def halves(values):
    high = values.astype(bf16)
    return high, (values - high.astype(f32)).astype(bf16)


def last_dims(left, right):
    return lax.dot_general(left, right, (((1,), (1,)), ((), ())), preferred_element_type=f32)


def pick(index, first, near, far):
    return jnp.where(index == first, near, jnp.where(index == first + 1, far, 0.0))


def rounded(values):
    return values.astype(bf16).astype(f32)


def coded(share):
    return jnp.clip(jnp.round(share * code_top), 0.0, code_top) - code_half


def stored(codes):
    return codes.astype(jnp.int32).astype(jnp.int16)


def density_codes(values):
    octave = jnp.log(jnp.maximum(values, 2.0**-40)) * (1.0 / log_two)
    return stored(coded((octave - term_low) * (1.0 / term_octaves)))


def densities(codes):
    codes = codes.astype(f32)
    octave = (codes + code_half) * (term_octaves / code_top) + term_low
    return jnp.where(codes == -code_half, 0.0, jnp.exp(octave * log_two))


def splat_kernel(
    tiles, parts, rows_in, cols_in, fracs_in, pin_weights_in, row_blocks_in, cap_in, block_in, out_ref,
    rows_ref, cols_ref, fracs_ref, pin_weights_ref, row_blocks_ref, cap_ref, block_ref, arrived,
):
    depth = cap_ref.shape[0]
    height = parts * depth
    sources = (rows_in, cols_in, fracs_in, pin_weights_in, row_blocks_in, cap_in, block_in)
    places = (rows_ref, cols_ref, fracs_ref, pin_weights_ref, row_blocks_ref, cap_ref, block_ref)
    copies = [
        pltpu.make_async_copy(source, place, arrived.at[n]) for n, (source, place) in enumerate(zip(sources, places))
    ]
    for copy in copies:
        copy.start()
    for copy in copies[:4]:
        copy.wait()
    rows, cols, sizes = rows_ref[...], cols_ref[...], pin_weights_ref[...]
    place = iota((height * (tiles + 1), LANES), 0)
    group, inner = place // height, place % height
    keys = ((inner // depth) * tiles + group - 1) * depth + inner % depth
    lane = iota((LANES + 8, LANES), 0)
    tables, lanes = [], []
    for j in range(rows.shape[0]):
        cut = slice(j * LANES, (j + 1) * LANES)
        fy, fx = fracs_ref[0:1, cut], fracs_ref[1:2, cut]
        size, col = sizes[j : j + 1], cols[j : j + 1]
        key = (col >> 7) * depth + rows[j : j + 1]
        tables.append(pick(keys, key, rounded(size * (1.0 - fy)), rounded(size * fy)).astype(bf16))
        lanes.append(pick(lane, col & 127, rounded(1.0 - fx), rounded(fx)).astype(bf16))
    total = last_dims(jnp.concatenate(tables, 1), jnp.concatenate(lanes, 1))
    for copy in copies[4:]:
        copy.wait()
    first_lane = iota((height, LANES), 1) == 0
    for t in range(tiles):
        own = total[(t + 1) * height : (t + 2) * height, :LANES]
        spill = total[t * height : (t + 1) * height, LANES : LANES + 1]
        own = own + jnp.where(first_lane, spill, 0.0)
        cut = slice(t * LANES, (t + 1) * LANES)
        out_ref[:height, cut] = density_codes(own)
        share = (row_blocks_ref[t * LANES : (t + 1) * LANES, :] - block_low) * (1.0 / block_span)
        out_ref[2 * height :, cut] = stored(coded(share))
    weights = cap_ref[...].astype(f32) * (1.0 - block_ref[...])
    code = coded((weights - weight_low) * (1.0 / weight_span))
    row = iota((height, weights.shape[1]), 0)
    mine = row // depth == lax.axis_index("cells")
    out_ref[height : 2 * height, :] = stored(jnp.where(mine, jnp.concatenate([code] * parts, 0), 0.0))


def sum_kernel(*refs):
    sent_refs, out_ref = refs[:-1], refs[-1]
    height = out_ref.shape[0] // 2
    terms, codes = 0.0, 0.0
    for sent_ref in sent_refs:
        terms += densities(sent_ref[:height, :])
        codes += sent_ref[height:, :].astype(f32)
    out_ref[:height, :] = density_codes(terms)
    out_ref[height:, :] = stored(codes)


def beside(values):
    width = values.shape[1]
    lane = iota((values.shape[0], LANES), 1)
    left, right = pltpu.roll(values, 1, 1), pltpu.roll(values, width - 1, 1)
    first = jnp.where(lane == 0, values[:, :LANES], left[:, :LANES])
    last = jnp.where(lane == LANES - 1, values[:, width - LANES :], right[:, width - LANES :])
    return (
        jnp.concatenate([first, left[:, LANES:]], 1),
        jnp.concatenate([right[:, : width - LANES], last], 1),
    )


class Turned:
    def __init__(self, tiles):
        self.tiles, self.turned = tiles, {}

    def turn(self, t, shift):
        if (t, shift) not in self.turned:
            self.turned[t, shift] = pltpu.roll(self.tiles[t], shift, 1)
        return self.turned[t, shift]

    def along(self, t):
        mine, back = self.tiles[t], LANES - 1
        lane = iota(mine.shape, 1)
        before = self.turn(t - 1, 1) if t else mine
        after = self.turn(t + 1, back) if t + 1 < len(self.tiles) else mine
        left = jnp.where(lane == 0, before, self.turn(t, 1))
        right = jnp.where(lane == back, after, self.turn(t, back))
        return 2.0 * mine - left - right


def delayed(count, first, second, delay=2):
    waiting, results = [], []
    for t in range(count + delay):
        if t < count:
            waiting.append(first(t))
        if t >= delay:
            results.append(second(t - delay, waiting[t - delay]))
            waiting[t - delay] = None
    return results


def across_lines(values):
    height = values.shape[0]
    row = iota((8, values.shape[1]), 0)
    above, below = pltpu.roll(values, 1, 0), pltpu.roll(values, height - 1, 0)
    first = jnp.where(row == 0, values[:8], above[:8])
    last = jnp.where(row == 7, values[height - 8 :], below[height - 8 :])
    above = jnp.concatenate([first, above[8:]], 0)
    below = jnp.concatenate([below[: height - 8], last], 0)
    return 2.0 * values - above - below


def col_products(residual, blocks):
    high, low = halves(residual)
    size = blocks[0].shape[0] // 2
    dot = functools.partial(jnp.dot, preferred_element_type=f32)
    cuts = [slice(k * size, (k + 1) * size) for k in range(len(blocks))]
    return [(dot(pair, high[cut]), dot(pair[:size], low[cut])) for pair, cut in zip(blocks, cuts)]


def col_sum(products):
    size = products[0][1].shape[0]
    result = [both[:size] + (both[size:] + rest) for both, rest in products]
    return result[0] if len(result) == 1 else jnp.concatenate(result, 0)


def each(count, body):
    if count == 1:
        body(0)
    else:
        pl.loop(0, count)(body)


def join_kernel(*refs):
    for n, ref in enumerate(refs[:-1]):
        refs[-1][n * ref.shape[0] : (n + 1) * ref.shape[0], :] = ref[...]


def tables_kernel(sizes, codes_ref, rows_ref, cols_ref, fracs_ref, pairs_ref, look_ref, share_ref):
    depth, tiles, parts, carried = sizes
    for k in range(pairs_ref.shape[0]):
        base = (k // tiles) * (carried + LANES) + carried
        code = codes_ref[base : base + LANES, k % tiles * LANES : (k % tiles + 1) * LANES].astype(f32)
        high, low = halves(((code + code_half) * (block_span / code_top) + block_low).T)
        pairs_ref[k, :, :LANES] = high
        pairs_ref[k, :, LANES:] = low
    half = LANES // 2
    many = parts * tiles * depth
    rows, cols = rows_ref[...], cols_ref[...]
    blank = jnp.zeros((LANES - many, LANES), bf16)
    keys, lane = iota((many, LANES), 0), iota((half + 8, LANES), 0)
    for j in range(rows.shape[0]):
        cut = slice(j * LANES, (j + 1) * LANES)
        fy, fx = fracs_ref[0:1, cut], fracs_ref[1:2, cut]
        col = cols[j : j + 1]
        key = (col >> 7) * depth + rows[j : j + 1]
        second = (col & half) != 0
        near, far = rounded(1.0 - fy), rounded(fy)
        looks = [
            pick(keys, jnp.where(second, -8, key), near, far).astype(bf16),
            blank,
            pick(keys, jnp.where(second, key, -8), near, far).astype(bf16),
            blank,
        ]
        look_ref[:, cut] = jnp.concatenate(looks, 0)
        share_ref[:, cut] = pick(lane, col & (half - 1), rounded(1.0 - fx), rounded(fx))


def field_kernel(
    sizes, orders, pairs, look_ref, share_ref, col_blocks_ref, *refs,
):
    depth, tiles, parts, strips = sizes
    sent_refs, (final_ref, velocity_ref, weights_ref, source_ref, field_ref, ordered) = refs[:-6], refs[-6:]
    width_part = tiles * LANES
    width = parts * width_part
    height = strips * depth
    chunk = min(GROUP, strips) * depth
    chunks = height // chunk
    strip, part = lax.axis_index("strip"), lax.axis_index("cells")

    slots = parts * depth
    if len(sent_refs) == 1:
        sent = sent_refs[0]
    else:
        sent = ordered
        for order, sent_ref in zip(orders, sent_refs):
            for n, bits in enumerate(order):
                ordered[strip ^ bits] = sent_ref[n * 2 * slots : (n + 1) * 2 * slots, :]
    group = chunk // depth
    target, origin = iota((parts * chunk, group * slots), 0), iota((parts * chunk, group * slots), 1)
    slot = origin % slots
    fits = (slot // depth == target // chunk) & (origin // slots * depth + slot % depth == target % chunk)
    chosen = jnp.where(fits, 1.0, 0.0).astype(bf16)

    def placed(values):
        high, low = halves(jnp.concatenate(values, 0))
        dot = functools.partial(jnp.dot, preferred_element_type=f32)
        return dot(chosen, high) + dot(chosen, low)

    @functools.partial(each, chunks)
    def place(g):
        terms, codes = [], []
        for n in range(group):
            got = sent[g * group + n]
            terms.append(densities(got[:slots]))
            codes.append(got[slots:].astype(f32))
        term = placed(terms)
        weight = (placed(codes) + code_half) * (weight_span / code_top) + weight_low
        here = pl.ds(pl.multiple_of(g * chunk, chunk), chunk)
        for p in range(parts):
            cut = slice(p * width_part, (p + 1) * width_part)
            weights_ref[here, cut] = weight[p * chunk : (p + 1) * chunk]
            source_ref[here, cut] = term[p * chunk : (p + 1) * chunk] / weight[p * chunk : (p + 1) * chunk]

    col_blocks = [jnp.concatenate(halves(col_blocks_ref[k]), 0) for k in range(col_blocks_ref.shape[0])]
    inner = pl.ds(8, height)
    lanes_at_once = 2 * LANES if chunks == 1 and width % (2 * LANES) == 0 else LANES
    at_once = width // lanes_at_once if chunks == 1 else 1

    def cuts_of(g):
        if at_once > 1:
            return [slice(n * lanes_at_once, (n + 1) * lanes_at_once) for n in range(at_once)]
        return [pl.ds(pl.multiple_of(g * lanes_at_once, lanes_at_once), lanes_at_once)]

    col_steps = width // lanes_at_once // at_once

    @functools.partial(each, col_steps)
    def start(g):
        for cut in cuts_of(g):
            current = source_ref[:, cut]
            field_ref[inner, cut] = current
            source_ref[:, cut] = weights_ref[:, cut] * current - coupling * across_lines(current)

    row_tiles = [slice(t * LANES, (t + 1) * LANES) for t in range(width // LANES)]
    for step in range(STEPS):

        @functools.partial(each, chunks)
        def solve_rows(g):
            here = pl.ds(pl.multiple_of(g * chunk, chunk), chunk)
            there = pl.ds(pl.multiple_of(g * chunk + 8, 8), chunk)
            current = [field_ref[there, cut] for cut in row_tiles]
            for sweep in range(SWEEPS):
                turned = Turned(current)

                def multiply(t):
                    cut = row_tiles[t]
                    now = weights_ref[here, cut] * turned.tiles[t] + coupling * turned.along(t)
                    both = jnp.concatenate(halves(source_ref[here, cut] - now), 0)
                    return jnp.dot(both, pairs[t], preferred_element_type=f32)

                def add(t, product):
                    high, low = product[:chunk], product[chunk:]
                    return turned.tiles[t] + (high[:, :LANES] + (high[:, LANES:] + low[:, :LANES]))

                current = delayed(len(current), multiply, add)
            turned = Turned(current)
            for t, cut in enumerate(row_tiles):
                field_ref[there, cut] = current[t]
                source_ref[here, cut] = weights_ref[here, cut] * current[t] - coupling * turned.along(t)

        @functools.partial(each, col_steps)
        def solve_cols(g):
            cuts = cuts_of(g)
            current = [field_ref[inner, cut] for cut in cuts]
            for sweep in range(SWEEPS):
                before = current

                def multiply(n):
                    now = weights_ref[:, cuts[n]] * before[n] + coupling * across_lines(before[n])
                    return col_products(source_ref[:, cuts[n]] - now, col_blocks)

                current = delayed(len(cuts), multiply, lambda n, products: before[n] + col_sum(products))
            for now, cut in zip(current, cuts):
                field_ref[inner, cut] = now
                if step + 1 < STEPS:
                    source_ref[:, cut] = weights_ref[:, cut] * now - coupling * across_lines(now)
                else:
                    field_ref[:8, cut] = jnp.broadcast_to(now[:1], (8, lanes_at_once))
                    field_ref[height + 8 :, cut] = jnp.broadcast_to(now[-1:], (8, lanes_at_once))

    row0 = strip * depth
    columns = pl.ds(pl.multiple_of(part * width_part, LANES), width_part)
    base, shift = pl.multiple_of(row0 // 8 * 8, 8), 17 - row0 % 8
    final_ref[...] = pltpu.roll(field_ref[pl.ds(base, 24), columns], shift, 0)[1 : 1 + depth]

    window = pltpu.roll(field_ref[pl.ds(base, 24), :], shift, 0)
    above, centre, below = window[:8], pltpu.roll(window, 23, 0)[:8], pltpu.roll(window, 22, 0)[:8]
    left, right = beside(centre)
    scale = jnp.maximum(centre, floor_level)
    velocity_y = rounded(-(0.5 * (below - above)) / scale)
    velocity_x = rounded(-(0.5 * (right - left)) / scale)

    upper = iota((8, LANES), 0) < depth

    def stacked(values):
        stack = []
        for t in range(0, parts * tiles, 2):
            even = values[:, t * LANES : (t + 1) * LANES]
            odd = values[:, (t + 1) * LANES : (t + 2) * LANES]
            stack.append(jnp.where(upper, even, pltpu.roll(odd, depth, 0)))
        return jnp.concatenate(stack, 0)

    half = LANES // 2

    def table_of(values):
        stack = stacked(values)
        many = stack.shape[0]
        blank = jnp.zeros((LANES - many, LANES), f32)
        turned = jnp.concatenate([stack, blank], 0).T
        after = jnp.concatenate([pltpu.roll(stack, many - depth, 0), blank], 0).T[:8]
        return jnp.concatenate([turned[: half + 8], jnp.concatenate([turned[half:], after], 0)], 1)

    table = jnp.concatenate([table_of(velocity_y), table_of(velocity_x)], 0).astype(bf16)
    pins = share_ref.shape[1]
    at_once = 2 * LANES if pins % (2 * LANES) == 0 else LANES
    for j in range(0, pins, at_once):
        cut = slice(j, j + at_once)
        sampled = jnp.dot(table, look_ref[:, cut], preferred_element_type=f32)
        share = share_ref[:, cut]
        velocity_ref[0:1, cut] = jnp.sum(sampled[: half + 8] * share, 0, keepdims=True)
        velocity_ref[1:2, cut] = jnp.sum(sampled[half + 8 :] * share, 0, keepdims=True)


def partner(values, axis, bits):
    return lax.ppermute(values, axis, [(n, n ^ bits) for n in range(lax.axis_size(axis))])


def local(pin_rows, pin_cols, pin_fracs, pin_weights, capacity, blockage, row_blocks, col_blocks):
    depth, width_part = capacity.shape
    parts, strips = lax.axis_size("cells"), lax.axis_size("strip")
    tiles = width_part // LANES
    height, width = depth * strips, width_part * parts
    pins = pin_rows.shape[0]
    by_lane = (pins // LANES, LANES)
    rows, cols = pin_rows.reshape(by_lane), pin_cols.reshape(by_lane)
    sizes = pin_weights.reshape(by_lane)
    vmem = pl.BlockSpec(memory_space=pltpu.VMEM)
    whole = pltpu.CompilerParams(vmem_limit_bytes=60 << 20)
    small = pltpu.CompilerParams(vmem_limit_bytes=16 * 1024 * 1024)
    grid_bytes = 4 * height * width
    large = pltpu.CompilerParams(vmem_limit_bytes=(20 << 20) + 6 * grid_bytes)

    carried = 2 * parts * depth
    read = (rows, cols, pin_fracs, sizes, row_blocks.reshape(-1, LANES), capacity, blockage)
    terms = pl.pallas_call(
        functools.partial(splat_kernel, tiles, parts),
        out_shape=jax.ShapeDtypeStruct((carried + LANES, width_part), jnp.int16),
        in_specs=[pl.BlockSpec(memory_space=pltpu.HBM)] * 7,
        out_specs=vmem,
        scratch_shapes=[pltpu.VMEM(item.shape, item.dtype) for item in read] + [pltpu.SemaphoreType.DMA((7,))],
        compiler_params=whole,
        name="splat",
    )(*read)
    blocks = lax.all_gather(terms, "cells", axis=0, tiled=True)

    def terms_of(part):
        place = part * (carried + LANES) // carried
        return pl.BlockSpec((carried, width_part), lambda i: (place, 0))

    sums = pl.pallas_call(
        sum_kernel,
        grid=(1,),
        out_shape=jax.ShapeDtypeStruct((carried, width_part), jnp.int16),
        in_specs=[terms_of(part) for part in range(parts)],
        out_specs=pl.BlockSpec((carried, width_part), lambda i: (0, 0)),
        compiler_params=small,
        name="sum_terms",
    )(*[blocks] * parts)
    if strips == 8:
        orders = ((0,), (1,), (4, 6, 2), (5, 7, 3))
        from_z = [partner(sums, "strip", bits) for bits in (4, 6, 2)]
        *from_z, near = lax.optimization_barrier((*from_z, partner(sums, "strip", 1)))
        held = pl.pallas_call(
            join_kernel,
            out_shape=jax.ShapeDtypeStruct((3 * carried, width_part), jnp.int16),
            in_specs=[vmem] * 3,
            out_specs=vmem,
            compiler_params=small,
            name="join",
        )(*from_z)
        held, blocks = lax.optimization_barrier((held, blocks))
        sent = [sums, near, held, partner(held, "strip", 1)]
    else:
        orders, sent = (), [lax.all_gather(sums, "strip", axis=0)]
    pairs, look, share = pl.pallas_call(
        functools.partial(tables_kernel, (depth, tiles, parts, carried)),
        out_shape=(
            jax.ShapeDtypeStruct((width // LANES, LANES, 2 * LANES), bf16),
            jax.ShapeDtypeStruct((2 * LANES, pins), bf16),
            jax.ShapeDtypeStruct((LANES // 2 + 8, pins), f32),
        ),
        in_specs=[vmem] * 4,
        out_specs=(vmem,) * 3,
        compiler_params=small,
        cost_estimate=pl.CostEstimate(flops=1 << 20, bytes_accessed=1 << 21, transcendentals=0),
        name="tables",
    )(blocks, rows, cols, pin_fracs)

    final, velocity = pl.pallas_call(
        functools.partial(field_kernel, (depth, tiles, parts, strips), orders),
        out_shape=(
            jax.ShapeDtypeStruct((depth, width_part), f32),
            jax.ShapeDtypeStruct((2, pins), f32),
        ),
        in_specs=[vmem] * (4 + len(sent)),
        out_specs=(vmem, vmem),
        scratch_shapes=[
            pltpu.VMEM((height, width), f32),
            pltpu.VMEM((height, width), f32),
            pltpu.VMEM((height + 16, width), f32),
            pltpu.VMEM((strips if len(sent) > 1 else 1, carried, width_part), jnp.int16),
        ],
        compiler_params=large,
        name="field",
    )(pairs, look, share, col_blocks, *sent)
    return final, velocity


def solution(mesh):
    placed = (
        P(("strip", "cells")),
        P(("strip", "cells")),
        P(None, ("strip", "cells")),
        P(("strip", "cells")),
        P("strip", "cells"),
        P("strip", "cells"),
        P("cells", None, None),
        P(),
    )
    return jax.shard_map(
        local,
        mesh=mesh,
        in_specs=placed,
        out_specs=(P("strip", "cells"), P(None, ("strip", "cells"))),
        check_vma=False,
    )
```

```python
import functools

import jax
import jax.numpy as jnp
from jax import lax
from jax.experimental import pallas as pl
from jax.experimental.pallas import tpu as pltpu
from jax.sharding import PartitionSpec as P

SWEEPS = 3
STEPS = 2
LANES = 128
GROUP = 8

coupling = 2.0
floor_level = 0.5
block_low, block_span = -0.002, 0.152
weight_low, weight_span = 0.5, 3.5
term_low, term_octaves = -24.0, 40.0
code_top = 65535.0
code_half = 32768.0
log_two = 0.6931471805599453

f32 = jnp.float32
bf16 = jnp.bfloat16


def iota(shape, axis):
    return lax.broadcasted_iota(jnp.int32, shape, axis)


def halves(values):
    high = values.astype(bf16)
    return high, (values - high.astype(f32)).astype(bf16)


def last_dims(left, right):
    return lax.dot_general(left, right, (((1,), (1,)), ((), ())), preferred_element_type=f32)


def pick(index, first, near, far):
    return jnp.where(index == first, near, jnp.where(index == first + 1, far, 0.0))


def rounded(values):
    return values.astype(bf16).astype(f32)


def coded(share):
    return jnp.clip(jnp.round(share * code_top), 0.0, code_top) - code_half


def stored(codes):
    return codes.astype(jnp.int32).astype(jnp.int16)


def density_codes(values):
    octave = jnp.log(jnp.maximum(values, 2.0**-40)) * (1.0 / log_two)
    return stored(coded((octave - term_low) * (1.0 / term_octaves)))


def densities(codes):
    codes = codes.astype(f32)
    octave = (codes + code_half) * (term_octaves / code_top) + term_low
    return jnp.where(codes == -code_half, 0.0, jnp.exp(octave * log_two))


def splat_kernel(
    tiles, parts, rows_in, cols_in, fracs_in, pin_weights_in, row_blocks_in, cap_in, block_in, out_ref,
    rows_ref, cols_ref, fracs_ref, pin_weights_ref, row_blocks_ref, cap_ref, block_ref, arrived,
):
    depth = cap_ref.shape[0]
    height = parts * depth
    sources = (rows_in, cols_in, fracs_in, pin_weights_in, row_blocks_in, cap_in, block_in)
    places = (rows_ref, cols_ref, fracs_ref, pin_weights_ref, row_blocks_ref, cap_ref, block_ref)
    copies = [
        pltpu.make_async_copy(source, place, arrived.at[n]) for n, (source, place) in enumerate(zip(sources, places))
    ]
    for copy in copies:
        copy.start()
    for copy in copies[:4]:
        copy.wait()
    rows, cols, sizes = rows_ref[...], cols_ref[...], pin_weights_ref[...]
    place = iota((height * (tiles + 1), LANES), 0)
    group, inner = place // height, place % height
    keys = ((inner // depth) * tiles + group - 1) * depth + inner % depth
    lane = iota((LANES + 8, LANES), 0)
    tables, lanes = [], []
    for j in range(rows.shape[0]):
        cut = slice(j * LANES, (j + 1) * LANES)
        fy, fx = fracs_ref[0:1, cut], fracs_ref[1:2, cut]
        size, col = sizes[j : j + 1], cols[j : j + 1]
        key = (col >> 7) * depth + rows[j : j + 1]
        tables.append(pick(keys, key, rounded(size * (1.0 - fy)), rounded(size * fy)).astype(bf16))
        lanes.append(pick(lane, col & 127, rounded(1.0 - fx), rounded(fx)).astype(bf16))
    total = last_dims(jnp.concatenate(tables, 1), jnp.concatenate(lanes, 1))
    for copy in copies[4:]:
        copy.wait()
    first_lane = iota((height, LANES), 1) == 0
    for t in range(tiles):
        own = total[(t + 1) * height : (t + 2) * height, :LANES]
        spill = total[t * height : (t + 1) * height, LANES : LANES + 1]
        own = own + jnp.where(first_lane, spill, 0.0)
        cut = slice(t * LANES, (t + 1) * LANES)
        out_ref[:height, cut] = density_codes(own)
        share = (row_blocks_ref[t * LANES : (t + 1) * LANES, :] - block_low) * (1.0 / block_span)
        out_ref[2 * height :, cut] = stored(coded(share))
    weights = cap_ref[...].astype(f32) * (1.0 - block_ref[...])
    code = coded((weights - weight_low) * (1.0 / weight_span))
    row = iota((height, weights.shape[1]), 0)
    mine = row // depth == lax.axis_index("cells")
    out_ref[height : 2 * height, :] = stored(jnp.where(mine, jnp.concatenate([code] * parts, 0), 0.0))


def sum_kernel(*refs):
    sent_refs, out_ref = refs[:-1], refs[-1]
    height = out_ref.shape[0] // 2
    terms, codes = 0.0, 0.0
    for sent_ref in sent_refs:
        terms += densities(sent_ref[:height, :])
        codes += sent_ref[height:, :].astype(f32)
    out_ref[:height, :] = density_codes(terms)
    out_ref[height:, :] = stored(codes)


def beside(values):
    width = values.shape[1]
    lane = iota((values.shape[0], LANES), 1)
    left, right = pltpu.roll(values, 1, 1), pltpu.roll(values, width - 1, 1)
    first = jnp.where(lane == 0, values[:, :LANES], left[:, :LANES])
    last = jnp.where(lane == LANES - 1, values[:, width - LANES :], right[:, width - LANES :])
    return (
        jnp.concatenate([first, left[:, LANES:]], 1),
        jnp.concatenate([right[:, : width - LANES], last], 1),
    )


class Turned:
    def __init__(self, tiles):
        self.tiles, self.turned = tiles, {}

    def turn(self, t, shift):
        if (t, shift) not in self.turned:
            self.turned[t, shift] = pltpu.roll(self.tiles[t], shift, 1)
        return self.turned[t, shift]

    def along(self, t):
        mine, back = self.tiles[t], LANES - 1
        lane = iota(mine.shape, 1)
        before = self.turn(t - 1, 1) if t else mine
        after = self.turn(t + 1, back) if t + 1 < len(self.tiles) else mine
        left = jnp.where(lane == 0, before, self.turn(t, 1))
        right = jnp.where(lane == back, after, self.turn(t, back))
        return 2.0 * mine - left - right


def delayed(count, first, second, delay=2):
    waiting, results = [], []
    for t in range(count + delay):
        if t < count:
            waiting.append(first(t))
        if t >= delay:
            results.append(second(t - delay, waiting[t - delay]))
            waiting[t - delay] = None
    return results


def across_lines(values):
    height = values.shape[0]
    row = iota((8, values.shape[1]), 0)
    above, below = pltpu.roll(values, 1, 0), pltpu.roll(values, height - 1, 0)
    first = jnp.where(row == 0, values[:8], above[:8])
    last = jnp.where(row == 7, values[height - 8 :], below[height - 8 :])
    above = jnp.concatenate([first, above[8:]], 0)
    below = jnp.concatenate([below[: height - 8], last], 0)
    return 2.0 * values - above - below


def col_products(residual, blocks):
    high, low = halves(residual)
    size = blocks[0].shape[0] // 2
    dot = functools.partial(jnp.dot, preferred_element_type=f32)
    cuts = [slice(k * size, (k + 1) * size) for k in range(len(blocks))]
    return [(dot(pair, high[cut]), dot(pair[:size], low[cut])) for pair, cut in zip(blocks, cuts)]


def col_sum(products):
    size = products[0][1].shape[0]
    result = [both[:size] + (both[size:] + rest) for both, rest in products]
    return result[0] if len(result) == 1 else jnp.concatenate(result, 0)


def each(count, body):
    if count == 1:
        body(0)
    else:
        pl.loop(0, count)(body)


def join_kernel(*refs):
    for n, ref in enumerate(refs[:-1]):
        refs[-1][n * ref.shape[0] : (n + 1) * ref.shape[0], :] = ref[...]


def tables_kernel(sizes, codes_ref, rows_ref, cols_ref, fracs_ref, pairs_ref, look_ref, share_ref):
    depth, tiles, parts, carried = sizes
    for k in range(pairs_ref.shape[0]):
        base = (k // tiles) * (carried + LANES) + carried
        code = codes_ref[base : base + LANES, k % tiles * LANES : (k % tiles + 1) * LANES].astype(f32)
        high, low = halves(((code + code_half) * (block_span / code_top) + block_low).T)
        pairs_ref[k, :, :LANES] = high
        pairs_ref[k, :, LANES:] = low
    half = LANES // 2
    many = parts * tiles * depth
    rows, cols = rows_ref[...], cols_ref[...]
    blank = jnp.zeros((LANES - many, LANES), bf16)
    keys, lane = iota((many, LANES), 0), iota((half + 8, LANES), 0)
    for j in range(rows.shape[0]):
        cut = slice(j * LANES, (j + 1) * LANES)
        fy, fx = fracs_ref[0:1, cut], fracs_ref[1:2, cut]
        col = cols[j : j + 1]
        key = (col >> 7) * depth + rows[j : j + 1]
        second = (col & half) != 0
        near, far = rounded(1.0 - fy), rounded(fy)
        looks = [
            pick(keys, jnp.where(second, -8, key), near, far).astype(bf16),
            blank,
            pick(keys, jnp.where(second, key, -8), near, far).astype(bf16),
            blank,
        ]
        look_ref[:, cut] = jnp.concatenate(looks, 0)
        share_ref[:, cut] = pick(lane, col & (half - 1), rounded(1.0 - fx), rounded(fx))


def field_kernel(
    sizes, orders, pairs, look_ref, share_ref, col_blocks_ref, *refs,
):
    depth, tiles, parts, strips = sizes
    sent_refs, (final_ref, velocity_ref, weights_ref, source_ref, field_ref, ordered) = refs[:-6], refs[-6:]
    width_part = tiles * LANES
    width = parts * width_part
    height = strips * depth
    chunk = min(GROUP, strips) * depth
    chunks = height // chunk
    strip, part = lax.axis_index("strip"), lax.axis_index("cells")

    slots = parts * depth
    if len(sent_refs) == 1:
        sent = sent_refs[0]
    else:
        sent = ordered
        for order, sent_ref in zip(orders, sent_refs):
            for n, bits in enumerate(order):
                ordered[strip ^ bits] = sent_ref[n * 2 * slots : (n + 1) * 2 * slots, :]
    group = chunk // depth
    target, origin = iota((parts * chunk, group * slots), 0), iota((parts * chunk, group * slots), 1)
    slot = origin % slots
    fits = (slot // depth == target // chunk) & (origin // slots * depth + slot % depth == target % chunk)
    chosen = jnp.where(fits, 1.0, 0.0).astype(bf16)

    def placed(values):
        high, low = halves(jnp.concatenate(values, 0))
        dot = functools.partial(jnp.dot, preferred_element_type=f32)
        return dot(chosen, high) + dot(chosen, low)

    @functools.partial(each, chunks)
    def place(g):
        terms, codes = [], []
        for n in range(group):
            got = sent[g * group + n]
            terms.append(densities(got[:slots]))
            codes.append(got[slots:].astype(f32))
        term = placed(terms)
        weight = (placed(codes) + code_half) * (weight_span / code_top) + weight_low
        here = pl.ds(pl.multiple_of(g * chunk, chunk), chunk)
        for p in range(parts):
            cut = slice(p * width_part, (p + 1) * width_part)
            weights_ref[here, cut] = weight[p * chunk : (p + 1) * chunk]
            source_ref[here, cut] = term[p * chunk : (p + 1) * chunk] / weight[p * chunk : (p + 1) * chunk]

    col_blocks = [jnp.concatenate(halves(col_blocks_ref[k]), 0) for k in range(col_blocks_ref.shape[0])]
    inner = pl.ds(8, height)
    lanes_at_once = 2 * LANES if chunks == 1 and width % (2 * LANES) == 0 else LANES
    at_once = width // lanes_at_once if chunks == 1 else 1

    def cuts_of(g):
        if at_once > 1:
            return [slice(n * lanes_at_once, (n + 1) * lanes_at_once) for n in range(at_once)]
        return [pl.ds(pl.multiple_of(g * lanes_at_once, lanes_at_once), lanes_at_once)]

    col_steps = width // lanes_at_once // at_once

    @functools.partial(each, col_steps)
    def start(g):
        for cut in cuts_of(g):
            current = source_ref[:, cut]
            field_ref[inner, cut] = current
            source_ref[:, cut] = weights_ref[:, cut] * current - coupling * across_lines(current)

    row_tiles = [slice(t * LANES, (t + 1) * LANES) for t in range(width // LANES)]
    for step in range(STEPS):

        @functools.partial(each, chunks)
        def solve_rows(g):
            here = pl.ds(pl.multiple_of(g * chunk, chunk), chunk)
            there = pl.ds(pl.multiple_of(g * chunk + 8, 8), chunk)
            current = [field_ref[there, cut] for cut in row_tiles]
            for sweep in range(SWEEPS):
                turned = Turned(current)

                def multiply(t):
                    cut = row_tiles[t]
                    now = weights_ref[here, cut] * turned.tiles[t] + coupling * turned.along(t)
                    both = jnp.concatenate(halves(source_ref[here, cut] - now), 0)
                    return jnp.dot(both, pairs[t], preferred_element_type=f32)

                def add(t, product):
                    high, low = product[:chunk], product[chunk:]
                    return turned.tiles[t] + (high[:, :LANES] + (high[:, LANES:] + low[:, :LANES]))

                current = delayed(len(current), multiply, add)
            turned = Turned(current)
            for t, cut in enumerate(row_tiles):
                field_ref[there, cut] = current[t]
                source_ref[here, cut] = weights_ref[here, cut] * current[t] - coupling * turned.along(t)

        @functools.partial(each, col_steps)
        def solve_cols(g):
            cuts = cuts_of(g)
            current = [field_ref[inner, cut] for cut in cuts]
            for sweep in range(SWEEPS):
                before = current

                def multiply(n):
                    now = weights_ref[:, cuts[n]] * before[n] + coupling * across_lines(before[n])
                    return col_products(source_ref[:, cuts[n]] - now, col_blocks)

                current = delayed(len(cuts), multiply, lambda n, products: before[n] + col_sum(products))
            for now, cut in zip(current, cuts):
                field_ref[inner, cut] = now
                if step + 1 < STEPS:
                    source_ref[:, cut] = weights_ref[:, cut] * now - coupling * across_lines(now)
                else:
                    field_ref[:8, cut] = jnp.broadcast_to(now[:1], (8, lanes_at_once))
                    field_ref[height + 8 :, cut] = jnp.broadcast_to(now[-1:], (8, lanes_at_once))

    row0 = strip * depth
    columns = pl.ds(pl.multiple_of(part * width_part, LANES), width_part)
    base, shift = pl.multiple_of(row0 // 8 * 8, 8), 17 - row0 % 8
    final_ref[...] = pltpu.roll(field_ref[pl.ds(base, 24), columns], shift, 0)[1 : 1 + depth]

    window = pltpu.roll(field_ref[pl.ds(base, 24), :], shift, 0)
    above, centre, below = window[:8], pltpu.roll(window, 23, 0)[:8], pltpu.roll(window, 22, 0)[:8]
    left, right = beside(centre)
    scale = jnp.maximum(centre, floor_level)
    velocity_y = rounded(-(0.5 * (below - above)) / scale)
    velocity_x = rounded(-(0.5 * (right - left)) / scale)

    upper = iota((8, LANES), 0) < depth

    def stacked(values):
        stack = []
        for t in range(0, parts * tiles, 2):
            even = values[:, t * LANES : (t + 1) * LANES]
            odd = values[:, (t + 1) * LANES : (t + 2) * LANES]
            stack.append(jnp.where(upper, even, pltpu.roll(odd, depth, 0)))
        return jnp.concatenate(stack, 0)

    half = LANES // 2

    def table_of(values):
        stack = stacked(values)
        many = stack.shape[0]
        blank = jnp.zeros((LANES - many, LANES), f32)
        turned = jnp.concatenate([stack, blank], 0).T
        after = jnp.concatenate([pltpu.roll(stack, many - depth, 0), blank], 0).T[:8]
        return jnp.concatenate([turned[: half + 8], jnp.concatenate([turned[half:], after], 0)], 1)

    table = jnp.concatenate([table_of(velocity_y), table_of(velocity_x)], 0).astype(bf16)
    pins = share_ref.shape[1]
    at_once = 2 * LANES if pins % (2 * LANES) == 0 else LANES
    for j in range(0, pins, at_once):
        cut = slice(j, j + at_once)
        sampled = jnp.dot(table, look_ref[:, cut], preferred_element_type=f32)
        share = share_ref[:, cut]
        velocity_ref[0:1, cut] = jnp.sum(sampled[: half + 8] * share, 0, keepdims=True)
        velocity_ref[1:2, cut] = jnp.sum(sampled[half + 8 :] * share, 0, keepdims=True)


def partner(values, axis, bits):
    return lax.ppermute(values, axis, [(n, n ^ bits) for n in range(lax.axis_size(axis))])


def local(pin_rows, pin_cols, pin_fracs, pin_weights, capacity, blockage, row_blocks, col_blocks):
    depth, width_part = capacity.shape
    parts, strips = lax.axis_size("cells"), lax.axis_size("strip")
    tiles = width_part // LANES
    height, width = depth * strips, width_part * parts
    pins = pin_rows.shape[0]
    by_lane = (pins // LANES, LANES)
    rows, cols = pin_rows.reshape(by_lane), pin_cols.reshape(by_lane)
    sizes = pin_weights.reshape(by_lane)
    vmem = pl.BlockSpec(memory_space=pltpu.VMEM)
    whole = pltpu.CompilerParams(vmem_limit_bytes=60 << 20)
    small = pltpu.CompilerParams(vmem_limit_bytes=16 * 1024 * 1024)
    grid_bytes = 4 * height * width
    large = pltpu.CompilerParams(vmem_limit_bytes=(20 << 20) + 6 * grid_bytes)

    carried = 2 * parts * depth
    read = (rows, cols, pin_fracs, sizes, row_blocks.reshape(-1, LANES), capacity, blockage)
    terms = pl.pallas_call(
        functools.partial(splat_kernel, tiles, parts),
        out_shape=jax.ShapeDtypeStruct((carried + LANES, width_part), jnp.int16),
        in_specs=[pl.BlockSpec(memory_space=pltpu.HBM)] * 7,
        out_specs=vmem,
        scratch_shapes=[pltpu.VMEM(item.shape, item.dtype) for item in read] + [pltpu.SemaphoreType.DMA((7,))],
        compiler_params=whole,
        name="splat",
    )(*read)
    blocks = lax.all_gather(terms, "cells", axis=0, tiled=True)

    def terms_of(part):
        place = part * (carried + LANES) // carried
        return pl.BlockSpec((carried, width_part), lambda i: (place, 0))

    sums = pl.pallas_call(
        sum_kernel,
        grid=(1,),
        out_shape=jax.ShapeDtypeStruct((carried, width_part), jnp.int16),
        in_specs=[terms_of(part) for part in range(parts)],
        out_specs=pl.BlockSpec((carried, width_part), lambda i: (0, 0)),
        compiler_params=small,
        name="sum_terms",
    )(*[blocks] * parts)
    if strips == 8:
        orders = ((0,), (1,), (4, 6, 2), (5, 7, 3))
        from_z = [partner(sums, "strip", bits) for bits in (4, 6, 2)]
        *from_z, near = lax.optimization_barrier((*from_z, partner(sums, "strip", 1)))
        held = pl.pallas_call(
            join_kernel,
            out_shape=jax.ShapeDtypeStruct((3 * carried, width_part), jnp.int16),
            in_specs=[vmem] * 3,
            out_specs=vmem,
            compiler_params=small,
            name="join",
        )(*from_z)
        held, blocks = lax.optimization_barrier((held, blocks))
        sent = [sums, near, held, partner(held, "strip", 1)]
    else:
        orders, sent = (), [lax.all_gather(sums, "strip", axis=0)]
    pairs, look, share = pl.pallas_call(
        functools.partial(tables_kernel, (depth, tiles, parts, carried)),
        out_shape=(
            jax.ShapeDtypeStruct((width // LANES, LANES, 2 * LANES), bf16),
            jax.ShapeDtypeStruct((2 * LANES, pins), bf16),
            jax.ShapeDtypeStruct((LANES // 2 + 8, pins), f32),
        ),
        in_specs=[vmem] * 4,
        out_specs=(vmem,) * 3,
        compiler_params=small,
        cost_estimate=pl.CostEstimate(flops=1 << 20, bytes_accessed=1 << 21, transcendentals=0),
        name="tables",
    )(blocks, rows, cols, pin_fracs)

    final, velocity = pl.pallas_call(
        functools.partial(field_kernel, (depth, tiles, parts, strips), orders),
        out_shape=(
            jax.ShapeDtypeStruct((depth, width_part), f32),
            jax.ShapeDtypeStruct((2, pins), f32),
        ),
        in_specs=[vmem] * (4 + len(sent)),
        out_specs=(vmem, vmem),
        scratch_shapes=[
            pltpu.VMEM((height, width), f32),
            pltpu.VMEM((height, width), f32),
            pltpu.VMEM((height + 16, width), f32),
            pltpu.VMEM((strips if len(sent) > 1 else 1, carried, width_part), jnp.int16),
        ],
        compiler_params=large,
        name="field",
    )(pairs, look, share, col_blocks, *sent)
    return final, velocity


def solution(mesh):
    placed = (
        P(("strip", "cells")),
        P(("strip", "cells")),
        P(None, ("strip", "cells")),
        P(("strip", "cells")),
        P("strip", "cells"),
        P("strip", "cells"),
        P("cells", None, None),
        P(),
    )
    return jax.shard_map(
        local,
        mesh=mesh,
        in_specs=placed,
        out_specs=(P("strip", "cells"), P(None, ("strip", "cells"))),
        check_vma=False,
    )
```

```python
import functools

import jax
import jax.numpy as jnp
from jax import lax
from jax.experimental import pallas as pl
from jax.experimental.pallas import tpu as pltpu
from jax.sharding import PartitionSpec as P

SWEEPS = 3
STEPS = 2
LANES = 128
GROUP = 8

coupling = 2.0
floor_level = 0.5
block_low, block_span = -0.002, 0.152
weight_low, weight_span = 0.5, 3.5
term_low, term_octaves = -24.0, 40.0
code_top = 65535.0
code_half = 32768.0
log_two = 0.6931471805599453

f32 = jnp.float32
bf16 = jnp.bfloat16


def iota(shape, axis):
    return lax.broadcasted_iota(jnp.int32, shape, axis)


def halves(values):
    high = values.astype(bf16)
    return high, (values - high.astype(f32)).astype(bf16)


def last_dims(left, right):
    return lax.dot_general(left, right, (((1,), (1,)), ((), ())), preferred_element_type=f32)


def pick(index, first, near, far):
    return jnp.where(index == first, near, jnp.where(index == first + 1, far, 0.0))


def rounded(values):
    return values.astype(bf16).astype(f32)


def coded(share):
    return jnp.clip(jnp.round(share * code_top), 0.0, code_top) - code_half


def stored(codes):
    return codes.astype(jnp.int32).astype(jnp.int16)


def density_codes(values):
    octave = jnp.log(jnp.maximum(values, 2.0**-40)) * (1.0 / log_two)
    return stored(coded((octave - term_low) * (1.0 / term_octaves)))


def densities(codes):
    codes = codes.astype(f32)
    octave = (codes + code_half) * (term_octaves / code_top) + term_low
    return jnp.where(codes == -code_half, 0.0, jnp.exp(octave * log_two))


def splat_kernel(
    tiles, parts, rows_in, cols_in, fracs_in, pin_weights_in, row_blocks_in, cap_in, block_in, out_ref,
    rows_ref, cols_ref, fracs_ref, pin_weights_ref, row_blocks_ref, cap_ref, block_ref, arrived,
):
    depth = cap_ref.shape[0]
    height = parts * depth
    sources = (rows_in, cols_in, fracs_in, pin_weights_in, row_blocks_in, cap_in, block_in)
    places = (rows_ref, cols_ref, fracs_ref, pin_weights_ref, row_blocks_ref, cap_ref, block_ref)
    copies = [
        pltpu.make_async_copy(source, place, arrived.at[n]) for n, (source, place) in enumerate(zip(sources, places))
    ]
    for copy in copies:
        copy.start()
    for copy in copies[:4]:
        copy.wait()
    rows, cols, sizes = rows_ref[...], cols_ref[...], pin_weights_ref[...]
    place = iota((height * (tiles + 1), LANES), 0)
    group, inner = place // height, place % height
    keys = ((inner // depth) * tiles + group - 1) * depth + inner % depth
    lane = iota((LANES + 8, LANES), 0)
    tables, lanes = [], []
    for j in range(rows.shape[0]):
        cut = slice(j * LANES, (j + 1) * LANES)
        fy, fx = fracs_ref[0:1, cut], fracs_ref[1:2, cut]
        size, col = sizes[j : j + 1], cols[j : j + 1]
        key = (col >> 7) * depth + rows[j : j + 1]
        tables.append(pick(keys, key, rounded(size * (1.0 - fy)), rounded(size * fy)).astype(bf16))
        lanes.append(pick(lane, col & 127, rounded(1.0 - fx), rounded(fx)).astype(bf16))
    total = last_dims(jnp.concatenate(tables, 1), jnp.concatenate(lanes, 1))
    for copy in copies[4:]:
        copy.wait()
    first_lane = iota((height, LANES), 1) == 0
    for t in range(tiles):
        own = total[(t + 1) * height : (t + 2) * height, :LANES]
        spill = total[t * height : (t + 1) * height, LANES : LANES + 1]
        own = own + jnp.where(first_lane, spill, 0.0)
        cut = slice(t * LANES, (t + 1) * LANES)
        out_ref[:height, cut] = density_codes(own)
        share = (row_blocks_ref[t * LANES : (t + 1) * LANES, :] - block_low) * (1.0 / block_span)
        out_ref[2 * height :, cut] = stored(coded(share))
    weights = cap_ref[...].astype(f32) * (1.0 - block_ref[...])
    code = coded((weights - weight_low) * (1.0 / weight_span))
    row = iota((height, weights.shape[1]), 0)
    mine = row // depth == lax.axis_index("cells")
    out_ref[height : 2 * height, :] = stored(jnp.where(mine, jnp.concatenate([code] * parts, 0), 0.0))


def sum_kernel(*refs):
    sent_refs, out_ref = refs[:-1], refs[-1]
    height = out_ref.shape[0] // 2
    terms, codes = 0.0, 0.0
    for sent_ref in sent_refs:
        terms += densities(sent_ref[:height, :])
        codes += sent_ref[height:, :].astype(f32)
    out_ref[:height, :] = density_codes(terms)
    out_ref[height:, :] = stored(codes)


def beside(values):
    width = values.shape[1]
    lane = iota((values.shape[0], LANES), 1)
    left, right = pltpu.roll(values, 1, 1), pltpu.roll(values, width - 1, 1)
    first = jnp.where(lane == 0, values[:, :LANES], left[:, :LANES])
    last = jnp.where(lane == LANES - 1, values[:, width - LANES :], right[:, width - LANES :])
    return (
        jnp.concatenate([first, left[:, LANES:]], 1),
        jnp.concatenate([right[:, : width - LANES], last], 1),
    )


class Turned:
    def __init__(self, tiles):
        self.tiles, self.turned = tiles, {}

    def turn(self, t, shift):
        if (t, shift) not in self.turned:
            self.turned[t, shift] = pltpu.roll(self.tiles[t], shift, 1)
        return self.turned[t, shift]

    def along(self, t):
        mine, back = self.tiles[t], LANES - 1
        lane = iota(mine.shape, 1)
        before = self.turn(t - 1, 1) if t else mine
        after = self.turn(t + 1, back) if t + 1 < len(self.tiles) else mine
        left = jnp.where(lane == 0, before, self.turn(t, 1))
        right = jnp.where(lane == back, after, self.turn(t, back))
        return 2.0 * mine - left - right


def delayed(count, first, second, delay=5):
    waiting, results = [], []
    for t in range(count + delay):
        if t < count:
            waiting.append(first(t))
        if t >= delay:
            results.append(second(t - delay, waiting[t - delay]))
            waiting[t - delay] = None
    return results


def across_lines(values):
    height = values.shape[0]
    row = iota((8, values.shape[1]), 0)
    above, below = pltpu.roll(values, 1, 0), pltpu.roll(values, height - 1, 0)
    first = jnp.where(row == 0, values[:8], above[:8])
    last = jnp.where(row == 7, values[height - 8 :], below[height - 8 :])
    above = jnp.concatenate([first, above[8:]], 0)
    below = jnp.concatenate([below[: height - 8], last], 0)
    return 2.0 * values - above - below


def col_products(residual, blocks):
    high, low = halves(residual)
    size = blocks[0].shape[0] // 2
    dot = functools.partial(jnp.dot, preferred_element_type=f32)
    cuts = [slice(k * size, (k + 1) * size) for k in range(len(blocks))]
    return [(dot(pair, high[cut]), dot(pair[:size], low[cut])) for pair, cut in zip(blocks, cuts)]


def col_sum(products):
    size = products[0][1].shape[0]
    result = [both[:size] + (both[size:] + rest) for both, rest in products]
    return result[0] if len(result) == 1 else jnp.concatenate(result, 0)


def each(count, body):
    if count == 1:
        body(0)
    else:
        pl.loop(0, count)(body)


def join_kernel(*refs):
    for n, ref in enumerate(refs[:-1]):
        refs[-1][n * ref.shape[0] : (n + 1) * ref.shape[0], :] = ref[...]


def tables_kernel(sizes, codes_ref, rows_ref, cols_ref, fracs_ref, pairs_ref, look_ref, share_ref):
    depth, tiles, parts, carried = sizes
    for k in range(pairs_ref.shape[0]):
        base = (k // tiles) * (carried + LANES) + carried
        code = codes_ref[base : base + LANES, k % tiles * LANES : (k % tiles + 1) * LANES].astype(f32)
        high, low = halves(((code + code_half) * (block_span / code_top) + block_low).T)
        pairs_ref[k, :, :LANES] = high
        pairs_ref[k, :, LANES:] = low
    half = LANES // 2
    many = parts * tiles * depth
    rows, cols = rows_ref[...], cols_ref[...]
    blank = jnp.zeros((LANES - many, LANES), bf16)
    keys, lane = iota((many, LANES), 0), iota((half + 8, LANES), 0)
    for j in range(rows.shape[0]):
        cut = slice(j * LANES, (j + 1) * LANES)
        fy, fx = fracs_ref[0:1, cut], fracs_ref[1:2, cut]
        col = cols[j : j + 1]
        key = (col >> 7) * depth + rows[j : j + 1]
        second = (col & half) != 0
        near, far = rounded(1.0 - fy), rounded(fy)
        looks = [
            pick(keys, jnp.where(second, -8, key), near, far).astype(bf16),
            blank,
            pick(keys, jnp.where(second, key, -8), near, far).astype(bf16),
            blank,
        ]
        look_ref[:, cut] = jnp.concatenate(looks, 0)
        share_ref[:, cut] = pick(lane, col & (half - 1), rounded(1.0 - fx), rounded(fx))


def field_kernel(
    sizes, orders, pairs, look_ref, share_ref, col_blocks_ref, *refs,
):
    depth, tiles, parts, strips = sizes
    sent_refs, (final_ref, velocity_ref, weights_ref, source_ref, field_ref, ordered) = refs[:-6], refs[-6:]
    width_part = tiles * LANES
    width = parts * width_part
    height = strips * depth
    chunk = min(GROUP, strips) * depth
    chunks = height // chunk
    strip, part = lax.axis_index("strip"), lax.axis_index("cells")

    slots = parts * depth
    if len(sent_refs) == 1:
        sent = sent_refs[0]
    else:
        sent = ordered
        for order, sent_ref in zip(orders, sent_refs):
            for n, bits in enumerate(order):
                ordered[strip ^ bits] = sent_ref[n * 2 * slots : (n + 1) * 2 * slots, :]
    group = chunk // depth
    target, origin = iota((parts * chunk, group * slots), 0), iota((parts * chunk, group * slots), 1)
    slot = origin % slots
    fits = (slot // depth == target // chunk) & (origin // slots * depth + slot % depth == target % chunk)
    chosen = jnp.where(fits, 1.0, 0.0).astype(bf16)

    def placed(values):
        high, low = halves(jnp.concatenate(values, 0))
        dot = functools.partial(jnp.dot, preferred_element_type=f32)
        return dot(chosen, high) + dot(chosen, low)

    @functools.partial(each, chunks)
    def place(g):
        terms, codes = [], []
        for n in range(group):
            got = sent[g * group + n]
            terms.append(densities(got[:slots]))
            codes.append(got[slots:].astype(f32))
        term = placed(terms)
        weight = (placed(codes) + code_half) * (weight_span / code_top) + weight_low
        here = pl.ds(pl.multiple_of(g * chunk, chunk), chunk)
        for p in range(parts):
            cut = slice(p * width_part, (p + 1) * width_part)
            weights_ref[here, cut] = weight[p * chunk : (p + 1) * chunk]
            source_ref[here, cut] = term[p * chunk : (p + 1) * chunk] / weight[p * chunk : (p + 1) * chunk]

    col_blocks = [jnp.concatenate(halves(col_blocks_ref[k]), 0) for k in range(col_blocks_ref.shape[0])]
    inner = pl.ds(8, height)
    lanes_at_once = 2 * LANES if chunks == 1 and width % (2 * LANES) == 0 else LANES
    at_once = width // lanes_at_once if chunks == 1 else 1

    def cuts_of(g):
        if at_once > 1:
            return [slice(n * lanes_at_once, (n + 1) * lanes_at_once) for n in range(at_once)]
        return [pl.ds(pl.multiple_of(g * lanes_at_once, lanes_at_once), lanes_at_once)]

    col_steps = width // lanes_at_once // at_once

    @functools.partial(each, col_steps)
    def start(g):
        for cut in cuts_of(g):
            current = source_ref[:, cut]
            field_ref[inner, cut] = current
            source_ref[:, cut] = weights_ref[:, cut] * current - coupling * across_lines(current)

    row_tiles = [slice(t * LANES, (t + 1) * LANES) for t in range(width // LANES)]
    for step in range(STEPS):

        @functools.partial(each, chunks)
        def solve_rows(g):
            here = pl.ds(pl.multiple_of(g * chunk, chunk), chunk)
            there = pl.ds(pl.multiple_of(g * chunk + 8, 8), chunk)
            current = [field_ref[there, cut] for cut in row_tiles]
            for sweep in range(SWEEPS):
                turned = Turned(current)

                def multiply(t):
                    cut = row_tiles[t]
                    now = weights_ref[here, cut] * turned.tiles[t] + coupling * turned.along(t)
                    both = jnp.concatenate(halves(source_ref[here, cut] - now), 0)
                    return jnp.dot(both, pairs[t], preferred_element_type=f32)

                def add(t, product):
                    high, low = product[:chunk], product[chunk:]
                    return turned.tiles[t] + (high[:, :LANES] + (high[:, LANES:] + low[:, :LANES]))

                current = delayed(len(current), multiply, add)
            turned = Turned(current)
            for t, cut in enumerate(row_tiles):
                field_ref[there, cut] = current[t]
                source_ref[here, cut] = weights_ref[here, cut] * current[t] - coupling * turned.along(t)

        @functools.partial(each, col_steps)
        def solve_cols(g):
            cuts = cuts_of(g)
            current = [field_ref[inner, cut] for cut in cuts]
            for sweep in range(SWEEPS):
                before = current

                def multiply(n):
                    now = weights_ref[:, cuts[n]] * before[n] + coupling * across_lines(before[n])
                    return col_products(source_ref[:, cuts[n]] - now, col_blocks)

                current = delayed(len(cuts), multiply, lambda n, products: before[n] + col_sum(products))
            for now, cut in zip(current, cuts):
                field_ref[inner, cut] = now
                if step + 1 < STEPS:
                    source_ref[:, cut] = weights_ref[:, cut] * now - coupling * across_lines(now)
                else:
                    field_ref[:8, cut] = jnp.broadcast_to(now[:1], (8, lanes_at_once))
                    field_ref[height + 8 :, cut] = jnp.broadcast_to(now[-1:], (8, lanes_at_once))

    row0 = strip * depth
    columns = pl.ds(pl.multiple_of(part * width_part, LANES), width_part)
    base, shift = pl.multiple_of(row0 // 8 * 8, 8), 17 - row0 % 8
    final_ref[...] = pltpu.roll(field_ref[pl.ds(base, 24), columns], shift, 0)[1 : 1 + depth]

    window = pltpu.roll(field_ref[pl.ds(base, 24), :], shift, 0)
    above, centre, below = window[:8], pltpu.roll(window, 23, 0)[:8], pltpu.roll(window, 22, 0)[:8]
    left, right = beside(centre)
    scale = jnp.maximum(centre, floor_level)
    velocity_y = rounded(-(0.5 * (below - above)) / scale)
    velocity_x = rounded(-(0.5 * (right - left)) / scale)

    upper = iota((8, LANES), 0) < depth

    def stacked(values):
        stack = []
        for t in range(0, parts * tiles, 2):
            even = values[:, t * LANES : (t + 1) * LANES]
            odd = values[:, (t + 1) * LANES : (t + 2) * LANES]
            stack.append(jnp.where(upper, even, pltpu.roll(odd, depth, 0)))
        return jnp.concatenate(stack, 0)

    half = LANES // 2

    def table_of(values):
        stack = stacked(values)
        many = stack.shape[0]
        blank = jnp.zeros((LANES - many, LANES), f32)
        turned = jnp.concatenate([stack, blank], 0).T
        after = jnp.concatenate([pltpu.roll(stack, many - depth, 0), blank], 0).T[:8]
        return jnp.concatenate([turned[: half + 8], jnp.concatenate([turned[half:], after], 0)], 1)

    table = jnp.concatenate([table_of(velocity_y), table_of(velocity_x)], 0).astype(bf16)
    pins = share_ref.shape[1]
    at_once = 2 * LANES if pins % (2 * LANES) == 0 else LANES
    for j in range(0, pins, at_once):
        cut = slice(j, j + at_once)
        sampled = jnp.dot(table, look_ref[:, cut], preferred_element_type=f32)
        share = share_ref[:, cut]
        velocity_ref[0:1, cut] = jnp.sum(sampled[: half + 8] * share, 0, keepdims=True)
        velocity_ref[1:2, cut] = jnp.sum(sampled[half + 8 :] * share, 0, keepdims=True)


def partner(values, axis, bits):
    return lax.ppermute(values, axis, [(n, n ^ bits) for n in range(lax.axis_size(axis))])


def local(pin_rows, pin_cols, pin_fracs, pin_weights, capacity, blockage, row_blocks, col_blocks):
    depth, width_part = capacity.shape
    parts, strips = lax.axis_size("cells"), lax.axis_size("strip")
    tiles = width_part // LANES
    height, width = depth * strips, width_part * parts
    pins = pin_rows.shape[0]
    by_lane = (pins // LANES, LANES)
    rows, cols = pin_rows.reshape(by_lane), pin_cols.reshape(by_lane)
    sizes = pin_weights.reshape(by_lane)
    vmem = pl.BlockSpec(memory_space=pltpu.VMEM)
    whole = pltpu.CompilerParams(vmem_limit_bytes=60 << 20)
    small = pltpu.CompilerParams(vmem_limit_bytes=16 * 1024 * 1024)
    grid_bytes = 4 * height * width
    large = pltpu.CompilerParams(vmem_limit_bytes=(20 << 20) + 6 * grid_bytes)

    carried = 2 * parts * depth
    read = (rows, cols, pin_fracs, sizes, row_blocks.reshape(-1, LANES), capacity, blockage)
    terms = pl.pallas_call(
        functools.partial(splat_kernel, tiles, parts),
        out_shape=jax.ShapeDtypeStruct((carried + LANES, width_part), jnp.int16),
        in_specs=[pl.BlockSpec(memory_space=pltpu.HBM)] * 7,
        out_specs=vmem,
        scratch_shapes=[pltpu.VMEM(item.shape, item.dtype) for item in read] + [pltpu.SemaphoreType.DMA((7,))],
        compiler_params=whole,
        name="splat",
    )(*read)
    blocks = lax.all_gather(terms, "cells", axis=0, tiled=True)

    def terms_of(part):
        place = part * (carried + LANES) // carried
        return pl.BlockSpec((carried, width_part), lambda i: (place, 0))

    sums = pl.pallas_call(
        sum_kernel,
        grid=(1,),
        out_shape=jax.ShapeDtypeStruct((carried, width_part), jnp.int16),
        in_specs=[terms_of(part) for part in range(parts)],
        out_specs=pl.BlockSpec((carried, width_part), lambda i: (0, 0)),
        compiler_params=small,
        name="sum_terms",
    )(*[blocks] * parts)
    if strips == 8:
        orders = ((0,), (1,), (4, 6, 2), (5, 7, 3))
        from_z = [partner(sums, "strip", bits) for bits in (4, 6, 2)]
        *from_z, near = lax.optimization_barrier((*from_z, partner(sums, "strip", 1)))
        held = pl.pallas_call(
            join_kernel,
            out_shape=jax.ShapeDtypeStruct((3 * carried, width_part), jnp.int16),
            in_specs=[vmem] * 3,
            out_specs=vmem,
            compiler_params=small,
            name="join",
        )(*from_z)
        held, blocks = lax.optimization_barrier((held, blocks))
        sent = [sums, near, held, partner(held, "strip", 1)]
    else:
        orders, sent = (), [lax.all_gather(sums, "strip", axis=0)]
    pairs, look, share = pl.pallas_call(
        functools.partial(tables_kernel, (depth, tiles, parts, carried)),
        out_shape=(
            jax.ShapeDtypeStruct((width // LANES, LANES, 2 * LANES), bf16),
            jax.ShapeDtypeStruct((2 * LANES, pins), bf16),
            jax.ShapeDtypeStruct((LANES // 2 + 8, pins), f32),
        ),
        in_specs=[vmem] * 4,
        out_specs=(vmem,) * 3,
        compiler_params=small,
        cost_estimate=pl.CostEstimate(flops=1 << 20, bytes_accessed=1 << 21, transcendentals=0),
        name="tables",
    )(blocks, rows, cols, pin_fracs)

    final, velocity = pl.pallas_call(
        functools.partial(field_kernel, (depth, tiles, parts, strips), orders),
        out_shape=(
            jax.ShapeDtypeStruct((depth, width_part), f32),
            jax.ShapeDtypeStruct((2, pins), f32),
        ),
        in_specs=[vmem] * (4 + len(sent)),
        out_specs=(vmem, vmem),
        scratch_shapes=[
            pltpu.VMEM((height, width), f32),
            pltpu.VMEM((height, width), f32),
            pltpu.VMEM((height + 16, width), f32),
            pltpu.VMEM((strips if len(sent) > 1 else 1, carried, width_part), jnp.int16),
        ],
        compiler_params=large,
        name="field",
    )(pairs, look, share, col_blocks, *sent)
    return final, velocity


def solution(mesh):
    placed = (
        P(("strip", "cells")),
        P(("strip", "cells")),
        P(None, ("strip", "cells")),
        P(("strip", "cells")),
        P("strip", "cells"),
        P("strip", "cells"),
        P("cells", None, None),
        P(),
    )
    return jax.shard_map(
        local,
        mesh=mesh,
        in_specs=placed,
        out_specs=(P("strip", "cells"), P(None, ("strip", "cells"))),
        check_vma=False,
    )
```

```python
import functools

import jax
import jax.numpy as jnp
from jax import lax
from jax.experimental import pallas as pl
from jax.experimental.pallas import tpu as pltpu
from jax.sharding import PartitionSpec as P

SWEEPS = 3
STEPS = 2
LANES = 128
GROUP = 8

coupling = 2.0
floor_level = 0.5
block_low, block_span = -0.002, 0.152
weight_low, weight_span = 0.5, 3.5
term_low, term_octaves = -24.0, 40.0
code_top = 65535.0
code_half = 32768.0
log_two = 0.6931471805599453

f32 = jnp.float32
bf16 = jnp.bfloat16


def iota(shape, axis):
    return lax.broadcasted_iota(jnp.int32, shape, axis)


def halves(values):
    high = values.astype(bf16)
    return high, (values - high.astype(f32)).astype(bf16)


def last_dims(left, right):
    return lax.dot_general(left, right, (((1,), (1,)), ((), ())), preferred_element_type=f32)


def pick(index, first, near, far):
    return jnp.where(index == first, near, jnp.where(index == first + 1, far, 0.0))


def rounded(values):
    return values.astype(bf16).astype(f32)


def coded(share):
    return jnp.clip(jnp.round(share * code_top), 0.0, code_top) - code_half


def stored(codes):
    return codes.astype(jnp.int32).astype(jnp.int16)


def density_codes(values):
    octave = jnp.log(jnp.maximum(values, 2.0**-40)) * (1.0 / log_two)
    return stored(coded((octave - term_low) * (1.0 / term_octaves)))


def densities(codes):
    codes = codes.astype(f32)
    octave = (codes + code_half) * (term_octaves / code_top) + term_low
    return jnp.where(codes == -code_half, 0.0, jnp.exp(octave * log_two))


def splat_kernel(
    tiles, parts, rows_in, cols_in, fracs_in, pin_weights_in, row_blocks_in, cap_in, block_in, out_ref,
    rows_ref, cols_ref, fracs_ref, pin_weights_ref, row_blocks_ref, cap_ref, block_ref, arrived,
):
    depth = cap_ref.shape[0]
    height = parts * depth
    sources = (rows_in, cols_in, fracs_in, pin_weights_in, row_blocks_in, cap_in, block_in)
    places = (rows_ref, cols_ref, fracs_ref, pin_weights_ref, row_blocks_ref, cap_ref, block_ref)
    copies = [
        pltpu.make_async_copy(source, place, arrived.at[n]) for n, (source, place) in enumerate(zip(sources, places))
    ]
    for copy in copies:
        copy.start()
    for copy in copies[:4]:
        copy.wait()
    rows, cols, sizes = rows_ref[...], cols_ref[...], pin_weights_ref[...]
    place = iota((height * (tiles + 1), LANES), 0)
    group, inner = place // height, place % height
    keys = ((inner // depth) * tiles + group - 1) * depth + inner % depth
    lane = iota((LANES + 8, LANES), 0)
    tables, lanes = [], []
    for j in range(rows.shape[0]):
        cut = slice(j * LANES, (j + 1) * LANES)
        fy, fx = fracs_ref[0:1, cut], fracs_ref[1:2, cut]
        size, col = sizes[j : j + 1], cols[j : j + 1]
        key = (col >> 7) * depth + rows[j : j + 1]
        tables.append(pick(keys, key, rounded(size * (1.0 - fy)), rounded(size * fy)).astype(bf16))
        lanes.append(pick(lane, col & 127, rounded(1.0 - fx), rounded(fx)).astype(bf16))
    total = last_dims(jnp.concatenate(tables, 1), jnp.concatenate(lanes, 1))
    for copy in copies[4:]:
        copy.wait()
    first_lane = iota((height, LANES), 1) == 0
    for t in range(tiles):
        own = total[(t + 1) * height : (t + 2) * height, :LANES]
        spill = total[t * height : (t + 1) * height, LANES : LANES + 1]
        own = own + jnp.where(first_lane, spill, 0.0)
        cut = slice(t * LANES, (t + 1) * LANES)
        out_ref[:height, cut] = density_codes(own)
        share = (row_blocks_ref[t * LANES : (t + 1) * LANES, :] - block_low) * (1.0 / block_span)
        out_ref[2 * height :, cut] = stored(coded(share))
    weights = cap_ref[...].astype(f32) * (1.0 - block_ref[...])
    code = coded((weights - weight_low) * (1.0 / weight_span))
    row = iota((height, weights.shape[1]), 0)
    mine = row // depth == lax.axis_index("cells")
    out_ref[height : 2 * height, :] = stored(jnp.where(mine, jnp.concatenate([code] * parts, 0), 0.0))


def sum_kernel(*refs):
    sent_refs, out_ref = refs[:-1], refs[-1]
    height = out_ref.shape[0] // 2
    terms, codes = 0.0, 0.0
    for sent_ref in sent_refs:
        terms += densities(sent_ref[:height, :])
        codes += sent_ref[height:, :].astype(f32)
    out_ref[:height, :] = density_codes(terms)
    out_ref[height:, :] = stored(codes)


def beside(values):
    width = values.shape[1]
    lane = iota((values.shape[0], LANES), 1)
    left, right = pltpu.roll(values, 1, 1), pltpu.roll(values, width - 1, 1)
    first = jnp.where(lane == 0, values[:, :LANES], left[:, :LANES])
    last = jnp.where(lane == LANES - 1, values[:, width - LANES :], right[:, width - LANES :])
    return (
        jnp.concatenate([first, left[:, LANES:]], 1),
        jnp.concatenate([right[:, : width - LANES], last], 1),
    )


class Turned:
    def __init__(self, tiles):
        self.tiles, self.turned = tiles, {}

    def turn(self, t, shift):
        if (t, shift) not in self.turned:
            self.turned[t, shift] = pltpu.roll(self.tiles[t], shift, 1)
        return self.turned[t, shift]

    def along(self, t):
        mine, back = self.tiles[t], LANES - 1
        lane = iota(mine.shape, 1)
        before = self.turn(t - 1, 1) if t else mine
        after = self.turn(t + 1, back) if t + 1 < len(self.tiles) else mine
        left = jnp.where(lane == 0, before, self.turn(t, 1))
        right = jnp.where(lane == back, after, self.turn(t, back))
        return 2.0 * mine - left - right


def delayed(count, first, second, delay=2):
    waiting, results = [], []
    for t in range(count + delay):
        if t < count:
            waiting.append(first(t))
        if t >= delay:
            results.append(second(t - delay, waiting[t - delay]))
            waiting[t - delay] = None
    return results


def across_lines(values):
    height = values.shape[0]
    row = iota((8, values.shape[1]), 0)
    above, below = pltpu.roll(values, 1, 0), pltpu.roll(values, height - 1, 0)
    first = jnp.where(row == 0, values[:8], above[:8])
    last = jnp.where(row == 7, values[height - 8 :], below[height - 8 :])
    above = jnp.concatenate([first, above[8:]], 0)
    below = jnp.concatenate([below[: height - 8], last], 0)
    return 2.0 * values - above - below


def col_products(residual, blocks):
    high, low = halves(residual)
    size = blocks[0].shape[0] // 2
    dot = functools.partial(jnp.dot, preferred_element_type=f32)
    cuts = [slice(k * size, (k + 1) * size) for k in range(len(blocks))]
    return [(dot(pair, high[cut]), dot(pair[:size], low[cut])) for pair, cut in zip(blocks, cuts)]


def col_sum(products):
    size = products[0][1].shape[0]
    result = [both[:size] + (both[size:] + rest) for both, rest in products]
    return result[0] if len(result) == 1 else jnp.concatenate(result, 0)


def each(count, body):
    if count == 1:
        body(0)
    else:
        pl.loop(0, count)(body)


def join_kernel(*refs):
    for n, ref in enumerate(refs[:-1]):
        refs[-1][n * ref.shape[0] : (n + 1) * ref.shape[0], :] = ref[...]


def tables_kernel(sizes, codes_ref, rows_ref, cols_ref, fracs_ref, pairs_ref, look_ref, share_ref):
    depth, tiles, parts, carried = sizes
    for k in range(pairs_ref.shape[0]):
        base = (k // tiles) * (carried + LANES) + carried
        code = codes_ref[base : base + LANES, k % tiles * LANES : (k % tiles + 1) * LANES].astype(f32)
        high, low = halves(((code + code_half) * (block_span / code_top) + block_low).T)
        pairs_ref[k, :, :LANES] = high
        pairs_ref[k, :, LANES:] = low
    half = LANES // 2
    many = parts * tiles * depth
    rows, cols = rows_ref[...], cols_ref[...]
    blank = jnp.zeros((LANES - many, LANES), bf16)
    keys, lane = iota((many, LANES), 0), iota((half + 8, LANES), 0)
    for j in range(rows.shape[0]):
        cut = slice(j * LANES, (j + 1) * LANES)
        fy, fx = fracs_ref[0:1, cut], fracs_ref[1:2, cut]
        col = cols[j : j + 1]
        key = (col >> 7) * depth + rows[j : j + 1]
        second = (col & half) != 0
        near, far = rounded(1.0 - fy), rounded(fy)
        looks = [
            pick(keys, jnp.where(second, -8, key), near, far).astype(bf16),
            blank,
            pick(keys, jnp.where(second, key, -8), near, far).astype(bf16),
            blank,
        ]
        look_ref[:, cut] = jnp.concatenate(looks, 0)
        share_ref[:, cut] = pick(lane, col & (half - 1), rounded(1.0 - fx), rounded(fx))


def field_kernel(
    sizes, orders, pairs, look_ref, share_ref, col_blocks_ref, *refs,
):
    depth, tiles, parts, strips = sizes
    sent_refs, (final_ref, velocity_ref, weights_ref, source_ref, field_ref, ordered) = refs[:-6], refs[-6:]
    width_part = tiles * LANES
    width = parts * width_part
    height = strips * depth
    chunk = min(GROUP, strips) * depth
    chunks = height // chunk
    strip, part = lax.axis_index("strip"), lax.axis_index("cells")

    slots = parts * depth
    if len(sent_refs) == 1:
        sent = sent_refs[0]
    else:
        sent = ordered
        for order, sent_ref in zip(orders, sent_refs):
            for n, bits in enumerate(order):
                ordered[strip ^ bits] = sent_ref[n * 2 * slots : (n + 1) * 2 * slots, :]
    group = chunk // depth
    target, origin = iota((parts * chunk, group * slots), 0), iota((parts * chunk, group * slots), 1)
    slot = origin % slots
    fits = (slot // depth == target // chunk) & (origin // slots * depth + slot % depth == target % chunk)
    chosen = jnp.where(fits, 1.0, 0.0).astype(bf16)

    def placed(values):
        high, low = halves(jnp.concatenate(values, 0))
        dot = functools.partial(jnp.dot, preferred_element_type=f32)
        return dot(chosen, high) + dot(chosen, low)

    @functools.partial(each, chunks)
    def place(g):
        terms, codes = [], []
        for n in range(group):
            got = sent[g * group + n]
            terms.append(densities(got[:slots]))
            codes.append(got[slots:].astype(f32))
        term = placed(terms)
        weight = (placed(codes) + code_half) * (weight_span / code_top) + weight_low
        here = pl.ds(pl.multiple_of(g * chunk, chunk), chunk)
        for p in range(parts):
            cut = slice(p * width_part, (p + 1) * width_part)
            weights_ref[here, cut] = weight[p * chunk : (p + 1) * chunk]
            source_ref[here, cut] = term[p * chunk : (p + 1) * chunk] / weight[p * chunk : (p + 1) * chunk]

    col_blocks = [jnp.concatenate(halves(col_blocks_ref[k]), 0) for k in range(col_blocks_ref.shape[0])]
    inner = pl.ds(8, height)
    lanes_at_once = 4 * LANES if chunks == 1 and width % (4 * LANES) == 0 else LANES
    at_once = width // lanes_at_once if chunks == 1 else 1

    def cuts_of(g):
        if at_once > 1:
            return [slice(n * lanes_at_once, (n + 1) * lanes_at_once) for n in range(at_once)]
        return [pl.ds(pl.multiple_of(g * lanes_at_once, lanes_at_once), lanes_at_once)]

    col_steps = width // lanes_at_once // at_once

    @functools.partial(each, col_steps)
    def start(g):
        for cut in cuts_of(g):
            current = source_ref[:, cut]
            field_ref[inner, cut] = current
            source_ref[:, cut] = weights_ref[:, cut] * current - coupling * across_lines(current)

    row_tiles = [slice(t * LANES, (t + 1) * LANES) for t in range(width // LANES)]
    for step in range(STEPS):

        @functools.partial(each, chunks)
        def solve_rows(g):
            here = pl.ds(pl.multiple_of(g * chunk, chunk), chunk)
            there = pl.ds(pl.multiple_of(g * chunk + 8, 8), chunk)
            current = [field_ref[there, cut] for cut in row_tiles]
            for sweep in range(SWEEPS):
                turned = Turned(current)

                def multiply(t):
                    cut = row_tiles[t]
                    now = weights_ref[here, cut] * turned.tiles[t] + coupling * turned.along(t)
                    both = jnp.concatenate(halves(source_ref[here, cut] - now), 0)
                    return jnp.dot(both, pairs[t], preferred_element_type=f32)

                def add(t, product):
                    high, low = product[:chunk], product[chunk:]
                    return turned.tiles[t] + (high[:, :LANES] + (high[:, LANES:] + low[:, :LANES]))

                current = delayed(len(current), multiply, add)
            turned = Turned(current)
            for t, cut in enumerate(row_tiles):
                field_ref[there, cut] = current[t]
                source_ref[here, cut] = weights_ref[here, cut] * current[t] - coupling * turned.along(t)

        @functools.partial(each, col_steps)
        def solve_cols(g):
            cuts = cuts_of(g)
            current = [field_ref[inner, cut] for cut in cuts]
            for sweep in range(SWEEPS):
                before = current

                def multiply(n):
                    now = weights_ref[:, cuts[n]] * before[n] + coupling * across_lines(before[n])
                    return col_products(source_ref[:, cuts[n]] - now, col_blocks)

                current = delayed(len(cuts), multiply, lambda n, products: before[n] + col_sum(products))
            for now, cut in zip(current, cuts):
                field_ref[inner, cut] = now
                if step + 1 < STEPS:
                    source_ref[:, cut] = weights_ref[:, cut] * now - coupling * across_lines(now)
                else:
                    field_ref[:8, cut] = jnp.broadcast_to(now[:1], (8, lanes_at_once))
                    field_ref[height + 8 :, cut] = jnp.broadcast_to(now[-1:], (8, lanes_at_once))

    row0 = strip * depth
    columns = pl.ds(pl.multiple_of(part * width_part, LANES), width_part)
    base, shift = pl.multiple_of(row0 // 8 * 8, 8), 17 - row0 % 8
    final_ref[...] = pltpu.roll(field_ref[pl.ds(base, 24), columns], shift, 0)[1 : 1 + depth]

    window = pltpu.roll(field_ref[pl.ds(base, 24), :], shift, 0)
    above, centre, below = window[:8], pltpu.roll(window, 23, 0)[:8], pltpu.roll(window, 22, 0)[:8]
    left, right = beside(centre)
    scale = jnp.maximum(centre, floor_level)
    velocity_y = rounded(-(0.5 * (below - above)) / scale)
    velocity_x = rounded(-(0.5 * (right - left)) / scale)

    upper = iota((8, LANES), 0) < depth

    def stacked(values):
        stack = []
        for t in range(0, parts * tiles, 2):
            even = values[:, t * LANES : (t + 1) * LANES]
            odd = values[:, (t + 1) * LANES : (t + 2) * LANES]
            stack.append(jnp.where(upper, even, pltpu.roll(odd, depth, 0)))
        return jnp.concatenate(stack, 0)

    half = LANES // 2

    def table_of(values):
        stack = stacked(values)
        many = stack.shape[0]
        blank = jnp.zeros((LANES - many, LANES), f32)
        turned = jnp.concatenate([stack, blank], 0).T
        after = jnp.concatenate([pltpu.roll(stack, many - depth, 0), blank], 0).T[:8]
        return jnp.concatenate([turned[: half + 8], jnp.concatenate([turned[half:], after], 0)], 1)

    table = jnp.concatenate([table_of(velocity_y), table_of(velocity_x)], 0).astype(bf16)
    pins = share_ref.shape[1]
    at_once = 2 * LANES if pins % (2 * LANES) == 0 else LANES
    for j in range(0, pins, at_once):
        cut = slice(j, j + at_once)
        sampled = jnp.dot(table, look_ref[:, cut], preferred_element_type=f32)
        share = share_ref[:, cut]
        velocity_ref[0:1, cut] = jnp.sum(sampled[: half + 8] * share, 0, keepdims=True)
        velocity_ref[1:2, cut] = jnp.sum(sampled[half + 8 :] * share, 0, keepdims=True)


def partner(values, axis, bits):
    return lax.ppermute(values, axis, [(n, n ^ bits) for n in range(lax.axis_size(axis))])


def local(pin_rows, pin_cols, pin_fracs, pin_weights, capacity, blockage, row_blocks, col_blocks):
    depth, width_part = capacity.shape
    parts, strips = lax.axis_size("cells"), lax.axis_size("strip")
    tiles = width_part // LANES
    height, width = depth * strips, width_part * parts
    pins = pin_rows.shape[0]
    by_lane = (pins // LANES, LANES)
    rows, cols = pin_rows.reshape(by_lane), pin_cols.reshape(by_lane)
    sizes = pin_weights.reshape(by_lane)
    vmem = pl.BlockSpec(memory_space=pltpu.VMEM)
    whole = pltpu.CompilerParams(vmem_limit_bytes=60 << 20)
    small = pltpu.CompilerParams(vmem_limit_bytes=16 * 1024 * 1024)
    grid_bytes = 4 * height * width
    large = pltpu.CompilerParams(vmem_limit_bytes=(20 << 20) + 6 * grid_bytes)

    carried = 2 * parts * depth
    read = (rows, cols, pin_fracs, sizes, row_blocks.reshape(-1, LANES), capacity, blockage)
    terms = pl.pallas_call(
        functools.partial(splat_kernel, tiles, parts),
        out_shape=jax.ShapeDtypeStruct((carried + LANES, width_part), jnp.int16),
        in_specs=[pl.BlockSpec(memory_space=pltpu.HBM)] * 7,
        out_specs=vmem,
        scratch_shapes=[pltpu.VMEM(item.shape, item.dtype) for item in read] + [pltpu.SemaphoreType.DMA((7,))],
        compiler_params=whole,
        name="splat",
    )(*read)
    blocks = lax.all_gather(terms, "cells", axis=0, tiled=True)

    def terms_of(part):
        place = part * (carried + LANES) // carried
        return pl.BlockSpec((carried, width_part), lambda i: (place, 0))

    sums = pl.pallas_call(
        sum_kernel,
        grid=(1,),
        out_shape=jax.ShapeDtypeStruct((carried, width_part), jnp.int16),
        in_specs=[terms_of(part) for part in range(parts)],
        out_specs=pl.BlockSpec((carried, width_part), lambda i: (0, 0)),
        compiler_params=small,
        name="sum_terms",
    )(*[blocks] * parts)
    if strips == 8:
        orders = ((0,), (1,), (4, 6, 2), (5, 7, 3))
        from_z = [partner(sums, "strip", bits) for bits in (4, 6, 2)]
        *from_z, near = lax.optimization_barrier((*from_z, partner(sums, "strip", 1)))
        held = pl.pallas_call(
            join_kernel,
            out_shape=jax.ShapeDtypeStruct((3 * carried, width_part), jnp.int16),
            in_specs=[vmem] * 3,
            out_specs=vmem,
            compiler_params=small,
            name="join",
        )(*from_z)
        held, blocks = lax.optimization_barrier((held, blocks))
        sent = [sums, near, held, partner(held, "strip", 1)]
    else:
        orders, sent = (), [lax.all_gather(sums, "strip", axis=0)]
    pairs, look, share = pl.pallas_call(
        functools.partial(tables_kernel, (depth, tiles, parts, carried)),
        out_shape=(
            jax.ShapeDtypeStruct((width // LANES, LANES, 2 * LANES), bf16),
            jax.ShapeDtypeStruct((2 * LANES, pins), bf16),
            jax.ShapeDtypeStruct((LANES // 2 + 8, pins), f32),
        ),
        in_specs=[vmem] * 4,
        out_specs=(vmem,) * 3,
        compiler_params=small,
        cost_estimate=pl.CostEstimate(flops=1 << 20, bytes_accessed=1 << 21, transcendentals=0),
        name="tables",
    )(blocks, rows, cols, pin_fracs)

    final, velocity = pl.pallas_call(
        functools.partial(field_kernel, (depth, tiles, parts, strips), orders),
        out_shape=(
            jax.ShapeDtypeStruct((depth, width_part), f32),
            jax.ShapeDtypeStruct((2, pins), f32),
        ),
        in_specs=[vmem] * (4 + len(sent)),
        out_specs=(vmem, vmem),
        scratch_shapes=[
            pltpu.VMEM((height, width), f32),
            pltpu.VMEM((height, width), f32),
            pltpu.VMEM((height + 16, width), f32),
            pltpu.VMEM((strips if len(sent) > 1 else 1, carried, width_part), jnp.int16),
        ],
        compiler_params=large,
        name="field",
    )(pairs, look, share, col_blocks, *sent)
    return final, velocity


def solution(mesh):
    placed = (
        P(("strip", "cells")),
        P(("strip", "cells")),
        P(None, ("strip", "cells")),
        P(("strip", "cells")),
        P("strip", "cells"),
        P("strip", "cells"),
        P("cells", None, None),
        P(),
    )
    return jax.shard_map(
        local,
        mesh=mesh,
        in_specs=placed,
        out_specs=(P("strip", "cells"), P(None, ("strip", "cells"))),
        check_vma=False,
    )
```

```python
import functools

import jax
import jax.numpy as jnp
from jax import lax
from jax.experimental import pallas as pl
from jax.experimental.pallas import tpu as pltpu
from jax.sharding import PartitionSpec as P

SWEEPS = 3
STEPS = 2
LANES = 128
GROUP = 8

coupling = 2.0
floor_level = 0.5
block_low, block_span = -0.002, 0.152
weight_low, weight_span = 0.5, 3.5
term_low, term_octaves = -24.0, 40.0
code_top = 65535.0
code_half = 32768.0
log_two = 0.6931471805599453

f32 = jnp.float32
bf16 = jnp.bfloat16


def iota(shape, axis):
    return lax.broadcasted_iota(jnp.int32, shape, axis)


def halves(values):
    high = values.astype(bf16)
    return high, (values - high.astype(f32)).astype(bf16)


def last_dims(left, right):
    return lax.dot_general(left, right, (((1,), (1,)), ((), ())), preferred_element_type=f32)


def pick(index, first, near, far):
    return jnp.where(index == first, near, jnp.where(index == first + 1, far, 0.0))


def rounded(values):
    return values.astype(bf16).astype(f32)


def coded(share):
    return jnp.clip(jnp.round(share * code_top), 0.0, code_top) - code_half


def stored(codes):
    return codes.astype(jnp.int32).astype(jnp.int16)


def density_codes(values):
    octave = jnp.log(jnp.maximum(values, 2.0**-40)) * (1.0 / log_two)
    return stored(coded((octave - term_low) * (1.0 / term_octaves)))


def densities(codes):
    codes = codes.astype(f32)
    octave = (codes + code_half) * (term_octaves / code_top) + term_low
    return jnp.where(codes == -code_half, 0.0, jnp.exp(octave * log_two))


def splat_kernel(
    tiles, parts, rows_in, cols_in, fracs_in, pin_weights_in, row_blocks_in, cap_in, block_in, out_ref,
    rows_ref, cols_ref, fracs_ref, pin_weights_ref, row_blocks_ref, cap_ref, block_ref, arrived,
):
    depth = cap_ref.shape[0]
    height = parts * depth
    sources = (rows_in, cols_in, fracs_in, pin_weights_in, row_blocks_in, cap_in, block_in)
    places = (rows_ref, cols_ref, fracs_ref, pin_weights_ref, row_blocks_ref, cap_ref, block_ref)
    copies = [
        pltpu.make_async_copy(source, place, arrived.at[n]) for n, (source, place) in enumerate(zip(sources, places))
    ]
    for copy in copies:
        copy.start()
    for copy in copies[:4]:
        copy.wait()
    rows, cols, sizes = rows_ref[...], cols_ref[...], pin_weights_ref[...]
    place = iota((height * (tiles + 1), LANES), 0)
    group, inner = place // height, place % height
    keys = ((inner // depth) * tiles + group - 1) * depth + inner % depth
    lane = iota((LANES + 8, LANES), 0)
    tables, lanes = [], []
    for j in range(rows.shape[0]):
        cut = slice(j * LANES, (j + 1) * LANES)
        fy, fx = fracs_ref[0:1, cut], fracs_ref[1:2, cut]
        size, col = sizes[j : j + 1], cols[j : j + 1]
        key = (col >> 7) * depth + rows[j : j + 1]
        tables.append(pick(keys, key, rounded(size * (1.0 - fy)), rounded(size * fy)).astype(bf16))
        lanes.append(pick(lane, col & 127, rounded(1.0 - fx), rounded(fx)).astype(bf16))
    total = last_dims(jnp.concatenate(tables, 1), jnp.concatenate(lanes, 1))
    for copy in copies[4:]:
        copy.wait()
    first_lane = iota((height, LANES), 1) == 0
    for t in range(tiles):
        own = total[(t + 1) * height : (t + 2) * height, :LANES]
        spill = total[t * height : (t + 1) * height, LANES : LANES + 1]
        own = own + jnp.where(first_lane, spill, 0.0)
        cut = slice(t * LANES, (t + 1) * LANES)
        out_ref[:height, cut] = density_codes(own)
        share = (row_blocks_ref[t * LANES : (t + 1) * LANES, :] - block_low) * (1.0 / block_span)
        out_ref[2 * height :, cut] = stored(coded(share))
    weights = cap_ref[...].astype(f32) * (1.0 - block_ref[...])
    code = coded((weights - weight_low) * (1.0 / weight_span))
    row = iota((height, weights.shape[1]), 0)
    mine = row // depth == lax.axis_index("cells")
    out_ref[height : 2 * height, :] = stored(jnp.where(mine, jnp.concatenate([code] * parts, 0), 0.0))


def sum_kernel(*refs):
    sent_refs, out_ref = refs[:-1], refs[-1]
    height = out_ref.shape[0] // 2
    terms, codes = 0.0, 0.0
    for sent_ref in sent_refs:
        terms += densities(sent_ref[:height, :])
        codes += sent_ref[height:, :].astype(f32)
    out_ref[:height, :] = density_codes(terms)
    out_ref[height:, :] = stored(codes)


def beside(values):
    width = values.shape[1]
    lane = iota((values.shape[0], LANES), 1)
    left, right = pltpu.roll(values, 1, 1), pltpu.roll(values, width - 1, 1)
    first = jnp.where(lane == 0, values[:, :LANES], left[:, :LANES])
    last = jnp.where(lane == LANES - 1, values[:, width - LANES :], right[:, width - LANES :])
    return (
        jnp.concatenate([first, left[:, LANES:]], 1),
        jnp.concatenate([right[:, : width - LANES], last], 1),
    )


class Turned:
    def __init__(self, tiles):
        self.tiles, self.turned = tiles, {}

    def turn(self, t, shift):
        if (t, shift) not in self.turned:
            self.turned[t, shift] = pltpu.roll(self.tiles[t], shift, 1)
        return self.turned[t, shift]

    def along(self, t):
        mine, back = self.tiles[t], LANES - 1
        lane = iota(mine.shape, 1)
        before = self.turn(t - 1, 1) if t else mine
        after = self.turn(t + 1, back) if t + 1 < len(self.tiles) else mine
        left = jnp.where(lane == 0, before, self.turn(t, 1))
        right = jnp.where(lane == back, after, self.turn(t, back))
        return 2.0 * mine - left - right


def delayed(count, first, second, delay=2):
    waiting, results = [], []
    for t in range(count + delay):
        if t < count:
            waiting.append(first(t))
        if t >= delay:
            results.append(second(t - delay, waiting[t - delay]))
            waiting[t - delay] = None
    return results


def across_lines(values):
    height = values.shape[0]
    row = iota((8, values.shape[1]), 0)
    above, below = pltpu.roll(values, 1, 0), pltpu.roll(values, height - 1, 0)
    first = jnp.where(row == 0, values[:8], above[:8])
    last = jnp.where(row == 7, values[height - 8 :], below[height - 8 :])
    above = jnp.concatenate([first, above[8:]], 0)
    below = jnp.concatenate([below[: height - 8], last], 0)
    return 2.0 * values - above - below


def col_products(residual, blocks):
    high, low = halves(residual)
    size = blocks[0].shape[0] // 2
    dot = functools.partial(jnp.dot, preferred_element_type=f32)
    cuts = [slice(k * size, (k + 1) * size) for k in range(len(blocks))]
    return [(dot(pair, high[cut]), dot(pair[:size], low[cut])) for pair, cut in zip(blocks, cuts)]


def col_sum(products):
    size = products[0][1].shape[0]
    result = [both[:size] + (both[size:] + rest) for both, rest in products]
    return result[0] if len(result) == 1 else jnp.concatenate(result, 0)


def each(count, body):
    if count == 1:
        body(0)
    else:
        pl.loop(0, count)(body)


def join_kernel(*refs):
    for n, ref in enumerate(refs[:-1]):
        refs[-1][n * ref.shape[0] : (n + 1) * ref.shape[0], :] = ref[...]


def tables_kernel(sizes, codes_ref, rows_ref, cols_ref, fracs_ref, pairs_ref, look_ref, share_ref):
    depth, tiles, parts, carried = sizes
    for k in range(pairs_ref.shape[0]):
        base = (k // tiles) * (carried + LANES) + carried
        code = codes_ref[base : base + LANES, k % tiles * LANES : (k % tiles + 1) * LANES].astype(f32)
        high, low = halves(((code + code_half) * (block_span / code_top) + block_low).T)
        pairs_ref[k, :, :LANES] = high
        pairs_ref[k, :, LANES:] = low
    half = LANES // 2
    many = parts * tiles * depth
    rows, cols = rows_ref[...], cols_ref[...]
    blank = jnp.zeros((LANES - many, LANES), bf16)
    keys, lane = iota((many, LANES), 0), iota((half + 8, LANES), 0)
    for j in range(rows.shape[0]):
        cut = slice(j * LANES, (j + 1) * LANES)
        fy, fx = fracs_ref[0:1, cut], fracs_ref[1:2, cut]
        col = cols[j : j + 1]
        key = (col >> 7) * depth + rows[j : j + 1]
        second = (col & half) != 0
        near, far = rounded(1.0 - fy), rounded(fy)
        looks = [
            pick(keys, jnp.where(second, -8, key), near, far).astype(bf16),
            blank,
            pick(keys, jnp.where(second, key, -8), near, far).astype(bf16),
            blank,
        ]
        look_ref[:, cut] = jnp.concatenate(looks, 0)
        share_ref[:, cut] = pick(lane, col & (half - 1), rounded(1.0 - fx), rounded(fx))


def field_kernel(
    sizes, orders, pairs, look_ref, share_ref, col_blocks_ref, *refs,
):
    depth, tiles, parts, strips = sizes
    sent_refs, (final_ref, velocity_ref, weights_ref, source_ref, field_ref, ordered) = refs[:-6], refs[-6:]
    width_part = tiles * LANES
    width = parts * width_part
    height = strips * depth
    chunk = min(GROUP, strips) * depth
    chunks = height // chunk
    strip, part = lax.axis_index("strip"), lax.axis_index("cells")

    slots = parts * depth
    if len(sent_refs) == 1:
        sent = sent_refs[0]
    else:
        sent = ordered
        for order, sent_ref in zip(orders, sent_refs):
            for n, bits in enumerate(order):
                ordered[strip ^ bits] = sent_ref[n * 2 * slots : (n + 1) * 2 * slots, :]
    group = chunk // depth
    target, origin = iota((parts * chunk, group * slots), 0), iota((parts * chunk, group * slots), 1)
    slot = origin % slots
    fits = (slot // depth == target // chunk) & (origin // slots * depth + slot % depth == target % chunk)
    chosen = jnp.where(fits, 1.0, 0.0).astype(bf16)

    def placed(values):
        high, low = halves(jnp.concatenate(values, 0))
        dot = functools.partial(jnp.dot, preferred_element_type=f32)
        return dot(chosen, high) + dot(chosen, low)

    @functools.partial(each, chunks)
    def place(g):
        terms, codes = [], []
        for n in range(group):
            got = sent[g * group + n]
            terms.append(densities(got[:slots]))
            codes.append(got[slots:].astype(f32))
        term = placed(terms)
        weight = (placed(codes) + code_half) * (weight_span / code_top) + weight_low
        here = pl.ds(pl.multiple_of(g * chunk, chunk), chunk)
        for p in range(parts):
            cut = slice(p * width_part, (p + 1) * width_part)
            weights_ref[here, cut] = weight[p * chunk : (p + 1) * chunk]
            source_ref[here, cut] = term[p * chunk : (p + 1) * chunk] / weight[p * chunk : (p + 1) * chunk]

    col_blocks = [jnp.concatenate(halves(col_blocks_ref[k]), 0) for k in range(col_blocks_ref.shape[0])]
    inner = pl.ds(8, height)
    lanes_at_once = 2 * LANES if chunks == 1 and width % (2 * LANES) == 0 else LANES
    at_once = width // lanes_at_once if chunks == 1 else 1

    def cuts_of(g):
        if at_once > 1:
            return [slice(n * lanes_at_once, (n + 1) * lanes_at_once) for n in range(at_once)]
        return [pl.ds(pl.multiple_of(g * lanes_at_once, lanes_at_once), lanes_at_once)]

    col_steps = width // lanes_at_once // at_once

    @functools.partial(each, col_steps)
    def start(g):
        for cut in cuts_of(g):
            current = source_ref[:, cut]
            field_ref[inner, cut] = current
            source_ref[:, cut] = weights_ref[:, cut] * current - coupling * across_lines(current)

    row_tiles = [slice(t * LANES, (t + 1) * LANES) for t in range(width // LANES)]
    for step in range(STEPS):

        @functools.partial(each, chunks)
        def solve_rows(g):
            here = pl.ds(pl.multiple_of(g * chunk, chunk), chunk)
            there = pl.ds(pl.multiple_of(g * chunk + 8, 8), chunk)
            current = [field_ref[there, cut] for cut in row_tiles]
            for sweep in range(SWEEPS):
                turned = Turned(current)

                def multiply(t):
                    cut = row_tiles[t]
                    now = weights_ref[here, cut] * turned.tiles[t] + coupling * turned.along(t)
                    both = jnp.concatenate(halves(source_ref[here, cut] - now), 0)
                    return jnp.dot(both, pairs[t], preferred_element_type=f32)

                def add(t, product):
                    high, low = product[:chunk], product[chunk:]
                    return turned.tiles[t] + (high[:, :LANES] + (high[:, LANES:] + low[:, :LANES]))

                current = delayed(len(current), multiply, add)
            turned = Turned(current)
            for t, cut in enumerate(row_tiles):
                field_ref[there, cut] = current[t]
                source_ref[here, cut] = weights_ref[here, cut] * current[t] - coupling * turned.along(t)

        @functools.partial(each, col_steps)
        def solve_cols(g):
            cuts = cuts_of(g)
            current = [field_ref[inner, cut] for cut in cuts]
            for sweep in range(SWEEPS):
                before = current

                def multiply(n):
                    now = weights_ref[:, cuts[n]] * before[n] + coupling * across_lines(before[n])
                    return col_products(source_ref[:, cuts[n]] - now, col_blocks)

                current = delayed(len(cuts), multiply, lambda n, products: before[n] + col_sum(products))
            for now, cut in zip(current, cuts):
                field_ref[inner, cut] = now
                if step + 1 < STEPS:
                    source_ref[:, cut] = weights_ref[:, cut] * now - coupling * across_lines(now)
                else:
                    field_ref[:8, cut] = jnp.broadcast_to(now[:1], (8, lanes_at_once))
                    field_ref[height + 8 :, cut] = jnp.broadcast_to(now[-1:], (8, lanes_at_once))

    row0 = strip * depth
    columns = pl.ds(pl.multiple_of(part * width_part, LANES), width_part)
    base, shift = pl.multiple_of(row0 // 8 * 8, 8), 17 - row0 % 8
    final_ref[...] = pltpu.roll(field_ref[pl.ds(base, 24), columns], shift, 0)[1 : 1 + depth]

    window = pltpu.roll(field_ref[pl.ds(base, 24), :], shift, 0)
    above, centre, below = window[:8], pltpu.roll(window, 23, 0)[:8], pltpu.roll(window, 22, 0)[:8]
    left, right = beside(centre)
    scale = jnp.maximum(centre, floor_level)
    velocity_y = rounded(-(0.5 * (below - above)) / scale)
    velocity_x = rounded(-(0.5 * (right - left)) / scale)

    upper = iota((8, LANES), 0) < depth

    def stacked(values):
        stack = []
        for t in range(0, parts * tiles, 2):
            even = values[:, t * LANES : (t + 1) * LANES]
            odd = values[:, (t + 1) * LANES : (t + 2) * LANES]
            stack.append(jnp.where(upper, even, pltpu.roll(odd, depth, 0)))
        return jnp.concatenate(stack, 0)

    half = LANES // 2

    def table_of(values):
        stack = stacked(values)
        many = stack.shape[0]
        blank = jnp.zeros((LANES - many, LANES), f32)
        turned = jnp.concatenate([stack, blank], 0).T
        after = jnp.concatenate([pltpu.roll(stack, many - depth, 0), blank], 0).T[:8]
        return jnp.concatenate([turned[: half + 8], jnp.concatenate([turned[half:], after], 0)], 1)

    table = jnp.concatenate([table_of(velocity_y), table_of(velocity_x)], 0).astype(bf16)
    pins = share_ref.shape[1]
    at_once = 4 * LANES if pins % (4 * LANES) == 0 else LANES
    for j in range(0, pins, at_once):
        cut = slice(j, j + at_once)
        sampled = jnp.dot(table, look_ref[:, cut], preferred_element_type=f32)
        share = share_ref[:, cut]
        velocity_ref[0:1, cut] = jnp.sum(sampled[: half + 8] * share, 0, keepdims=True)
        velocity_ref[1:2, cut] = jnp.sum(sampled[half + 8 :] * share, 0, keepdims=True)


def partner(values, axis, bits):
    return lax.ppermute(values, axis, [(n, n ^ bits) for n in range(lax.axis_size(axis))])


def local(pin_rows, pin_cols, pin_fracs, pin_weights, capacity, blockage, row_blocks, col_blocks):
    depth, width_part = capacity.shape
    parts, strips = lax.axis_size("cells"), lax.axis_size("strip")
    tiles = width_part // LANES
    height, width = depth * strips, width_part * parts
    pins = pin_rows.shape[0]
    by_lane = (pins // LANES, LANES)
    rows, cols = pin_rows.reshape(by_lane), pin_cols.reshape(by_lane)
    sizes = pin_weights.reshape(by_lane)
    vmem = pl.BlockSpec(memory_space=pltpu.VMEM)
    whole = pltpu.CompilerParams(vmem_limit_bytes=60 << 20)
    small = pltpu.CompilerParams(vmem_limit_bytes=16 * 1024 * 1024)
    grid_bytes = 4 * height * width
    large = pltpu.CompilerParams(vmem_limit_bytes=(20 << 20) + 6 * grid_bytes)

    carried = 2 * parts * depth
    read = (rows, cols, pin_fracs, sizes, row_blocks.reshape(-1, LANES), capacity, blockage)
    terms = pl.pallas_call(
        functools.partial(splat_kernel, tiles, parts),
        out_shape=jax.ShapeDtypeStruct((carried + LANES, width_part), jnp.int16),
        in_specs=[pl.BlockSpec(memory_space=pltpu.HBM)] * 7,
        out_specs=vmem,
        scratch_shapes=[pltpu.VMEM(item.shape, item.dtype) for item in read] + [pltpu.SemaphoreType.DMA((7,))],
        compiler_params=whole,
        name="splat",
    )(*read)
    blocks = lax.all_gather(terms, "cells", axis=0, tiled=True)

    def terms_of(part):
        place = part * (carried + LANES) // carried
        return pl.BlockSpec((carried, width_part), lambda i: (place, 0))

    sums = pl.pallas_call(
        sum_kernel,
        grid=(1,),
        out_shape=jax.ShapeDtypeStruct((carried, width_part), jnp.int16),
        in_specs=[terms_of(part) for part in range(parts)],
        out_specs=pl.BlockSpec((carried, width_part), lambda i: (0, 0)),
        compiler_params=small,
        name="sum_terms",
    )(*[blocks] * parts)
    if strips == 8:
        orders = ((0,), (1,), (4, 6, 2), (5, 7, 3))
        from_z = [partner(sums, "strip", bits) for bits in (4, 6, 2)]
        *from_z, near = lax.optimization_barrier((*from_z, partner(sums, "strip", 1)))
        held = pl.pallas_call(
            join_kernel,
            out_shape=jax.ShapeDtypeStruct((3 * carried, width_part), jnp.int16),
            in_specs=[vmem] * 3,
            out_specs=vmem,
            compiler_params=small,
            name="join",
        )(*from_z)
        held, blocks = lax.optimization_barrier((held, blocks))
        sent = [sums, near, held, partner(held, "strip", 1)]
    else:
        orders, sent = (), [lax.all_gather(sums, "strip", axis=0)]
    pairs, look, share = pl.pallas_call(
        functools.partial(tables_kernel, (depth, tiles, parts, carried)),
        out_shape=(
            jax.ShapeDtypeStruct((width // LANES, LANES, 2 * LANES), bf16),
            jax.ShapeDtypeStruct((2 * LANES, pins), bf16),
            jax.ShapeDtypeStruct((LANES // 2 + 8, pins), f32),
        ),
        in_specs=[vmem] * 4,
        out_specs=(vmem,) * 3,
        compiler_params=small,
        cost_estimate=pl.CostEstimate(flops=1 << 20, bytes_accessed=1 << 21, transcendentals=0),
        name="tables",
    )(blocks, rows, cols, pin_fracs)

    final, velocity = pl.pallas_call(
        functools.partial(field_kernel, (depth, tiles, parts, strips), orders),
        out_shape=(
            jax.ShapeDtypeStruct((depth, width_part), f32),
            jax.ShapeDtypeStruct((2, pins), f32),
        ),
        in_specs=[vmem] * (4 + len(sent)),
        out_specs=(vmem, vmem),
        scratch_shapes=[
            pltpu.VMEM((height, width), f32),
            pltpu.VMEM((height, width), f32),
            pltpu.VMEM((height + 16, width), f32),
            pltpu.VMEM((strips if len(sent) > 1 else 1, carried, width_part), jnp.int16),
        ],
        compiler_params=large,
        name="field",
    )(pairs, look, share, col_blocks, *sent)
    return final, velocity


def solution(mesh):
    placed = (
        P(("strip", "cells")),
        P(("strip", "cells")),
        P(None, ("strip", "cells")),
        P(("strip", "cells")),
        P("strip", "cells"),
        P("strip", "cells"),
        P("cells", None, None),
        P(),
    )
    return jax.shard_map(
        local,
        mesh=mesh,
        in_specs=placed,
        out_specs=(P("strip", "cells"), P(None, ("strip", "cells"))),
        check_vma=False,
    )
```
